32 devices in a mesh: dp: 8 (over y, x, core), head: 4 (over z).
Axes of the slice: x: 2, y: 2, z: 4, core: 2. Of those that a mesh axis runs over, the one named last changes fastest.
Arguments:
- features: bfloat16 [2048, 16384], P(None, ('dp', 'head'))
- crop_rows: int32 [2], replicated, may hold values from 32 to 64, as said below
- crop_cols: int32 [2], replicated, may hold values from 64 to 128, as said below
- labels: int32 [16384], P('dp'), may hold values from 0 to 18
- offset_targets: float32 [2, 16384], P(None, 'dp'), may hold values from -6 to 6
- depth_targets: float32 [16384], P('dp'), may hold values from 0.1 to 3
- lidar_mask: int32 [16384], P('dp'), may hold values from 0 to 1, as said below
- trunk_aspp: float32 [4, 30336, 128], P('head', 'dp')
- aspp_first: float32 [4, 30336, 128], P('head', 'dp'), may hold values from -7.6293945e-06 to 7.6293945e-06
- aspp_second: float32 [4, 30336, 128], P('head', 'dp'), may hold values from 6.5348386e-12 to 2.6040343e-11
- trunk_neck: float32 [4, 8704, 128], P('head', 'dp')
- neck_first: float32 [4, 8704, 128], P('head', 'dp'), may hold values from -7.6293945e-06 to 7.6293945e-06
- neck_second: float32 [4, 8704, 128], P('head', 'dp'), may hold values from 6.5348386e-12 to 2.6040343e-11
- norm_params: float32 [2, 4352], replicated
- norm_first: float32 [2, 4352], replicated, may hold values from -7.6293945e-05 to 7.6293945e-05
- norm_second: float32 [2, 4352], replicated, may hold values from 6.534839e-10 to 2.6040343e-09
- decoders: float32 [790, 256], replicated
- decoder_first: float32 [790, 256], replicated, may hold values from -2.2888184e-05 to 2.2888184e-05
- decoder_second: float32 [790, 256], replicated, may hold values from 5.84175e-11 to 2.3466012e-10
- log_vars: float32 [3], replicated, may hold values from -0.5 to 0.5
- log_first: float32 [3], replicated, may hold values from -0.0068359375 to 0.0068359375
- log_second: float32 [3], replicated, may hold values from 5.3e-06 to 2.1e-05
Outputs:
- total_loss: float32 [], replicated
- grad_norm: float32 [], replicated
- aspp_new: float32 [4, 30336, 128], P('head', 'dp')
- aspp_first_new: float32 [4, 30336, 128], P('head', 'dp')
- aspp_second_new: float32 [4, 30336, 128], P('head', 'dp')
- neck_new: float32 [4, 8704, 128], P('head', 'dp')
- neck_first_new: float32 [4, 8704, 128], P('head', 'dp')
- neck_second_new: float32 [4, 8704, 128], P('head', 'dp')
- norm_new: float32 [2, 4352], replicated
- norm_first_new: float32 [2, 4352], replicated
- norm_second_new: float32 [2, 4352], replicated
- decoder_new: float32 [790, 256], replicated
- decoder_first_new: float32 [790, 256], replicated
- decoder_second_new: float32 [790, 256], replicated
- log_new: float32 [3], replicated
- log_first_new: float32 [3], replicated
- log_second_new: float32 [3], replicated
The draws below stay inside these ranges and needn't reach their ends.
Inputs may be any that keep to these rules, and one draw needn't show every extreme that they name: `crop_rows`: one crop, drawn from the seed, has all 64 rows. `crop_cols`: one crop, drawn from the seed, has all 128 columns. `lidar_mask`: every pixel of column 0 is 1.
All inputs are finite; a program needn't handle non-finite values.
Results may differ from the reference program's by a relative error of at most 0.014.
Values may be sent and summed in bfloat16 or wider, within the bound.
No kernel may reach another device: no remote copies, remote signals or barrier semaphores. Data moves between devices by JAX's collectives and lax.ppermute only.
A program may use at most 384 MiB of HBM per device.

```python
import math
import jax
import jax.numpy as jnp
from jax import lax

FEAT = 2048
BOT = 512
ASP = 256
CLS = 19
OUTS = 22
WIDTH = 128
STEP = 10
CROP_ROWS = 64
CROPS = 2
PIX_ALL = 16384
NORMS = 4352
ROWS_A = 30336
ROWS_B = 8704
NALL = 20199427


def draw_features(key, part):
    key = jax.random.fold_in(key, 1)
    row_place = jnp.arange(PIX_ALL, dtype=jnp.int32) // WIDTH
    rising = row_place.astype(jnp.float32) / (PIX_ALL // WIDTH - 1)
    noise_draw = jax.random.normal(key, (FEAT, PIX_ALL), jnp.float32)
    return (noise_draw * (1.0 + 2.0 * rising)[None, :]).astype(jnp.bfloat16)


def crop_sizes(key, largest):
    height_key, pick_key = jax.random.split(key)
    heights = jax.random.randint(height_key, (CROPS,), largest // 2, largest + 1)
    chosen = jax.random.randint(pick_key, (), 0, CROPS)
    return jnp.where(jnp.arange(CROPS) == chosen, largest, heights).astype(jnp.int32)


def draw_crop_rows(key, part):
    key = jax.random.fold_in(key, 2)
    return crop_sizes(key, CROP_ROWS)


def draw_crop_cols(key, part):
    key = jax.random.fold_in(key, 3)
    return crop_sizes(key, WIDTH)


def draw_lidar_mask(key, part):
    key = jax.random.fold_in(key, 4)
    pixel_place = jnp.arange(PIX_ALL, dtype=jnp.int32)
    row_place = pixel_place // WIDTH
    threshold = 25 + 50 * row_place // (PIX_ALL // WIDTH - 1)
    rolled = jax.random.randint(key, (PIX_ALL,), 0, 100)
    return jnp.where((rolled < threshold) | (pixel_place % WIDTH == 0), 1, 0).astype(jnp.int32)


def scaled_flat(noise_draw, pieces):
    total_size = noise_draw.shape[1]
    used_size = sum((amount for amount, factor in pieces))
    scales = jnp.concatenate([jnp.full((amount,), factor, jnp.float32) for amount, factor in pieces] + [jnp.full((total_size - used_size,), 0.02, jnp.float32)])
    return noise_draw * scales[None, :]


def draw_trunk_aspp(key, part):
    key = jax.random.fold_in(key, 5)
    noise_draw = jax.random.normal(key, (4, ROWS_A * 128), jnp.float32)
    quarter = ASP // 4
    pieces = [(quarter * FEAT, FEAT ** (-0.5)), (27 * quarter * FEAT, (9 * FEAT) ** (-0.5)), (quarter * FEAT, FEAT ** (-0.5)), (5 * quarter * ASP, (5 * ASP) ** (-0.5))]
    return scaled_flat(noise_draw, pieces).reshape(4, ROWS_A, 128)


def draw_trunk_neck(key, part):
    key = jax.random.fold_in(key, 6)
    noise_draw = jax.random.normal(key, (4, ROWS_B * 128), jnp.float32)
    quarter = BOT // 4
    pieces = [(quarter * FEAT, FEAT ** (-0.5)), (9 * quarter * BOT, (9 * BOT) ** (-0.5)), (FEAT // 4 * BOT, BOT ** (-0.5))]
    return scaled_flat(noise_draw, pieces).reshape(4, ROWS_B, 128)


def draw_norm_params(key, part):
    key = jax.random.fold_in(key, 7)
    gain_key, shift_key = jax.random.split(key)
    gains = jnp.exp(jax.random.uniform(gain_key, (NORMS,), jnp.float32, -0.69, 0.69))
    shifts = 0.3 * jax.random.normal(shift_key, (NORMS,), jnp.float32)
    return jnp.stack([gains, shifts])


def draw_decoders(key, part):
    key = jax.random.fold_in(key, 8)
    noise_draw = jax.random.normal(key, (3 * ASP + OUTS, ASP), jnp.float32)
    row_scale = jnp.where(jnp.arange(3 * ASP + OUTS) < 3 * ASP, 1.0, 3.0) * ASP ** (-0.5)
    return noise_draw * row_scale[:, None]


def place_ends(entries, stream_key, smallest, top_value):
    place = [jax.random.randint(jax.random.fold_in(stream_key, axis), (), 0, length) for axis, length in enumerate(entries.shape)]
    longest = entries.shape.index(max(entries.shape))
    beside = place[:longest] + [(place[longest] + 1) % entries.shape[longest]] + place[longest + 1:]
    return entries.at[tuple(place)].set(smallest).at[tuple(beside)].set(top_value)


def steps_of(rng, extent, cuts, least, high):
    level, own = 1.0, jax.random.fold_in(rng, 6)
    for axis_at, parts in cuts:
        draws = jnp.exp(jax.random.uniform(jax.random.fold_in(own, axis_at), (parts,), jnp.float32, least / len(cuts), high / len(cuts)))
        level = level * jnp.repeat(draws, extent[axis_at] // parts).reshape([-1 if axis == axis_at else 1 for axis in range(len(extent))])
    return level


def centred(own_key, dims, width, most, cuts=(), kind=jnp.bfloat16):
    factor_of = steps_of(own_key, dims, cuts, -0.22, 0.18) if cuts else 1.0
    values = jax.random.normal(own_key, dims, jnp.float32) * width * factor_of
    return jnp.minimum(jnp.maximum(values, -most), most).astype(kind)


def setup_inputs(seed: int = 0) -> dict:
    keys = jax.random.split(jax.random.key(seed), 23)
    features = draw_features(jax.random.fold_in(keys[22], 71), 0)
    crop_rows = draw_crop_rows(jax.random.fold_in(keys[22], 71), 0)
    crop_cols = draw_crop_cols(jax.random.fold_in(keys[22], 71), 0)
    labels = place_ends(jax.random.randint(keys[3], (PIX_ALL,), 0, CLS), jax.random.fold_in(keys[3], 1), 0, CLS - 1).astype(jnp.int32)
    offset_targets = centred(keys[4], (2, PIX_ALL), 1.0, 6.0, ((1, 8),), jnp.float32)
    depth_targets = jnp.clip(jnp.exp(math.log(3.0) - 3.4011974 * jax.random.uniform(keys[5], (PIX_ALL,), jnp.float32) ** steps_of(keys[5], (PIX_ALL,), ((0, 8),), -0.2, 0.2)), 0.1, 3.0)
    lidar_mask = draw_lidar_mask(jax.random.fold_in(keys[22], 71), 0)
    trunk_aspp = draw_trunk_aspp(jax.random.fold_in(keys[22], 71), 0)
    aspp_first = centred(keys[8], (4, ROWS_A, 128), (0.0055 / NALL ** 0.5), 7.62939453125e-06, ((0, 4), (1, 8)), jnp.float32)
    aspp_second = jnp.clip(6.5348386424357585e-12 + 1.9505504850192423e-11 * jax.random.uniform(keys[9], (4, ROWS_A, 128), jnp.float32) ** steps_of(keys[9], (4, ROWS_A, 128), ((0, 4), (1, 8)), -0.2, 0.2), 6.5348386424357585e-12, 2.6040343492628182e-11)
    trunk_neck = draw_trunk_neck(jax.random.fold_in(keys[22], 71), 0)
    neck_first = centred(keys[11], (4, ROWS_B, 128), (0.0055 / NALL ** 0.5), 7.62939453125e-06, ((0, 4), (1, 8)), jnp.float32)
    neck_second = jnp.clip(6.5348386424357585e-12 + 1.9505504850192423e-11 * jax.random.uniform(keys[12], (4, ROWS_B, 128), jnp.float32) ** steps_of(keys[12], (4, ROWS_B, 128), ((0, 4), (1, 8)), -0.2, 0.2), 6.5348386424357585e-12, 2.6040343492628182e-11)
    norm_params = draw_norm_params(jax.random.fold_in(keys[22], 71), 0)
    norm_first = centred(keys[14], (2, NORMS), (0.055 / NALL ** 0.5), 7.62939453125e-05, (), jnp.float32)
    norm_second = jnp.clip(jax.random.uniform(keys[15], (2, NORMS), jnp.float32, 6.534838781213637e-10, 2.6040343215072426e-09), 6.534838781213637e-10, 2.6040343215072426e-09)
    decoders = draw_decoders(jax.random.fold_in(keys[22], 71), 0)
    decoder_first = centred(keys[17], (3 * ASP + OUTS, ASP), (0.0167 / NALL ** 0.5), 2.288818359375e-05, (), jnp.float32)
    decoder_second = jnp.clip(jax.random.uniform(keys[18], (3 * ASP + OUTS, ASP), jnp.float32, 5.841750000401547e-11, 2.346601246649982e-10), 5.841750000401547e-11, 2.346601246649982e-10)
    log_vars = jnp.clip(jax.random.uniform(keys[19], (3,), jnp.float32, -0.5, 0.5), -0.5, 0.5)
    log_first = centred(keys[20], (3,), 0.0011, 0.0068359375, (), jnp.float32)
    log_second = jnp.clip(jax.random.uniform(keys[21], (3,), jnp.float32, 5.299999884300632e-06, 2.099999983329326e-05), 5.299999884300632e-06, 2.099999983329326e-05)
    return {"features": features, "crop_rows": crop_rows, "crop_cols": crop_cols, "labels": labels, "offset_targets": offset_targets, "depth_targets": depth_targets, "lidar_mask": lidar_mask, "trunk_aspp": trunk_aspp, "aspp_first": aspp_first, "aspp_second": aspp_second, "trunk_neck": trunk_neck, "neck_first": neck_first, "neck_second": neck_second, "norm_params": norm_params, "norm_first": norm_first, "norm_second": norm_second, "decoders": decoders, "decoder_first": decoder_first, "decoder_second": decoder_second, "log_vars": log_vars, "log_first": log_first, "log_second": log_second}


EPSILON = 1e-05
BETA_ONE = 0.9
BETA_TWO = 0.95
ADAM_EPSILON = 1e-08
CLIP_LIMIT = 0.05
PRECISE = lax.Precision.HIGHEST
RATES = (12, 24, 36)

@jax.custom_vjp
def low(v):
    return lax.optimization_barrier(v.astype(jnp.bfloat16)).astype(jnp.float32)

@jax.custom_vjp
def low_back(v):
    return v

def low_keep(v):
    return (low(v), None)

def low_pass(kept, grad):
    return (grad,)

def back_keep(v):
    return (v, None)

def back_low(kept, grad):
    return (low(grad),)
low.defvjp(low_keep, low_pass)
low_back.defvjp(back_keep, back_low)

def unpack_front(flat):
    quarter = ASP // 4
    flat_line = flat.reshape(4, -1)
    first_end = quarter * FEAT
    taps_end = first_end + 27 * quarter * FEAT
    pool_end = taps_end + quarter * FEAT
    proj_end = pool_end + quarter * 5 * ASP
    one_w = flat_line[:, :first_end].reshape(ASP, FEAT)
    taps = flat_line[:, first_end:taps_end].reshape(4, 27, quarter, FEAT).transpose(1, 0, 2, 3).reshape(27, ASP, FEAT)
    pool_w = flat_line[:, taps_end:pool_end].reshape(ASP, FEAT)
    project_w = flat_line[:, pool_end:proj_end].reshape(ASP, 5 * ASP)
    return (one_w, taps, pool_w, project_w)

def unpack_back(flat):
    quarter = BOT // 4
    flat_line = flat.reshape(4, -1)
    first_end = quarter * FEAT
    second_end = first_end + 9 * quarter * BOT
    third_end = second_end + FEAT // 4 * BOT
    reduce_w = flat_line[:, :first_end].reshape(BOT, FEAT)
    middle = flat_line[:, first_end:second_end].reshape(4, 9, quarter, BOT).transpose(1, 0, 2, 3).reshape(9, BOT, BOT)
    expand_w = flat_line[:, second_end:third_end].reshape(FEAT, BOT)
    return (reduce_w, middle, expand_w)

def mixing(weight, input_grid):
    return jnp.einsum('oc,cnrw->onrw', weight, input_grid, precision=PRECISE)

def dilated(input_grid, tap_weights, dilation):
    padded = jnp.pad(input_grid, ((0, 0), (0, 0), (dilation, dilation), (dilation, dilation)))

    def one_tap(summed, tap_index):
        row_start = tap_index // 3 * dilation
        col_start = tap_index % 3 * dilation
        zero_start = jnp.zeros((), jnp.int32)
        window = lax.dynamic_slice(padded, (zero_start, zero_start, row_start, col_start), input_grid.shape)
        weight = lax.dynamic_index_in_dim(tap_weights, tap_index, 0, keepdims=False)
        return (summed + mixing(weight, window), None)
    initial = jnp.zeros((tap_weights.shape[1],) + input_grid.shape[1:], jnp.float32)
    summed, _ = lax.scan(jax.checkpoint(one_tap), initial, jnp.arange(9, dtype=jnp.int32))
    return summed

def norm_act(pre_norm, gain_vec, shift_vec, valid_mask, valid_count, residual):
    axes_sum = (1, 2, 3)
    mean_value = lax.optimization_barrier(jnp.sum(pre_norm * valid_mask, axis=axes_sum, keepdims=True)) / valid_count
    second = lax.optimization_barrier(jnp.sum(pre_norm * pre_norm * valid_mask, axis=axes_sum, keepdims=True)) / valid_count
    normed = (pre_norm - mean_value) * lax.rsqrt(second - mean_value * mean_value + EPSILON)
    activation_in = gain_vec[:, None, None, None] * normed + shift_vec[:, None, None, None] + residual
    return jax.nn.silu(activation_in) * valid_mask

def adam_step(weight, first_m, second_m, gradient, factor, rate, decay):
    clipped = gradient * factor
    new_first = BETA_ONE * first_m + (1.0 - BETA_ONE) * clipped
    new_second = BETA_TWO * second_m + (1.0 - BETA_TWO) * clipped * clipped
    corrected = new_first / (1.0 - BETA_ONE ** STEP) / (jnp.sqrt(new_second / (1.0 - BETA_TWO ** STEP)) + ADAM_EPSILON)
    return (weight - rate * (corrected + decay * weight), new_first, new_second)

def reference(features, crop_rows, crop_cols, labels, offset_targets, depth_targets, lidar_mask, trunk_aspp, aspp_first, aspp_second, trunk_neck, neck_first, neck_second, norm_params, norm_first, norm_second, decoders, decoder_first, decoder_second, log_vars, log_first, log_second):
    crop_total = crop_rows.shape[0]
    row_place = jnp.arange(CROP_ROWS, dtype=jnp.int32)
    col_place = jnp.arange(WIDTH, dtype=jnp.int32)
    valid_mask = ((row_place[None, :, None] < crop_rows[:, None, None]) & (col_place[None, None, :] < crop_cols[:, None, None])).astype(jnp.float32)[None]
    valid_count = jnp.sum(valid_mask)
    crop_count = lax.optimization_barrier(jnp.sum(valid_mask, axis=(2, 3), keepdims=True))
    valid_flat = valid_mask.reshape(-1)
    lidar_valid = lidar_mask.astype(jnp.float32) * valid_flat
    lidar_count = jnp.sum(lidar_valid)
    input_grid = features.astype(jnp.float32).reshape(FEAT, crop_total, CROP_ROWS, WIDTH) * valid_mask
    label_hot = (jnp.arange(CLS, dtype=jnp.int32)[:, None] == labels[None, :]).astype(jnp.float32)
    bounds = [0, BOT, 2 * BOT, 2 * BOT + FEAT, 2 * BOT + FEAT + 4 * ASP, 2 * BOT + FEAT + 5 * ASP]

    def forward(trunk_aspp, trunk_neck, norm_params, decoders, log_vars):
        one_w, aspp_taps, pool_w, project_w = unpack_front(low(trunk_aspp))
        reduce_w, middle, expand_w = unpack_back(low(trunk_neck))

        def norm_slot(pre_norm, slot_index, residual):
            return norm_act(pre_norm, norm_params[0, bounds[slot_index]:bounds[slot_index + 1]], norm_params[1, bounds[slot_index]:bounds[slot_index + 1]], valid_mask, valid_count, residual)
        act_one = low(norm_slot(low_back(mixing(reduce_w, input_grid)), 0, 0.0))
        act_two = low(norm_slot(low_back(dilated(act_one, middle, 4)), 1, 0.0))
        act_y = low(norm_slot(low_back(mixing(expand_w, act_two)), 2, input_grid))
        branches = [mixing(one_w, act_y)]
        for branch_slot, dilation in enumerate(RATES):
            branches.append(dilated(act_y, aspp_taps[9 * branch_slot:9 * branch_slot + 9], dilation))
        act_aspp = norm_slot(low_back(jnp.concatenate(branches, axis=0)), 3, 0.0)
        pooled = low(lax.optimization_barrier(jnp.sum(act_y * valid_mask, axis=(2, 3), keepdims=True)) / crop_count)
        pool_pre = low_back(mixing(pool_w, pooled))
        pool_map = jax.nn.silu(pool_pre) * valid_mask
        joined = low(jnp.concatenate([act_aspp, pool_map], axis=0))
        act_feat = low(norm_slot(low_back(mixing(project_w, joined)), 4, 0.0))
        flat_feat = act_feat.reshape(ASP, -1)
        low_dec = low(decoders)
        rows_of = ((0, CLS), (CLS, CLS + 2), (CLS + 2, CLS + 3))
        task_logits = []
        for task_slot in range(3):
            hidden = low(jax.nn.silu(low_back(jnp.dot(low_dec[task_slot * ASP:(task_slot + 1) * ASP], flat_feat, precision=PRECISE))))
            start_row, stop_row = rows_of[task_slot]
            task_logits.append(low_back(jnp.dot(low_dec[3 * ASP + start_row:3 * ASP + stop_row], hidden, precision=PRECISE)))
        sem_logits, off_logits, dep_logits = task_logits
        log_total = jax.nn.logsumexp(sem_logits, axis=0)
        sem_sum = jnp.sum((log_total - lax.optimization_barrier(jnp.sum(label_hot * sem_logits, axis=0))) * valid_flat)
        off_diff = off_logits - offset_targets
        off_sum = jnp.sum((jnp.sqrt(off_diff * off_diff + 1.0) - 1.0) * valid_flat)
        dep_diff = jax.nn.softplus(dep_logits[0]) - depth_targets
        dep_sum = jnp.sum((jnp.sqrt(dep_diff * dep_diff + 1.0) - 1.0) * lidar_valid)
        losses = jnp.stack([sem_sum / valid_count, off_sum / valid_count, dep_sum / lidar_count])
        return jnp.sum(jnp.exp(-log_vars) * losses + log_vars)
    total_loss, pullback = jax.vjp(forward, trunk_aspp, trunk_neck, norm_params, decoders, log_vars)
    gradients = pullback(jnp.ones_like(total_loss))
    square = sum((jnp.sum(gradient * gradient) for gradient in gradients))
    grad_norm = jnp.sqrt(square)
    factor = jnp.minimum(1.0, CLIP_LIMIT / grad_norm)
    aspp_out = adam_step(trunk_aspp, aspp_first, aspp_second, gradients[0], factor, 0.04, 0.01)
    neck_out = adam_step(trunk_neck, neck_first, neck_second, gradients[1], factor, 0.04, 0.01)
    norm_out = adam_step(norm_params, norm_first, norm_second, gradients[2], factor, 0.6, 0.0)
    dec_out = adam_step(decoders, decoder_first, decoder_second, gradients[3], factor, 0.12, 0.01)
    log_out = adam_step(log_vars, log_first, log_second, gradients[4], factor, 0.5, 0.0)
    return (total_loss, grad_norm, aspp_out[0], aspp_out[1], aspp_out[2], neck_out[0], neck_out[1], neck_out[2], norm_out[0], norm_out[1], norm_out[2], dec_out[0], dec_out[1], dec_out[2], log_out[0], log_out[1], log_out[2])
```

```python
import functools

import jax
import jax.numpy as jnp
from jax import lax
from jax.experimental import pallas as pl
from jax.experimental.pallas import tpu as pltpu
from jax.sharding import PartitionSpec as P

FEAT = 2048
BOT = 512
ASP = 256
CLS = 19
OUTS = 22
WIDTH = 128
CROP_DP = 4
QUAD = 512
STEP = 10

EPSILON = 1e-05
BETA_ONE = 0.9
BETA_TWO = 0.95
ADAM_EPSILON = 1e-08
CLIP_LIMIT = 0.05
RATES = (12, 24, 36)

BF = jnp.bfloat16
F32 = jnp.float32


def silu_slope(pre_norm):
    sigmoid_value = jax.nn.sigmoid(pre_norm)
    return sigmoid_value * (1.0 + pre_norm * (1.0 - sigmoid_value))


def dot(a, b, ca, cb):
    return lax.dot_general(a, b, ((ca, cb), ((), ())), preferred_element_type=F32)


def xor_move(x, axis, mask):
    n = lax.axis_size(axis)
    return lax.ppermute(x, axis, [(i, i ^ mask) for i in range(n)])


def xor_round(x, axis, bits):
    if len(bits) == 1:
        return x + xor_move(x, axis, bits[0])
    one, two = bits
    a = xor_move(x, axis, one)
    b = xor_move(x, axis, two)
    c = xor_move(x, axis, one | two)
    return (x + a) + (b + c)


def sum_crop(x):
    return xor_round(xor_round(x, "dp", (1,)), "dp", (2,))


def rounds_of(first, n):
    bits = []
    while first < n:
        bits.append(first)
        first *= 2
    return [tuple(bits[i : i + 2]) for i in range(0, len(bits), 2)]


def sum_dp(x):
    x = xor_round(x, "dp", (1,))
    for bits in rounds_of(2, lax.axis_size("dp")):
        x = xor_round(x, "dp", bits)
    return x


def sum_head(x):
    for bits in rounds_of(1, lax.axis_size("head")):
        x = xor_round(x, "head", bits)
    return x


def sum_all(x):
    return sum_head(sum_dp(x))


def pack(vectors):
    return jnp.concatenate([v.reshape(-1) for v in vectors])


def unpack(joined, sizes):
    out, at = [], 0
    for size in sizes:
        out.append(joined[at : at + size])
        at += size
    return out


def crop_shift(x, by):
    n = lax.axis_size("dp")
    pairs = [(i, i + by) for i in range(n) if i // CROP_DP == (i + by) // CROP_DP and 0 <= i + by < n]
    return lax.ppermute(x, "dp", pairs)


def line_shift(x, by):
    n = lax.axis_size("head")
    return lax.ppermute(x, "head", [(i, i + by) for i in range(n) if 0 <= i + by < n])


def gather_line(own, z):
    n = lax.axis_size("head")
    left, right = [own], [own]
    for _ in range(n - 1):
        left.append(line_shift(left[-1], 1))
        right.append(line_shift(right[-1], -1))
    blocks = []
    for j in range(n):
        block = None
        for at in range(n):
            source = own if at == j else (left[at - j] if at > j else right[j - at])
            block = source if block is None else jnp.where(z == at, source, block)
        blocks.append(block)
    return blocks


def shift_lanes(tile, by, lanes):
    if by == 0:
        return tile
    rolled = pltpu.roll(tile, (-by) % WIDTH, 1)
    keep = (lanes < WIDTH - by) if by > 0 else (lanes >= -by)
    return jnp.where(keep, rolled, 0.0)


def neck_columns_kernel(flip, ext_ref, out_ref):
    rows = ext_ref.shape[0]
    lanes = lax.broadcasted_iota(jnp.int32, (rows, WIDTH), 1)
    count = ext_ref.shape[1] // WIDTH
    for t in range(count):
        tile = ext_ref[:, t * WIDTH : (t + 1) * WIDTH].astype(F32)
        for j in range(3):
            moved = shift_lanes(tile, (j - 1) * 4, lanes).astype(BF)
            for i in range(3):
                at = t - 4 * i
                if 0 <= at < count - 8:
                    tap = 3 * i + j
                    out_ref[8 - tap if flip else tap, :, at * WIDTH : (at + 1) * WIDTH] = moved


def neck_columns(ext, flip):
    rows, width = ext.shape
    block = 64
    return pl.pallas_call(
        functools.partial(neck_columns_kernel, flip),
        grid=(rows // block,),
        in_specs=[pl.BlockSpec((block, width), lambda i: (i, 0))],
        out_specs=pl.BlockSpec((9, block, width - 1024), lambda i: (0, i, 0)),
        out_shape=jax.ShapeDtypeStruct((9, rows, width - 1024), BF),
        compiler_params=pltpu.CompilerParams(vmem_limit_bytes=40 << 20),
        cost_estimate=pl.CostEstimate(flops=0, bytes_accessed=2 * 12 * rows * width, transcendentals=0),
    )(ext)


def aspp_gather_kernel(p_ref, core_ref, side_ref, pool_ref):
    lanes = lax.broadcasted_iota(jnp.int32, (64, WIDTH), 1)
    core_ref[0] = p_ref[0:64, :]
    pool_sum = jnp.zeros((64, WIDTH), F32)
    for t in range(4):
        part = slice(t * WIDTH, (t + 1) * WIDTH)
        pool_sum = pool_sum + p_ref[64 * 28 : 64 * 29, part]
        for br, rate in enumerate(RATES):
            for i in range(3):
                total = None
                for j in range(3):
                    at = 64 * (1 + 9 * br + 3 * i + j)
                    moved = shift_lanes(p_ref[at : at + 64, part], (j - 1) * rate, lanes)
                    total = moved if total is None else total + moved
                if i == 1:
                    core_ref[1 + br, :, part] = total
                else:
                    side_ref[2 * br + i // 2, 0, :, part] = total.astype(BF)
    pool_ref[0] = pool_sum


def aspp_gather(products):
    rows, width = products.shape
    quads = width // QUAD
    return pl.pallas_call(
        aspp_gather_kernel,
        grid=(quads,),
        in_specs=[pl.BlockSpec((rows, QUAD), lambda a: (0, a))],
        out_specs=[
            pl.BlockSpec((4, 64, QUAD), lambda a: (0, 0, a)),
            pl.BlockSpec((6, 1, 64, QUAD), lambda a: (0, a, 0, 0)),
            pl.BlockSpec((1, 64, WIDTH), lambda a: (a, 0, 0)),
        ],
        out_shape=[
            jax.ShapeDtypeStruct((4, 64, width), F32),
            jax.ShapeDtypeStruct((6, quads, 64, QUAD), BF),
            jax.ShapeDtypeStruct((quads, 64, WIDTH), F32),
        ],
        compiler_params=pltpu.CompilerParams(vmem_limit_bytes=40 << 20),
        cost_estimate=pl.CostEstimate(flops=0, bytes_accessed=5 * rows * width, transcendentals=0),
    )(products)


def aspp_spread_kernel(one_ref, rows_ref, pool_ref, mask_ref, out_ref):
    lanes = lax.broadcasted_iota(jnp.int32, (64, WIDTH), 1)
    out_ref[0:64, :] = one_ref[...].astype(BF)
    for t in range(4):
        part = slice(t * WIDTH, (t + 1) * WIDTH)
        out_ref[64 * 28 : 64 * 29, part] = (pool_ref[...] * mask_ref[0:1, part]).astype(BF)
        for br, rate in enumerate(RATES):
            for i in range(3):
                tile = rows_ref[br, i, 0, :, part].astype(F32)
                for j in range(3):
                    at = 64 * (1 + 9 * br + 3 * i + j)
                    out_ref[at : at + 64, part] = shift_lanes(tile, (1 - j) * rate, lanes).astype(BF)


def aspp_spread(one, rows, pool, mask):
    width = one.shape[1]
    quads = width // QUAD
    count = 64 * 29
    return pl.pallas_call(
        aspp_spread_kernel,
        grid=(quads,),
        in_specs=[
            pl.BlockSpec((64, QUAD), lambda a: (0, a)),
            pl.BlockSpec((3, 3, 1, 64, QUAD), lambda a: (0, 0, a, 0, 0)),
            pl.BlockSpec((64, WIDTH), lambda a: (0, 0)),
            pl.BlockSpec((8, QUAD), lambda a: (0, a)),
        ],
        out_specs=pl.BlockSpec((count, QUAD), lambda a: (0, a)),
        out_shape=jax.ShapeDtypeStruct((count, width), BF),
        compiler_params=pltpu.CompilerParams(vmem_limit_bytes=40 << 20),
        cost_estimate=pl.CostEstimate(flops=0, bytes_accessed=3 * count * width, transcendentals=0),
    )(one, rows, pool, mask)


def side_rows(side):
    zero = jnp.zeros_like(side[0, :1])
    result = []
    from_one = crop_shift(jnp.concatenate([side[0, 1:4], side[2, 0:2]]), 1)
    from_two = crop_shift(jnp.concatenate([side[2, 2:4], side[4, 0:3]]), 2)
    from_three = crop_shift(side[4, 3:4], 3)
    to_one = crop_shift(jnp.concatenate([side[1, 0:3], side[3, 2:4]]), -1)
    to_two = crop_shift(jnp.concatenate([side[3, 0:2], side[5, 1:4]]), -2)
    to_three = crop_shift(side[5, 0:1], -3)
    del zero
    result.append(jnp.concatenate([from_one[0:3], side[0, 0:1]]))
    result.append(jnp.concatenate([side[1, 3:4], to_one[0:3]]))
    result.append(jnp.concatenate([from_two[0:2], from_one[3:5]]))
    result.append(jnp.concatenate([to_one[3:5], to_two[0:2]]))
    result.append(jnp.concatenate([from_three, from_two[2:5]]))
    result.append(jnp.concatenate([to_two[2:5], to_three]))
    return result


def adam_step(weight, first_m, second_m, gradient, factor, rate, decay):
    clipped = gradient * factor
    new_first = BETA_ONE * first_m + (1.0 - BETA_ONE) * clipped
    new_second = BETA_TWO * second_m + (1.0 - BETA_TWO) * clipped * clipped
    corrected = (
        new_first
        / (1.0 - BETA_ONE**STEP)
        / (jnp.sqrt(new_second / (1.0 - BETA_TWO**STEP)) + ADAM_EPSILON)
    )
    return (weight - rate * (corrected + decay * weight), new_first, new_second)


def flat_rows(quads):
    return jnp.concatenate([quads[a] for a in range(quads.shape[0])], axis=1)


def quad_blocks(flat):
    return [flat[..., a * QUAD : (a + 1) * QUAD] for a in range(flat.shape[-1] // QUAD)]


def shards(
    features,
    crop_rows,
    crop_cols,
    labels,
    offset_targets,
    depth_targets,
    lidar_mask,
    trunk_aspp,
    aspp_first,
    aspp_second,
    trunk_neck,
    neck_first,
    neck_second,
    norm_params,
    norm_first,
    norm_second,
    decoders,
    decoder_first,
    decoder_second,
    log_vars,
    log_first,
    log_second,
):
    heads = lax.axis_size("head")
    z = lax.axis_index("head")
    group = lax.axis_index("dp")
    crop = group // CROP_DP
    pixels = heads * QUAD
    share = 1.0 / heads
    quarter = ASP // heads

    neck_low = lax.all_gather(trunk_neck.astype(BF), "head", axis=0, tiled=True)
    neck_low = lax.all_gather(neck_low, "dp", axis=1, tiled=True)
    line = neck_low.reshape(heads, -1)
    first_end = BOT // heads * FEAT
    second_end = first_end + 9 * BOT // heads * BOT
    third_end = second_end + FEAT // heads * BOT
    reduce_w = line[:, :first_end].reshape(BOT, FEAT)
    middle = line[:, first_end:second_end].reshape(heads, 9, BOT // heads, BOT)
    middle = jnp.moveaxis(middle, 0, 1).reshape(9, BOT, BOT)
    expand_w = line[:, second_end:third_end].reshape(FEAT, BOT)

    x_group = lax.all_gather(features, "head", axis=1, tiled=True)
    aspp_low = lax.all_gather(trunk_aspp[0].astype(BF), "dp", axis=0, tiled=True)
    aspp_rows = aspp_low.reshape(-1, FEAT)
    tap_w = aspp_rows[: 29 * quarter]
    project_q = aspp_rows[29 * quarter :].reshape(quarter, 5 * ASP)
    project_w = lax.all_gather(project_q, "head", axis=0, tiled=True)
    project_own = lax.dynamic_slice_in_dim(
        project_w.reshape(ASP, 5, heads, quarter), z, 1, 2
    ).reshape(ASP, 5 * quarter)

    place = jnp.arange(pixels, dtype=jnp.int32)
    row_place = group % CROP_DP * (pixels // WIDTH) + place // WIDTH
    col_place = place % WIDTH
    mask = ((row_place < crop_rows[crop]) & (col_place < crop_cols[crop])).astype(F32)[None, :]
    mask_own = lax.dynamic_slice_in_dim(mask, z * QUAD, QUAD, 1)
    total_n = jnp.sum((crop_rows * crop_cols).astype(F32))
    crop_n = (crop_rows[crop] * crop_cols[crop]).astype(F32)

    def own_pixels(a):
        return lax.dynamic_slice_in_dim(a, z * QUAD, QUAD, a.ndim - 1)

    labels_own = own_pixels(labels)
    offset_own = own_pixels(offset_targets)
    depth_own = own_pixels(depth_targets)
    lidar_own = own_pixels(lidar_mask).astype(F32) * mask_own[0]

    gains, shifts = (norm_params[0], norm_params[1])
    bounds = [0, BOT, 2 * BOT, 2 * BOT + FEAT, 2 * BOT + FEAT + 4 * ASP, 2 * BOT + FEAT + 5 * ASP]

    def slot(vector, index):
        return vector[bounds[index] : bounds[index + 1]]

    def own_aspp(vector):
        return lax.dynamic_slice_in_dim(vector.reshape(4, heads, quarter), z, 1, 1).reshape(-1)

    gain_one, gain_two, gain_three, gain_proj = [slot(gains, i) for i in (0, 1, 2, 4)]
    shift_one, shift_two, shift_three, shift_proj = [slot(shifts, i) for i in (0, 1, 2, 4)]
    gain_aspp, shift_aspp = own_aspp(slot(gains, 3)), own_aspp(slot(shifts, 3))

    def moments(pre, m):
        masked = pre * m
        return jnp.sum(masked, axis=-1), jnp.sum(masked * pre, axis=-1)

    def coefficients(total, square):
        mean = total / total_n
        inv = lax.rsqrt(square / total_n - mean * mean + EPSILON)
        return mean, inv

    def normed(pre, mean, inv):
        return (pre - mean[:, None]) * inv[:, None]

    def scaled(hat, gain, shift):
        return gain[:, None] * hat + shift[:, None]

    x_own = features * mask_own.astype(BF)
    pre_one = jnp.dot(reduce_w, x_own, preferred_element_type=F32)
    sums = sum_all(pack((*moments(pre_one, mask_own), jnp.broadcast_to(jnp.sum(lidar_own), (128,)))))
    total, square, lidar = unpack(sums, (BOT, BOT, 128))
    lidar_n = lidar[0]
    mean_one, inv_one = coefficients(total, square)
    low_one = (jax.nn.silu(scaled(normed(pre_one, mean_one, inv_one), gain_one, shift_one)) * mask_own).astype(BF)
    blocks = gather_line(low_one, z)
    before = crop_shift(blocks[-1], 1)
    after = crop_shift(blocks[0], -1)
    h_one = jnp.concatenate(blocks, axis=1)
    columns = neck_columns(jnp.concatenate([before, h_one, after], axis=1), False)
    pre_two = lax.dot_general(middle, columns, (((0, 2), (0, 1)), ((), ())), preferred_element_type=F32)
    mean_two, inv_two = coefficients(*unpack(sum_dp(pack(moments(pre_two, mask))), (BOT, BOT)))
    hat_two = normed(pre_two, mean_two, inv_two)
    in_two = scaled(hat_two, gain_two, shift_two)
    h_two = (jax.nn.silu(in_two) * mask).astype(BF)
    pre_three = jnp.dot(expand_w, h_two, preferred_element_type=F32)
    mean_three, inv_three = coefficients(*unpack(sum_dp(pack(moments(pre_three, mask))), (FEAT, FEAT)))
    x_group = x_group * mask.astype(BF)
    hat_three = normed(pre_three, mean_three, inv_three)
    in_three = scaled(hat_three, gain_three, shift_three) + x_group.astype(F32)
    y = (jax.nn.silu(in_three) * mask).astype(BF)

    products = jnp.dot(tap_w, y, preferred_element_type=F32)
    middle_rows, side, pool_part = aspp_gather(products)
    moved = side_rows(side)
    branches = [middle_rows[0]]
    for br in range(3):
        branches.append(
            middle_rows[1 + br]
            + flat_rows(moved[2 * br]).astype(F32)
            + flat_rows(moved[2 * br + 1]).astype(F32)
        )
    pre_aspp = jnp.concatenate(branches, axis=0)
    pool_local = jnp.sum(pool_part, axis=(0, 2))
    local = pack((*moments(pre_aspp, mask), pool_local, jnp.zeros((64,), F32)))
    local = sum_crop(local)
    pool_sum = local[2 * ASP : 2 * ASP + quarter]
    for bits in rounds_of(4, lax.axis_size("dp")):
        local = xor_round(local, "dp", bits)
    mean_aspp, inv_aspp = coefficients(local[:ASP], local[ASP : 2 * ASP])
    hat_aspp = normed(pre_aspp, mean_aspp, inv_aspp)
    in_aspp = scaled(hat_aspp, gain_aspp, shift_aspp)
    act_aspp = jax.nn.silu(in_aspp) * mask
    pool_pre = pool_sum / crop_n
    joined = jnp.concatenate([act_aspp, jax.nn.silu(pool_pre)[:, None] * mask], axis=0).astype(BF)

    part_proj = jnp.dot(project_own, joined, preferred_element_type=F32)
    pre_proj = lax.psum_scatter(part_proj.astype(BF), "head", scatter_dimension=1, tiled=True).astype(F32)
    mean_proj, inv_proj = coefficients(*unpack(sum_all(pack(moments(pre_proj, mask_own))), (ASP, ASP)))
    hat_proj = normed(pre_proj, mean_proj, inv_proj)
    in_proj = scaled(hat_proj, gain_proj, shift_proj)
    feat = (jax.nn.silu(in_proj) * mask_own).astype(BF)

    low_dec = decoders.astype(BF)
    hidden_w, out_w = low_dec[: 3 * ASP], low_dec[3 * ASP :]
    dec_pre = jnp.dot(hidden_w, feat, preferred_element_type=F32)
    hidden = jax.nn.silu(dec_pre).astype(BF)
    row_sets = ((0, CLS), (CLS, CLS + 2), (CLS + 2, CLS + 3))
    logits = [
        jnp.dot(out_w, hidden[t * ASP : (t + 1) * ASP], preferred_element_type=F32)[lo:hi]
        for t, (lo, hi) in enumerate(row_sets)
    ]
    sem_logits, off_logits, dep_logits = logits
    valid_own = mask_own[0]
    label_hot = (jnp.arange(CLS, dtype=jnp.int32)[:, None] == labels_own[None, :]).astype(F32)
    log_total = jax.nn.logsumexp(sem_logits, axis=0)
    sem_sum = jnp.sum((log_total - jnp.sum(label_hot * sem_logits, axis=0)) * valid_own)
    off_diff = off_logits - offset_own
    off_root = jnp.sqrt(off_diff * off_diff + 1.0)
    off_sum = jnp.sum((off_root - 1.0) * valid_own)
    dep_logit = dep_logits[0]
    dep_diff = jax.nn.softplus(dep_logit) - depth_own
    dep_root = jnp.sqrt(dep_diff * dep_diff + 1.0)
    dep_sum = jnp.sum((dep_root - 1.0) * lidar_own)
    divisors = jnp.stack([total_n, total_n, lidar_n])
    weights = jnp.exp(-log_vars) / divisors
    grad_sem = (jax.nn.softmax(sem_logits, axis=0) - label_hot) * valid_own * weights[0]
    grad_off = off_diff / off_root * valid_own * weights[1]
    grad_dep = (dep_diff / dep_root * jax.nn.sigmoid(dep_logit) * lidar_own * weights[2])[None, :]
    grad_logits = [g.astype(BF) for g in (grad_sem, grad_off, grad_dep)]
    grad_out_w = []
    grad_hidden = []
    for t, (lo, hi) in enumerate(row_sets):
        grad_out_w.append(dot(grad_logits[t], hidden[t * ASP : (t + 1) * ASP], (1,), (1,)))
        grad_hidden.append(dot(out_w[lo:hi], grad_logits[t], (0,), (0,)))
    grad_dec_pre = (jnp.concatenate(grad_hidden, axis=0) * silu_slope(dec_pre)).astype(BF)
    grad_hidden_w = dot(grad_dec_pre, feat, (1,), (1,))
    grad_feat = dot(hidden_w, grad_dec_pre, (0,), (0,))
    dec_grad = lax.psum(jnp.concatenate([grad_hidden_w, *grad_out_w], axis=0), ("dp", "head"))

    grad_act = grad_feat * mask_own * silu_slope(in_proj)
    sums = sum_all(
        pack(
            (
                jnp.sum(grad_act, axis=-1),
                jnp.sum(grad_act * hat_proj, axis=-1),
                jnp.stack([sem_sum, off_sum, dep_sum]),
                jnp.zeros((125,), F32),
            )
        )
    )
    back_shift_proj, back_gain_proj, loss_sums = unpack(sums, (ASP, ASP, 3))
    losses = loss_sums / divisors
    total_loss = jnp.sum(jnp.exp(-log_vars) * losses + log_vars)
    grad_logvar = 1.0 - jnp.exp(-log_vars) * losses
    grad_proj = (
        mask_own
        * (gain_proj * inv_proj)[:, None]
        * (grad_act - (back_shift_proj / total_n)[:, None] - hat_proj * (back_gain_proj / total_n)[:, None])
    ).astype(BF)
    grad_proj = lax.all_gather(grad_proj, "head", axis=1, tiled=True)
    grad_project = dot(grad_proj, joined, (1,), (1,))
    grad_joined = dot(project_own, grad_proj, (0,), (0,))

    grad_act = grad_joined[:ASP] * mask * silu_slope(in_aspp)
    local = pack(
        (
            jnp.sum(grad_act, axis=-1),
            jnp.sum(grad_act * hat_aspp, axis=-1),
            jnp.sum(grad_joined[ASP:] * mask, axis=-1),
            jnp.zeros((64,), F32),
        )
    )
    local = sum_crop(local)
    pool_row = local[2 * ASP : 2 * ASP + quarter]
    for bits in rounds_of(4, lax.axis_size("dp")):
        local = xor_round(local, "dp", bits)
    back_shift_aspp, back_gain_aspp = local[:ASP], local[ASP : 2 * ASP]
    grad_aspp = (
        mask
        * (gain_aspp * inv_aspp)[:, None]
        * (grad_act - (back_shift_aspp / total_n)[:, None] - hat_aspp * (back_gain_aspp / total_n)[:, None])
    ).astype(BF)
    grad_pool = (pool_row * silu_slope(pool_pre)).astype(BF).astype(F32) / crop_n
    parts = [jnp.stack(quad_blocks(grad_aspp[quarter * (br + 1) : quarter * (br + 2)])) for br in range(3)]
    moved = side_rows(jnp.stack([part for part in parts for _ in range(2)]))
    rows = jnp.stack(
        [jnp.stack([moved[2 * br + 1], parts[br], moved[2 * br]]) for br in range(3)]
    )
    spread = aspp_spread(
        grad_aspp[:quarter],
        rows,
        jnp.broadcast_to(grad_pool[:, None], (quarter, WIDTH)),
        jnp.broadcast_to(mask, (8, pixels)),
    )
    grad_y = dot(tap_w, spread, (0,), (0,))
    grad_taps = dot(spread, y, (1,), (1,))

    grad_act = grad_y * mask * silu_slope(in_three)
    sums = sum_all(pack((jnp.sum(grad_act, axis=-1), jnp.sum(grad_act * hat_three, axis=-1))))
    back_shift_three, back_gain_three = unpack(sums, (FEAT, FEAT))

    def norm_back(grad_act, hat, gain, inv, back_shift, back_gain):
        scale = share / total_n
        return (
            mask
            * (gain * inv)[:, None]
            * (grad_act - (back_shift * scale)[:, None] - hat * (back_gain * scale)[:, None])
        ).astype(BF)

    grad_three = norm_back(grad_act, hat_three, gain_three, inv_three, back_shift_three, back_gain_three)
    grad_expand = dot(grad_three, h_two, (1,), (1,))
    grad_act = dot(expand_w, grad_three, (0,), (0,)) * mask * silu_slope(in_two)
    sums = sum_all(pack((jnp.sum(grad_act, axis=-1), jnp.sum(grad_act * hat_two, axis=-1))))
    back_shift_two, back_gain_two = unpack(sums, (BOT, BOT))
    grad_two = norm_back(grad_act, hat_two, gain_two, inv_two, back_shift_two, back_gain_two)
    before = crop_shift(grad_two[:, -QUAD:], 1)
    after = crop_shift(grad_two[:, :QUAD], -1)
    columns = neck_columns(jnp.concatenate([before, grad_two, after], axis=1), True)
    grad_middle = dot(columns, h_one, (2,), (1,))
    grad_h_one = lax.dot_general(middle, columns, (((0, 1), (0, 1)), ((), ())), preferred_element_type=F32)
    group_one = jnp.dot(reduce_w, x_group, preferred_element_type=F32)
    hat_one = normed(group_one, mean_one, inv_one)
    grad_act = grad_h_one * mask * silu_slope(scaled(hat_one, gain_one, shift_one))
    sums = sum_all(pack((jnp.sum(grad_act, axis=-1), jnp.sum(grad_act * hat_one, axis=-1))))
    back_shift_one, back_gain_one = unpack(sums, (BOT, BOT))
    grad_one = norm_back(grad_act, hat_one, gain_one, inv_one, back_shift_one, back_gain_one)
    grad_reduce = dot(grad_one, x_group, (1,), (1,))

    swapped = lax.all_to_all(
        grad_project.astype(BF).reshape(heads, quarter, 5 * quarter), "head", 0, 0, tiled=True
    )
    own_project = jnp.moveaxis(swapped.reshape(heads, quarter, 5, quarter), 0, 2).reshape(-1, FEAT)
    flat_aspp = jnp.concatenate([grad_taps.astype(BF), own_project], axis=0).reshape(-1, 128)
    shard_aspp = lax.psum_scatter(flat_aspp, "dp", scatter_dimension=0, tiled=True).astype(F32)[None]
    flat_neck = jnp.concatenate(
        [
            grad_reduce.astype(BF).reshape(heads, -1),
            jnp.moveaxis(grad_middle.astype(BF).reshape(9, heads, BOT // heads, BOT), 1, 0).reshape(heads, -1),
            grad_expand.astype(BF).reshape(heads, -1),
        ],
        axis=1,
    ).reshape(heads, -1, 128)
    flat_neck = lax.psum_scatter(flat_neck, "dp", scatter_dimension=1, tiled=True)
    shard_neck = lax.psum_scatter(flat_neck, "head", scatter_dimension=0, tiled=True).astype(F32)

    both = lax.all_gather(jnp.stack([back_gain_aspp, back_shift_aspp]).reshape(2, 4, quarter), "head", axis=2)
    both = both.reshape(2, 4 * ASP)
    grad_norms = jnp.stack(
        [
            jnp.concatenate([back_gain_one, back_gain_two, back_gain_three, both[0], back_gain_proj]),
            jnp.concatenate([back_shift_one, back_shift_two, back_shift_three, both[1], back_shift_proj]),
        ]
    )
    local_square = jnp.sum(shard_aspp * shard_aspp) + jnp.sum(shard_neck * shard_neck)
    total_square = (
        sum_all(jnp.broadcast_to(local_square, (128,)))[0]
        + jnp.sum(grad_norms * grad_norms)
        + jnp.sum(dec_grad * dec_grad)
        + jnp.sum(grad_logvar * grad_logvar)
    )
    grad_norm = jnp.sqrt(total_square)
    factor = jnp.minimum(1.0, CLIP_LIMIT / grad_norm)
    aspp_out = adam_step(trunk_aspp, aspp_first, aspp_second, shard_aspp, factor, 0.04, 0.01)
    neck_out = adam_step(trunk_neck, neck_first, neck_second, shard_neck, factor, 0.04, 0.01)
    norm_out = adam_step(norm_params, norm_first, norm_second, grad_norms, factor, 0.6, 0.0)
    dec_out = adam_step(decoders, decoder_first, decoder_second, dec_grad, factor, 0.12, 0.01)
    log_out = adam_step(log_vars, log_first, log_second, grad_logvar, factor, 0.5, 0.0)
    return (total_loss, grad_norm, *aspp_out, *neck_out, *norm_out, *dec_out, *log_out)


def solution(mesh):
    trunk = P("head", "dp", None)
    return jax.shard_map(
        shards,
        mesh=mesh,
        in_specs=(
            P(None, ("dp", "head")),
            P(),
            P(),
            P("dp"),
            P(None, "dp"),
            P("dp"),
            P("dp"),
            *[trunk] * 6,
            *[P()] * 9,
        ),
        out_specs=(P(), P(), *[trunk] * 6, *[P()] * 9),
        check_vma=False,
    )
```

```python
import functools

import jax
import jax.numpy as jnp
from jax import lax
from jax.experimental import pallas as pl
from jax.experimental.pallas import tpu as pltpu
from jax.sharding import PartitionSpec as P

FEAT = 2048
BOT = 512
ASP = 256
CLS = 19
OUTS = 22
WIDTH = 128
CROP_DP = 4
QUAD = 512
STEP = 10

EPSILON = 1e-05
BETA_ONE = 0.9
BETA_TWO = 0.95
ADAM_EPSILON = 1e-08
CLIP_LIMIT = 0.05
RATES = (12, 24, 36)

BF = jnp.bfloat16
F32 = jnp.float32


def silu_slope(pre_norm):
    sigmoid_value = jax.nn.sigmoid(pre_norm)
    return sigmoid_value * (1.0 + pre_norm * (1.0 - sigmoid_value))


def dot(a, b, ca, cb):
    return lax.dot_general(a, b, ((ca, cb), ((), ())), preferred_element_type=F32)


def xor_move(x, axis, mask):
    n = lax.axis_size(axis)
    return lax.ppermute(x, axis, [(i, i ^ mask) for i in range(n)])


def xor_round(x, axis, bits):
    if len(bits) == 1:
        return x + xor_move(x, axis, bits[0])
    one, two = bits
    a = xor_move(x, axis, one)
    b = xor_move(x, axis, two)
    c = xor_move(x, axis, one | two)
    return (x + a) + (b + c)


def sum_crop(x):
    return xor_round(xor_round(x, "dp", (1,)), "dp", (2,))


def rounds_of(first, n):
    bits = []
    while first < n:
        bits.append(first)
        first *= 2
    return [tuple(bits[i : i + 2]) for i in range(0, len(bits), 2)]


def sum_dp(x):
    x = xor_round(x, "dp", (1,))
    for bits in rounds_of(2, lax.axis_size("dp")):
        x = xor_round(x, "dp", bits)
    return x


def sum_head(x):
    for bits in rounds_of(1, lax.axis_size("head")):
        x = xor_round(x, "head", bits)
    return x


def sum_all(x):
    return sum_head(sum_dp(x))


def pack(vectors):
    return jnp.concatenate([v.reshape(-1) for v in vectors])


def unpack(joined, sizes):
    out, at = [], 0
    for size in sizes:
        out.append(joined[at : at + size])
        at += size
    return out


def crop_shift(x, by):
    n = lax.axis_size("dp")
    pairs = [(i, i + by) for i in range(n) if i // CROP_DP == (i + by) // CROP_DP and 0 <= i + by < n]
    return lax.ppermute(x, "dp", pairs)


def line_shift(x, by):
    n = lax.axis_size("head")
    return lax.ppermute(x, "head", [(i, i + by) for i in range(n) if 0 <= i + by < n])


def exchange(own):
    return [own] + [xor_move(own, "head", m) for m in range(1, lax.axis_size("head"))]


def in_order(blocks, z):
    stack = jnp.stack(blocks)
    return [lax.dynamic_index_in_dim(stack, z ^ j, 0, False) for j in range(len(blocks))]


def scatter_head(blocks, z):
    n = blocks.shape[0]
    total = lax.dynamic_index_in_dim(blocks, z, 0, False).astype(F32)
    for m in range(1, n):
        total = total + xor_move(lax.dynamic_index_in_dim(blocks, z ^ m, 0, False), "head", m).astype(F32)
    return total


def halve(t, axis, bits, bit, position):
    at = bits.index(bit)
    low = 1 << at
    shape = t.shape
    split = t.reshape(shape[:axis] + (shape[axis] // (2 * low), 2, low) + shape[axis + 1 :])
    mine = (position >> (bit.bit_length() - 1)) & 1
    keep = lax.dynamic_index_in_dim(split, mine, axis + 1, False)
    send = lax.dynamic_index_in_dim(split, 1 - mine, axis + 1, False)
    got = xor_move(send, "dp", bit)
    out = (keep.astype(F32) + got.astype(F32)).astype(BF)
    return out.reshape(shape[:axis] + (shape[axis] // 2,) + shape[axis + 1 :]), [x for x in bits if x != bit]


def scatter_dp(t, axis):
    n = lax.axis_size("dp")
    position = lax.axis_index("dp")
    bits = [1 << k for k in range(n.bit_length() - 1)]
    t, bits = halve(t, axis, bits, 1, position)
    t = yield (t,)
    t = t[0]
    half = t.shape[-1] // 2
    parts = [(t[..., :half], bits), (t[..., half:], bits)]
    order = [1 << k for k in range(1, n.bit_length() - 1)]
    for k in range(0, len(order), 2):
        pair = order[k : k + 2]
        for step in range(len(pair)):
            parts = [
                halve(part, axis, left, pair[step if h == 0 else len(pair) - 1 - step], position)
                for h, (part, left) in enumerate(parts)
            ]
            arrays = yield tuple(part for part, _ in parts)
            parts = [(array, left) for array, (_, left) in zip(arrays, parts)]
    return


def tie(*trees):
    return lax.optimization_barrier(trees)


def last_step(steps, now):
    while True:
        try:
            now = steps.send(now)
        except StopIteration:
            return jnp.concatenate(now, axis=-1) if len(now) > 1 else now[0]


def shift_lanes(tile, by, lanes):
    if by == 0:
        return tile
    rolled = pltpu.roll(tile, (-by) % WIDTH, 1)
    keep = (lanes < WIDTH - by) if by > 0 else (lanes >= -by)
    return jnp.where(keep, rolled, 0.0)


def neck_columns_kernel(flip, ext_ref, out_ref):
    rows = ext_ref.shape[0]
    lanes = lax.broadcasted_iota(jnp.int32, (rows, WIDTH), 1)
    count = ext_ref.shape[1] // WIDTH
    for t in range(count):
        tile = ext_ref[:, t * WIDTH : (t + 1) * WIDTH].astype(F32)
        for j in range(3):
            moved = shift_lanes(tile, (j - 1) * 4, lanes).astype(BF)
            for i in range(3):
                at = t - 4 * i
                if 0 <= at < count - 8:
                    tap = 3 * i + j
                    out_ref[8 - tap if flip else tap, :, at * WIDTH : (at + 1) * WIDTH] = moved


def neck_columns(ext, flip):
    rows, width = ext.shape
    block = 64
    return pl.pallas_call(
        functools.partial(neck_columns_kernel, flip),
        grid=(rows // block,),
        in_specs=[pl.BlockSpec((block, width), lambda i: (i, 0))],
        out_specs=pl.BlockSpec((9, block, width - 1024), lambda i: (0, i, 0)),
        out_shape=jax.ShapeDtypeStruct((9, rows, width - 1024), BF),
        compiler_params=pltpu.CompilerParams(vmem_limit_bytes=40 << 20),
        cost_estimate=pl.CostEstimate(flops=0, bytes_accessed=2 * 12 * rows * width, transcendentals=0),
    )(ext)


def frames_of(own_rows, n_dp):
    starts = [own_rows * s // 256 * 16 for s in range(n_dp)]
    ends = [-(-own_rows * (s + 1) // 16) for s in range(n_dp)]
    rows = max(end - start for start, end in zip(starts, ends))
    return starts, -(-rows // 16) * 16


def assemble_kernel(pieces, in_ref, out_ref):
    for start, stop, sources in pieces:
        total = None
        for s, at in sources:
            part = in_ref[s, at : at + stop - start, :]
            total = part if total is None else total + part
        out_ref[start:stop, :] = total


def assemble(framed, own_rows, total_rows):
    n_dp, frame_rows, width = framed.shape
    starts, _ = frames_of(own_rows, n_dp)
    rows = -(-total_rows // 16) * 16
    pieces = []
    for g in range(0, rows, 16):
        sources = tuple(
            (s, g - starts[s])
            for s in range(n_dp)
            if own_rows * s < (g + 16) * 16 and own_rows * (s + 1) > g * 16
        )
        if pieces and len(sources) == 1 and len(pieces[-1][2]) == 1 and pieces[-1][2][0][0] == sources[0][0]:
            pieces[-1] = (pieces[-1][0], g + 16, pieces[-1][2])
        else:
            pieces.append((g, g + 16, sources))
    block = 256
    return pl.pallas_call(
        functools.partial(assemble_kernel, pieces),
        grid=(width // block,),
        in_specs=[pl.BlockSpec((n_dp, frame_rows, block), lambda i: (0, 0, i))],
        out_specs=pl.BlockSpec((rows, block), lambda i: (0, i)),
        out_shape=jax.ShapeDtypeStruct((rows, width), BF),
        compiler_params=pltpu.CompilerParams(vmem_limit_bytes=40 << 20),
        cost_estimate=pl.CostEstimate(flops=0, bytes_accessed=4 * rows * width, transcendentals=0),
    )(framed)


def aspp_gather_kernel(p_ref, core_ref, side_ref, pool_ref):
    lanes = lax.broadcasted_iota(jnp.int32, (64, WIDTH), 1)
    core_ref[0] = p_ref[0:64, :]
    pool_sum = jnp.zeros((64, WIDTH), F32)
    for t in range(4):
        part = slice(t * WIDTH, (t + 1) * WIDTH)
        pool_sum = pool_sum + p_ref[64 * 28 : 64 * 29, part]
        for br, rate in enumerate(RATES):
            for i in range(3):
                total = None
                for j in range(3):
                    at = 64 * (1 + 9 * br + 3 * i + j)
                    moved = shift_lanes(p_ref[at : at + 64, part], (j - 1) * rate, lanes)
                    total = moved if total is None else total + moved
                if i == 1:
                    core_ref[1 + br, :, part] = total
                else:
                    side_ref[2 * br + i // 2, 0, :, part] = total.astype(BF)
    pool_ref[0] = pool_sum


def aspp_gather(products):
    rows, width = products.shape
    quads = width // QUAD
    return pl.pallas_call(
        aspp_gather_kernel,
        grid=(quads,),
        in_specs=[pl.BlockSpec((rows, QUAD), lambda a: (0, a))],
        out_specs=[
            pl.BlockSpec((4, 64, QUAD), lambda a: (0, 0, a)),
            pl.BlockSpec((6, 1, 64, QUAD), lambda a: (0, a, 0, 0)),
            pl.BlockSpec((1, 64, WIDTH), lambda a: (a, 0, 0)),
        ],
        out_shape=[
            jax.ShapeDtypeStruct((4, 64, width), F32),
            jax.ShapeDtypeStruct((6, quads, 64, QUAD), BF),
            jax.ShapeDtypeStruct((quads, 64, WIDTH), F32),
        ],
        compiler_params=pltpu.CompilerParams(vmem_limit_bytes=40 << 20),
        cost_estimate=pl.CostEstimate(flops=0, bytes_accessed=5 * rows * width, transcendentals=0),
    )(products)


def aspp_spread_kernel(one_ref, rows_ref, pool_ref, mask_ref, out_ref):
    lanes = lax.broadcasted_iota(jnp.int32, (64, WIDTH), 1)
    out_ref[0:64, :] = one_ref[...].astype(BF)
    for t in range(4):
        part = slice(t * WIDTH, (t + 1) * WIDTH)
        out_ref[64 * 28 : 64 * 29, part] = (pool_ref[...] * mask_ref[0:1, part]).astype(BF)
        for br, rate in enumerate(RATES):
            for i in range(3):
                tile = rows_ref[br, i, 0, :, part].astype(F32)
                for j in range(3):
                    at = 64 * (1 + 9 * br + 3 * i + j)
                    out_ref[at : at + 64, part] = shift_lanes(tile, (1 - j) * rate, lanes).astype(BF)


def aspp_spread(one, rows, pool, mask):
    width = one.shape[1]
    quads = width // QUAD
    count = 64 * 29
    return pl.pallas_call(
        aspp_spread_kernel,
        grid=(quads,),
        in_specs=[
            pl.BlockSpec((64, QUAD), lambda a: (0, a)),
            pl.BlockSpec((3, 3, 1, 64, QUAD), lambda a: (0, 0, a, 0, 0)),
            pl.BlockSpec((64, WIDTH), lambda a: (0, 0)),
            pl.BlockSpec((8, QUAD), lambda a: (0, a)),
        ],
        out_specs=pl.BlockSpec((count, QUAD), lambda a: (0, a)),
        out_shape=jax.ShapeDtypeStruct((count, width), BF),
        compiler_params=pltpu.CompilerParams(vmem_limit_bytes=40 << 20),
        cost_estimate=pl.CostEstimate(flops=0, bytes_accessed=3 * count * width, transcendentals=0),
    )(one, rows, pool, mask)


def side_rows(side):
    zero = jnp.zeros_like(side[0, :1])
    result = []
    from_one = crop_shift(jnp.concatenate([side[0, 1:4], side[2, 0:2]]), 1)
    from_two = crop_shift(jnp.concatenate([side[2, 2:4], side[4, 0:3]]), 2)
    from_three = crop_shift(side[4, 3:4], 3)
    to_one = crop_shift(jnp.concatenate([side[1, 0:3], side[3, 2:4]]), -1)
    to_two = crop_shift(jnp.concatenate([side[3, 0:2], side[5, 1:4]]), -2)
    to_three = crop_shift(side[5, 0:1], -3)
    del zero
    result.append(jnp.concatenate([from_one[0:3], side[0, 0:1]]))
    result.append(jnp.concatenate([side[1, 3:4], to_one[0:3]]))
    result.append(jnp.concatenate([from_two[0:2], from_one[3:5]]))
    result.append(jnp.concatenate([to_one[3:5], to_two[0:2]]))
    result.append(jnp.concatenate([from_three, from_two[2:5]]))
    result.append(jnp.concatenate([to_two[2:5], to_three]))
    return result


def adam_step(weight, first_m, second_m, gradient, factor, rate, decay):
    clipped = gradient * factor
    new_first = BETA_ONE * first_m + (1.0 - BETA_ONE) * clipped
    new_second = BETA_TWO * second_m + (1.0 - BETA_TWO) * clipped * clipped
    corrected = (
        new_first
        / (1.0 - BETA_ONE**STEP)
        / (jnp.sqrt(new_second / (1.0 - BETA_TWO**STEP)) + ADAM_EPSILON)
    )
    return (weight - rate * (corrected + decay * weight), new_first, new_second)


def flat_rows(quads):
    return jnp.concatenate([quads[a] for a in range(quads.shape[0])], axis=1)


def quad_blocks(flat):
    return [flat[..., a * QUAD : (a + 1) * QUAD] for a in range(flat.shape[-1] // QUAD)]


def shards(
    features,
    crop_rows,
    crop_cols,
    labels,
    offset_targets,
    depth_targets,
    lidar_mask,
    trunk_aspp,
    aspp_first,
    aspp_second,
    trunk_neck,
    neck_first,
    neck_second,
    norm_params,
    norm_first,
    norm_second,
    decoders,
    decoder_first,
    decoder_second,
    log_vars,
    log_first,
    log_second,
):
    heads = lax.axis_size("head")
    z = lax.axis_index("head")
    group = lax.axis_index("dp")
    crop = group // CROP_DP
    pixels = heads * QUAD
    share = 1.0 / heads
    quarter = ASP // heads

    n_dp = lax.axis_size("dp")
    neck_low = trunk_neck.reshape(1, -1, BOT).astype(BF)
    neck_low = lax.all_gather(neck_low, "head", axis=0, tiled=True)
    neck_low = lax.all_gather(neck_low, "dp", axis=1, tiled=True)
    first_end = FEAT // heads
    second_end = first_end + 9 * BOT // heads
    reduce_w = neck_low[:, :first_end].reshape(BOT, FEAT)
    middle = neck_low[:, first_end:second_end].reshape(heads, 9, BOT // heads, BOT)
    middle = jnp.moveaxis(middle, 0, 1).reshape(9, BOT, BOT)
    expand_w = neck_low[:, second_end:].reshape(FEAT, BOT)

    x_left, x_right = [features], [features]
    for _ in range(heads // 2):
        x_left.append(line_shift(x_left[-1], 1))
        x_right.append(line_shift(x_right[-1], -1))

    flat_total = trunk_aspp.shape[1] * n_dp // 16
    own_rows = trunk_aspp.shape[1]
    frames, frame_rows = frames_of(own_rows, n_dp)
    inset = (group * own_rows) % 256
    framed = lax.dynamic_update_slice_in_dim(
        jnp.zeros((frame_rows * 16, 128), F32), trunk_aspp[0], inset, 0
    )
    framed = framed.reshape(frame_rows, FEAT).astype(BF)
    aspp_rows = assemble(lax.all_gather(framed, "dp", axis=0), own_rows, flat_total)
    tap_w = aspp_rows[: 29 * quarter]
    project_q = aspp_rows[29 * quarter : flat_total].reshape(quarter, 5, heads, quarter)
    project_q = jnp.moveaxis(project_q, 2, 0).reshape(heads, quarter, 5 * quarter)
    received = [lax.dynamic_index_in_dim(project_q, z, 0, False)]
    for m in range(1, heads):
        received.append(xor_move(lax.dynamic_index_in_dim(project_q, z ^ m, 0, False), "head", m))
    project_own = jnp.concatenate(in_order(received, z), axis=0)
    tap_w, tap_wt, project_own = lax.optimization_barrier((tap_w, tap_w.T, project_own))

    place = jnp.arange(pixels, dtype=jnp.int32)
    row_place = group % CROP_DP * (pixels // WIDTH) + place // WIDTH
    col_place = place % WIDTH
    mask = ((row_place < crop_rows[crop]) & (col_place < crop_cols[crop])).astype(F32)[None, :]
    mask_own = lax.dynamic_slice_in_dim(mask, z * QUAD, QUAD, 1)
    total_n = jnp.sum((crop_rows * crop_cols).astype(F32))
    crop_n = (crop_rows[crop] * crop_cols[crop]).astype(F32)

    def own_pixels(a):
        return lax.dynamic_slice_in_dim(a, z * QUAD, QUAD, a.ndim - 1)

    labels_own = own_pixels(labels)
    offset_own = own_pixels(offset_targets)
    depth_own = own_pixels(depth_targets)
    lidar_own = own_pixels(lidar_mask).astype(F32) * mask_own[0]

    gains, shifts = (norm_params[0], norm_params[1])
    bounds = [0, BOT, 2 * BOT, 2 * BOT + FEAT, 2 * BOT + FEAT + 4 * ASP, 2 * BOT + FEAT + 5 * ASP]

    def slot(vector, index):
        return vector[bounds[index] : bounds[index + 1]]

    def own_aspp(vector):
        return lax.dynamic_slice_in_dim(vector.reshape(4, heads, quarter), z, 1, 1).reshape(-1)

    gain_one, gain_two, gain_three, gain_proj = [slot(gains, i) for i in (0, 1, 2, 4)]
    shift_one, shift_two, shift_three, shift_proj = [slot(shifts, i) for i in (0, 1, 2, 4)]
    gain_aspp, shift_aspp = own_aspp(slot(gains, 3)), own_aspp(slot(shifts, 3))

    def moments(pre, m):
        masked = pre * m
        return jnp.sum(masked, axis=-1), jnp.sum(masked * pre, axis=-1)

    def coefficients(total, square):
        mean = total / total_n
        inv = lax.rsqrt(square / total_n - mean * mean + EPSILON)
        return mean, inv

    def normed(pre, mean, inv):
        return (pre - mean[:, None]) * inv[:, None]

    def scaled(hat, gain, shift):
        return gain[:, None] * hat + shift[:, None]

    x_own = features * mask_own.astype(BF)
    pre_one = jnp.dot(reduce_w, x_own, preferred_element_type=F32)
    sums = sum_all(pack((*moments(pre_one, mask_own), jnp.broadcast_to(jnp.sum(lidar_own), (128,)))))
    total, square, lidar = unpack(sums, (BOT, BOT, 128))
    lidar_n = lidar[0]
    mean_one, inv_one = coefficients(total, square)
    low_one = (jax.nn.silu(scaled(normed(pre_one, mean_one, inv_one), gain_one, shift_one)) * mask_own).astype(BF)
    blocks = in_order(exchange(low_one), z)
    before = crop_shift(blocks[-1], 1)
    after = crop_shift(blocks[0], -1)
    h_one = jnp.concatenate(blocks, axis=1)
    columns = neck_columns(jnp.concatenate([before, h_one, after], axis=1), False)
    columns, x_left[-1], x_right[-1] = tie(columns, x_left[-1], x_right[-1])
    for _ in range(heads // 2, heads - 1):
        x_left.append(line_shift(x_left[-1], 1))
        x_right.append(line_shift(x_right[-1], -1))
    pre_two = lax.dot_general(middle, columns, (((0, 2), (0, 1)), ((), ())), preferred_element_type=F32)
    mean_two, inv_two = coefficients(*unpack(sum_dp(pack(moments(pre_two, mask))), (BOT, BOT)))
    hat_two = normed(pre_two, mean_two, inv_two)
    in_two = scaled(hat_two, gain_two, shift_two)
    h_two = (jax.nn.silu(in_two) * mask).astype(BF)
    pre_three = jnp.dot(expand_w, h_two, preferred_element_type=F32)
    mean_three, inv_three = coefficients(*unpack(sum_dp(pack(moments(pre_three, mask))), (FEAT, FEAT)))
    ring = [features]
    for k in range(1, heads):
        ring.append(jnp.where(z + k < heads, x_right[k], x_left[heads - k]))
    ring = jnp.stack(ring)
    x_group = jnp.concatenate(
        [lax.dynamic_index_in_dim(ring, (a - z) % heads, 0, False) for a in range(heads)], axis=1
    )
    x_group = x_group * mask.astype(BF)
    hat_three = normed(pre_three, mean_three, inv_three)
    in_three = scaled(hat_three, gain_three, shift_three) + x_group.astype(F32)
    y = (jax.nn.silu(in_three) * mask).astype(BF)

    products = jnp.dot(tap_w, y, preferred_element_type=F32)
    middle_rows, side, pool_part = aspp_gather(products)
    moved = side_rows(side)
    branches = [middle_rows[0]]
    for br in range(3):
        branches.append(
            middle_rows[1 + br]
            + flat_rows(moved[2 * br]).astype(F32)
            + flat_rows(moved[2 * br + 1]).astype(F32)
        )
    pre_aspp = jnp.concatenate(branches, axis=0)
    pool_local = jnp.sum(pool_part, axis=(0, 2))
    local = pack((*moments(pre_aspp, mask), pool_local, jnp.zeros((64,), F32)))
    local = sum_crop(local)
    pool_sum = local[2 * ASP : 2 * ASP + quarter]
    for bits in rounds_of(4, lax.axis_size("dp")):
        local = xor_round(local, "dp", bits)
    mean_aspp, inv_aspp = coefficients(local[:ASP], local[ASP : 2 * ASP])
    hat_aspp = normed(pre_aspp, mean_aspp, inv_aspp)
    in_aspp = scaled(hat_aspp, gain_aspp, shift_aspp)
    act_aspp = jax.nn.silu(in_aspp) * mask
    pool_pre = pool_sum / crop_n
    joined = jnp.concatenate([act_aspp, jax.nn.silu(pool_pre)[:, None] * mask], axis=0).astype(BF)

    part_proj = jnp.dot(project_own, joined, preferred_element_type=F32)
    pre_proj = scatter_head(jnp.stack(quad_blocks(part_proj.astype(BF))), z)
    mean_proj, inv_proj = coefficients(*unpack(sum_all(pack(moments(pre_proj, mask_own))), (ASP, ASP)))
    hat_proj = normed(pre_proj, mean_proj, inv_proj)
    in_proj = scaled(hat_proj, gain_proj, shift_proj)
    feat = (jax.nn.silu(in_proj) * mask_own).astype(BF)

    low_dec = decoders.astype(BF)
    hidden_w, out_w = low_dec[: 3 * ASP], low_dec[3 * ASP :]
    dec_pre = jnp.dot(hidden_w, feat, preferred_element_type=F32)
    hidden = jax.nn.silu(dec_pre).astype(BF)
    row_sets = ((0, CLS), (CLS, CLS + 2), (CLS + 2, CLS + 3))
    logits = [
        jnp.dot(out_w, hidden[t * ASP : (t + 1) * ASP], preferred_element_type=F32)[lo:hi]
        for t, (lo, hi) in enumerate(row_sets)
    ]
    sem_logits, off_logits, dep_logits = logits
    valid_own = mask_own[0]
    label_hot = (jnp.arange(CLS, dtype=jnp.int32)[:, None] == labels_own[None, :]).astype(F32)
    log_total = jax.nn.logsumexp(sem_logits, axis=0)
    sem_sum = jnp.sum((log_total - jnp.sum(label_hot * sem_logits, axis=0)) * valid_own)
    off_diff = off_logits - offset_own
    off_root = jnp.sqrt(off_diff * off_diff + 1.0)
    off_sum = jnp.sum((off_root - 1.0) * valid_own)
    dep_logit = dep_logits[0]
    dep_diff = jax.nn.softplus(dep_logit) - depth_own
    dep_root = jnp.sqrt(dep_diff * dep_diff + 1.0)
    dep_sum = jnp.sum((dep_root - 1.0) * lidar_own)
    divisors = jnp.stack([total_n, total_n, lidar_n])
    weights = jnp.exp(-log_vars) / divisors
    grad_sem = (jax.nn.softmax(sem_logits, axis=0) - label_hot) * valid_own * weights[0]
    grad_off = off_diff / off_root * valid_own * weights[1]
    grad_dep = (dep_diff / dep_root * jax.nn.sigmoid(dep_logit) * lidar_own * weights[2])[None, :]
    grad_logits = [g.astype(BF) for g in (grad_sem, grad_off, grad_dep)]
    grad_out_w = []
    grad_hidden = []
    for t, (lo, hi) in enumerate(row_sets):
        grad_out_w.append(dot(grad_logits[t], hidden[t * ASP : (t + 1) * ASP], (1,), (1,)))
        grad_hidden.append(dot(out_w[lo:hi], grad_logits[t], (0,), (0,)))
    grad_dec_pre = (jnp.concatenate(grad_hidden, axis=0) * silu_slope(dec_pre)).astype(BF)
    grad_hidden_w = dot(grad_dec_pre, feat, (1,), (1,))
    grad_feat = dot(hidden_w, grad_dec_pre, (0,), (0,))
    dec_grad = lax.psum(jnp.concatenate([grad_hidden_w, *grad_out_w], axis=0), ("dp", "head"))

    grad_act = grad_feat * mask_own * silu_slope(in_proj)
    sums = sum_all(
        pack(
            (
                jnp.sum(grad_act, axis=-1),
                jnp.sum(grad_act * hat_proj, axis=-1),
                jnp.stack([sem_sum, off_sum, dep_sum]),
                jnp.zeros((125,), F32),
            )
        )
    )
    back_shift_proj, back_gain_proj, loss_sums = unpack(sums, (ASP, ASP, 3))
    losses = loss_sums / divisors
    total_loss = jnp.sum(jnp.exp(-log_vars) * losses + log_vars)
    grad_logvar = 1.0 - jnp.exp(-log_vars) * losses
    grad_proj = (
        mask_own
        * (gain_proj * inv_proj)[:, None]
        * (grad_act - (back_shift_proj / total_n)[:, None] - hat_proj * (back_gain_proj / total_n)[:, None])
    ).astype(BF)
    grad_proj = jnp.concatenate(in_order(exchange(grad_proj), z), axis=1)
    grad_project = dot(grad_proj, joined, (1,), (1,)).astype(BF).reshape(heads, quarter, 5 * quarter)
    grad_joined = dot(project_own, grad_proj, (0,), (0,))

    grad_act = grad_joined[:ASP] * mask * silu_slope(in_aspp)
    local = pack(
        (
            jnp.sum(grad_act, axis=-1),
            jnp.sum(grad_act * hat_aspp, axis=-1),
            jnp.sum(grad_joined[ASP:] * mask, axis=-1),
            jnp.zeros((64,), F32),
        )
    )
    local = sum_crop(local)
    pool_row = local[2 * ASP : 2 * ASP + quarter]
    for bits in rounds_of(4, lax.axis_size("dp")):
        local = xor_round(local, "dp", bits)
    back_shift_aspp, back_gain_aspp = local[:ASP], local[ASP : 2 * ASP]
    grad_aspp = (
        mask
        * (gain_aspp * inv_aspp)[:, None]
        * (grad_act - (back_shift_aspp / total_n)[:, None] - hat_aspp * (back_gain_aspp / total_n)[:, None])
    ).astype(BF)
    grad_pool = (pool_row * silu_slope(pool_pre)).astype(BF).astype(F32) / crop_n
    parts = [jnp.stack(quad_blocks(grad_aspp[quarter * (br + 1) : quarter * (br + 2)])) for br in range(3)]
    moved = side_rows(jnp.stack([part for part in parts for _ in range(2)]))
    rows = jnp.stack(
        [jnp.stack([moved[2 * br + 1], parts[br], moved[2 * br]]) for br in range(3)]
    )
    spread = aspp_spread(
        grad_aspp[:quarter],
        rows,
        jnp.broadcast_to(grad_pool[:, None], (quarter, WIDTH)),
        jnp.broadcast_to(mask, (8, pixels)),
    )
    grad_y = dot(tap_wt, spread, (1,), (0,))
    grad_taps = dot(spread, y, (1,), (1,)).astype(BF)

    grad_act = grad_y * mask * silu_slope(in_three)
    spread_norms = jnp.stack([back_gain_aspp, back_shift_aspp]).reshape(2, 4, 1, quarter)
    own_place = (jnp.arange(heads) == z)[None, None, :, None] & (group == 0)
    spread_norms = jnp.where(own_place, spread_norms, 0.0)
    sums = sum_all(pack((jnp.sum(grad_act, axis=-1), jnp.sum(grad_act * hat_three, axis=-1), spread_norms)))

    swapped = [
        xor_move(lax.dynamic_index_in_dim(grad_project, z ^ m, 0, False), "head", m)
        if m
        else lax.dynamic_index_in_dim(grad_project, z, 0, False)
        for m in range(heads)
    ]
    own_project = jnp.stack(in_order(swapped, z)).reshape(heads, quarter, 5, quarter)
    own_project = jnp.moveaxis(own_project, 0, 2).reshape(-1, FEAT)
    whole = jnp.concatenate(
        [grad_taps, own_project, jnp.zeros((-flat_total % 16, FEAT), BF)], axis=0
    )
    framed = jnp.stack([whole[start : start + frame_rows] for start in frames])
    sums, framed, dec_grad = tie(sums, framed, dec_grad)
    aspp_steps = scatter_dp(framed, 0)
    aspp_now = next(aspp_steps)
    back_shift_three, back_gain_three, both = unpack(sums, (FEAT, FEAT, 8 * ASP))
    both = both.reshape(2, 4 * ASP)

    def norm_back(grad_act, hat, gain, inv, back_shift, back_gain):
        scale = share / total_n
        return (
            mask
            * (gain * inv)[:, None]
            * (grad_act - (back_shift * scale)[:, None] - hat * (back_gain * scale)[:, None])
        ).astype(BF)

    grad_three = norm_back(grad_act, hat_three, gain_three, inv_three, back_shift_three, back_gain_three)
    grad_act = dot(expand_w, grad_three, (0,), (0,)) * mask * silu_slope(in_two)
    sums = sum_all(pack((jnp.sum(grad_act, axis=-1), jnp.sum(grad_act * hat_two, axis=-1))))
    grad_expand = dot(grad_three, h_two, (1,), (1,)).astype(BF).reshape(heads, n_dp, -1, BOT)
    sums, grad_expand, aspp_now = tie(sums, grad_expand, aspp_now)
    aspp_now = aspp_steps.send(aspp_now)
    expand_steps = scatter_dp(grad_expand, 1)
    expand_now = next(expand_steps)
    back_shift_two, back_gain_two = unpack(sums, (BOT, BOT))
    grad_two = norm_back(grad_act, hat_two, gain_two, inv_two, back_shift_two, back_gain_two)
    before = crop_shift(grad_two[:, -QUAD:], 1)
    after = crop_shift(grad_two[:, :QUAD], -1)
    columns = neck_columns(jnp.concatenate([before, grad_two, after], axis=1), True)
    grad_h_one = lax.dot_general(middle, columns, (((0, 1), (0, 1)), ((), ())), preferred_element_type=F32)
    group_one = jnp.dot(reduce_w, x_group, preferred_element_type=F32)
    hat_one = normed(group_one, mean_one, inv_one)
    grad_act = grad_h_one * mask * silu_slope(scaled(hat_one, gain_one, shift_one))
    sums = sum_all(pack((jnp.sum(grad_act, axis=-1), jnp.sum(grad_act * hat_one, axis=-1))))
    grad_middle = dot(columns, h_one, (2,), (1,)).astype(BF).reshape(9, heads, n_dp, -1, BOT)
    sums, grad_middle, aspp_now, expand_now = tie(sums, grad_middle, aspp_now, expand_now)
    aspp_block = last_step(aspp_steps, aspp_now)
    expand_block = last_step(expand_steps, expand_now)
    middle_steps = scatter_dp(grad_middle, 2)
    middle_block = last_step(middle_steps, next(middle_steps))
    back_shift_one, back_gain_one = unpack(sums, (BOT, BOT))
    grad_one = norm_back(grad_act, hat_one, gain_one, inv_one, back_shift_one, back_gain_one)
    grad_reduce = dot(grad_one, x_group, (1,), (1,)).astype(BF).reshape(heads, n_dp, -1, FEAT)
    reduce_steps = scatter_dp(grad_reduce, 1)
    reduce_block = last_step(reduce_steps, next(reduce_steps))

    shard_aspp = lax.dynamic_slice_in_dim(
        aspp_block.astype(F32).reshape(frame_rows * 16, 128), inset, own_rows, 0
    )[None]
    expand_own = scatter_head(expand_block.reshape(heads, -1, BOT), z)
    middle_own = scatter_head(jnp.moveaxis(middle_block.reshape(9, heads, -1, BOT), 1, 0), z)
    reduce_own = scatter_head(reduce_block.reshape(heads, -1, FEAT), z)
    expand_all = lax.all_gather(expand_own, "dp", axis=0, tiled=True)
    middle_all = lax.all_gather(middle_own, "dp", axis=1, tiled=True)
    reduce_all = lax.all_gather(reduce_own, "dp", axis=0, tiled=True)
    neck_rows = jnp.concatenate(
        [reduce_all.reshape(-1, BOT), middle_all.reshape(-1, BOT), expand_all], axis=0
    )
    shard_neck = lax.dynamic_slice_in_dim(
        neck_rows, group * (neck_rows.shape[0] // n_dp), neck_rows.shape[0] // n_dp, 0
    ).reshape(trunk_neck.shape)

    grad_norms = jnp.stack(
        [
            jnp.concatenate([back_gain_one, back_gain_two, back_gain_three, both[0], back_gain_proj]),
            jnp.concatenate([back_shift_one, back_shift_two, back_shift_three, both[1], back_shift_proj]),
        ]
    )
    local_square = (
        jnp.sum(shard_aspp * shard_aspp)
        + jnp.sum(expand_own * expand_own)
        + jnp.sum(middle_own * middle_own)
        + jnp.sum(reduce_own * reduce_own)
    )
    total_square = (
        sum_all(jnp.broadcast_to(local_square, (128,)))[0]
        + jnp.sum(grad_norms * grad_norms)
        + jnp.sum(dec_grad * dec_grad)
        + jnp.sum(grad_logvar * grad_logvar)
    )
    grad_norm = jnp.sqrt(total_square)
    factor = jnp.minimum(1.0, CLIP_LIMIT / grad_norm)
    aspp_out = adam_step(trunk_aspp, aspp_first, aspp_second, shard_aspp, factor, 0.04, 0.01)
    neck_out = adam_step(trunk_neck, neck_first, neck_second, shard_neck, factor, 0.04, 0.01)
    norm_out = adam_step(norm_params, norm_first, norm_second, grad_norms, factor, 0.6, 0.0)
    dec_out = adam_step(decoders, decoder_first, decoder_second, dec_grad, factor, 0.12, 0.01)
    log_out = adam_step(log_vars, log_first, log_second, grad_logvar, factor, 0.5, 0.0)
    return (total_loss, grad_norm, *aspp_out, *neck_out, *norm_out, *dec_out, *log_out)


def solution(mesh):
    trunk = P("head", "dp", None)
    return jax.shard_map(
        shards,
        mesh=mesh,
        in_specs=(
            P(None, ("dp", "head")),
            P(),
            P(),
            P("dp"),
            P(None, "dp"),
            P("dp"),
            P("dp"),
            *[trunk] * 6,
            *[P()] * 9,
        ),
        out_specs=(P(), P(), *[trunk] * 6, *[P()] * 9),
        check_vma=False,
    )
```

```python
import functools

import jax
import jax.numpy as jnp
import numpy as np
from jax import lax
from jax.experimental import pallas as pl
from jax.experimental.pallas import tpu as pltpu
from jax.sharding import PartitionSpec as P

FEAT = 2048
BOT = 512
ASP = 256
CLS = 19
OUTS = 22
WIDTH = 128
CROP_DP = 4
QUAD = 512
STEP = 10

EPSILON = 1e-05
BETA_ONE = 0.9
BETA_TWO = 0.95
ADAM_EPSILON = 1e-08
CLIP_LIMIT = 0.05
RATES = (12, 24, 36)

BF = jnp.bfloat16
F32 = jnp.float32


def silu_slope(pre_norm):
    sigmoid_value = jax.nn.sigmoid(pre_norm)
    return sigmoid_value * (1.0 + pre_norm * (1.0 - sigmoid_value))


def dot(a, b, ca, cb):
    return lax.dot_general(a, b, ((ca, cb), ((), ())), preferred_element_type=F32)


def xor_move(x, axis, mask):
    n = lax.axis_size(axis)
    return lax.ppermute(x, axis, [(i, i ^ mask) for i in range(n)])


def xor_round(x, axis, bits):
    if len(bits) == 1:
        return x + xor_move(x, axis, bits[0])
    one, two = bits
    a = xor_move(x, axis, one)
    b = xor_move(x, axis, two)
    c = xor_move(x, axis, one | two)
    return (x + a) + (b + c)


def sum_crop(x):
    return xor_round(xor_round(x, "dp", (1,)), "dp", (2,))


def rounds_of(first, n):
    bits = []
    while first < n:
        bits.append(first)
        first *= 2
    return [tuple(bits[i : i + 2]) for i in range(0, len(bits), 2)]


def sum_dp(x):
    x = xor_round(x, "dp", (1,))
    for bits in rounds_of(2, lax.axis_size("dp")):
        x = xor_round(x, "dp", bits)
    return x


def sum_head(x):
    for bits in rounds_of(1, lax.axis_size("head")):
        x = xor_round(x, "head", bits)
    return x


def sum_all(x):
    return sum_head(sum_dp(x))


def pack(vectors):
    return jnp.concatenate([v.reshape(-1) for v in vectors])


def unpack(joined, sizes):
    out, at = [], 0
    for size in sizes:
        out.append(joined[at : at + size])
        at += size
    return out


def crop_shift(x, by):
    n = lax.axis_size("dp")
    pairs = [(i, i + by) for i in range(n) if i // CROP_DP == (i + by) // CROP_DP and 0 <= i + by < n]
    return lax.ppermute(x, "dp", pairs)


def line_shift(x, by):
    n = lax.axis_size("head")
    return lax.ppermute(x, "head", [(i, i + by) for i in range(n) if 0 <= i + by < n])


def exchange(own):
    return [own] + [xor_move(own, "head", m) for m in range(1, lax.axis_size("head"))]


def in_order(blocks, z):
    stack = jnp.stack(blocks)
    return [lax.dynamic_index_in_dim(stack, z ^ j, 0, False) for j in range(len(blocks))]


def scatter_head(blocks, z):
    n = blocks.shape[0]
    total = lax.dynamic_index_in_dim(blocks, z, 0, False).astype(F32)
    for m in range(1, n):
        total = total + xor_move(lax.dynamic_index_in_dim(blocks, z ^ m, 0, False), "head", m).astype(F32)
    return total


def halve(t, axis, bits, bit, position):
    at = bits.index(bit)
    low = 1 << at
    shape = t.shape
    split = t.reshape(shape[:axis] + (shape[axis] // (2 * low), 2, low) + shape[axis + 1 :])
    mine = (position >> (bit.bit_length() - 1)) & 1
    keep = lax.dynamic_index_in_dim(split, mine, axis + 1, False)
    send = lax.dynamic_index_in_dim(split, 1 - mine, axis + 1, False)
    got = xor_move(send, "dp", bit)
    out = (keep.astype(F32) + got.astype(F32)).astype(BF)
    return out.reshape(shape[:axis] + (shape[axis] // 2,) + shape[axis + 1 :]), [x for x in bits if x != bit]


def scatter_dp(t, axis):
    n = lax.axis_size("dp")
    position = lax.axis_index("dp")
    bits = [1 << k for k in range(n.bit_length() - 1)]
    if not isinstance(t, tuple):
        t, bits = halve(t, axis, bits, 1, position)
        t = yield (t,)
        t = t[0]
        half = t.shape[-1] // 2
        parts = [(t[..., :half], bits), (t[..., half:], bits)]
    else:
        parts = [halve(part, axis, bits, 1, position) for part in t]
        arrays = yield tuple(part for part, _ in parts)
        parts = [(array, left) for array, (_, left) in zip(arrays, parts)]
    order = [1 << k for k in range(1, n.bit_length() - 1)]
    for k in range(0, len(order), 2):
        pair = order[k : k + 2]
        for step in range(len(pair)):
            parts = [
                halve(part, axis, left, pair[step if h == 0 else len(pair) - 1 - step], position)
                for h, (part, left) in enumerate(parts)
            ]
            arrays = yield tuple(part for part, _ in parts)
            parts = [(array, left) for array, (_, left) in zip(arrays, parts)]
    return


def tie(*trees):
    return lax.optimization_barrier(trees)


def held_until(value, *others):
    return lax.optimization_barrier((value, others))[0]


def last_step(steps, now):
    while True:
        try:
            now = steps.send(now)
        except StopIteration:
            return jnp.concatenate(now, axis=-1) if len(now) > 1 else now[0]


def shift_lanes(tile, by, lanes):
    if by == 0:
        return tile
    rolled = pltpu.roll(tile, (-by) % WIDTH, 1)
    keep = (lanes < WIDTH - by) if by > 0 else (lanes >= -by)
    return jnp.where(keep, rolled, 0.0)


def neck_columns_kernel(flip, ext_ref, out_ref):
    rows = ext_ref.shape[0]
    lanes = lax.broadcasted_iota(jnp.int32, (rows, WIDTH), 1)
    count = ext_ref.shape[1] // WIDTH
    for t in range(count):
        tile = ext_ref[:, t * WIDTH : (t + 1) * WIDTH].astype(F32)
        for j in range(3):
            moved = shift_lanes(tile, (j - 1) * 4, lanes).astype(BF)
            for i in range(3):
                at = t - 4 * i
                if 0 <= at < count - 8:
                    tap = 3 * i + j
                    out_ref[8 - tap if flip else tap, :, at * WIDTH : (at + 1) * WIDTH] = moved


def neck_columns(ext, flip):
    rows, width = ext.shape
    block = 64
    return pl.pallas_call(
        functools.partial(neck_columns_kernel, flip),
        grid=(rows // block,),
        in_specs=[pl.BlockSpec((block, width), lambda i: (i, 0))],
        out_specs=pl.BlockSpec((9, block, width - 1024), lambda i: (0, i, 0)),
        out_shape=jax.ShapeDtypeStruct((9, rows, width - 1024), BF),
        compiler_params=pltpu.CompilerParams(vmem_limit_bytes=40 << 20),
        cost_estimate=pl.CostEstimate(flops=0, bytes_accessed=2 * 12 * rows * width, transcendentals=0),
    )(ext)


TAP_STEP = 240


def frames_of(own_rows, n_dp):
    starts = [own_rows * s // 256 * 16 for s in range(n_dp)]
    ends = [-(-own_rows * (s + 1) // 16) for s in range(n_dp)]
    rows = max(end - start for start, end in zip(starts, ends))
    return starts, -(-rows // 16) * 16


def assemble_kernel(pieces, in_ref, out_ref):
    for start, stop, sources in pieces:
        total = None
        for s, at in sources:
            part = in_ref[s, at : at + stop - start, :]
            total = part if total is None else total + part
        out_ref[start:stop, :] = total
    end = pieces[-1][1]
    if end < out_ref.shape[0]:
        out_ref[end:, :] = jnp.zeros((out_ref.shape[0] - end, out_ref.shape[1]), BF)


def assemble(framed, own_rows, total_rows):
    n_dp, frame_rows, width = framed.shape
    starts, _ = frames_of(own_rows, n_dp)
    rows = -(-total_rows // TAP_STEP) * TAP_STEP
    pieces = []
    for g in range(0, -(-total_rows // 16) * 16, 16):
        sources = tuple(
            (s, g - starts[s])
            for s in range(n_dp)
            if own_rows * s < (g + 16) * 16 and own_rows * (s + 1) > g * 16
        )
        if pieces and len(sources) == 1 and len(pieces[-1][2]) == 1 and pieces[-1][2][0][0] == sources[0][0]:
            pieces[-1] = (pieces[-1][0], g + 16, pieces[-1][2])
        else:
            pieces.append((g, g + 16, sources))
    block = 256
    return pl.pallas_call(
        functools.partial(assemble_kernel, pieces),
        grid=(width // block,),
        in_specs=[pl.BlockSpec((n_dp, frame_rows, block), lambda i: (0, 0, i))],
        out_specs=pl.BlockSpec((rows, block), lambda i: (0, i)),
        out_shape=jax.ShapeDtypeStruct((rows, width), BF),
        compiler_params=pltpu.CompilerParams(vmem_limit_bytes=40 << 20),
        cost_estimate=pl.CostEstimate(flops=0, bytes_accessed=4 * rows * width, transcendentals=0),
    )(framed)


def whole(shape):
    return pl.BlockSpec(shape, lambda *_: (0,) * len(shape), pipeline_mode=pl.Buffered(1))


def lane_parts(value):
    total = value[:, :WIDTH]
    for t in range(1, value.shape[1] // WIDTH):
        total = total + value[:, t * WIDTH : (t + 1) * WIDTH]
    return total


def sigmoid_of(value):
    return 0.5 * jnp.tanh(0.5 * value) + 0.5


def shift_quad(value, by, lanes):
    return jnp.concatenate(
        [shift_lanes(value[:, t * WIDTH : (t + 1) * WIDTH], by, lanes) for t in range(4)], axis=1
    )


def neck_conv_kernel(z_ref, s0, s1, s2, s3, before, after, w_ref, mask_ref, out_ref, own_ref, one_ref, two_ref, ext):
    a = pl.program_id(0)

    @pl.when(a == 0)
    def _():
        z = z_ref[0]
        ext[0] = before[...]
        ext[5] = after[...]
        for m, slot in enumerate((s0, s1, s2, s3)):
            ext[1 + jnp.bitwise_xor(z, m)] = slot[...]
        one_ref[...] = jnp.zeros_like(one_ref)
        two_ref[...] = jnp.zeros_like(two_ref)

    own_ref[...] = ext[a + 1]
    rows = out_ref.shape[0]
    lanes = lax.broadcasted_iota(jnp.int32, (rows, WIDTH), 1)
    for j in (1, 0, 2):
        total = None
        for i in range(3):
            part = jnp.dot(w_ref[3 * i + j], ext[a + i], preferred_element_type=F32)
            total = part if total is None else total + part
        if j == 1:
            out_ref[...] = total
        else:
            out_ref[...] += shift_quad(total, (j - 1) * 4, lanes)
    value = out_ref[...]
    masked = value * mask_ref[0:1, :]
    one_ref[...] += lane_parts(masked)
    two_ref[...] += lane_parts(masked * value)


def neck_conv(z, slots, before, after, weights, mask8):
    rows = weights.shape[1]
    width = mask8.shape[1]
    block = lambda a, z_ref: (0, a)
    return pl.pallas_call(
        neck_conv_kernel,
        grid_spec=pltpu.PrefetchScalarGridSpec(
            num_scalar_prefetch=1,
            grid=(width // QUAD,),
            in_specs=[whole(before.shape)] * 6
            + [whole(weights.shape), pl.BlockSpec((8, QUAD), block)],
            out_specs=[
                pl.BlockSpec((rows, QUAD), block),
                pl.BlockSpec((rows, QUAD), block),
                pl.BlockSpec((rows, WIDTH), lambda a, z_ref: (0, 0)),
                pl.BlockSpec((rows, WIDTH), lambda a, z_ref: (0, 0)),
            ],
            scratch_shapes=[pltpu.VMEM((6, rows, QUAD), BF)],
        ),
        out_shape=[
            jax.ShapeDtypeStruct((rows, width), F32),
            jax.ShapeDtypeStruct((rows, width), BF),
            jax.ShapeDtypeStruct((rows, WIDTH), F32),
            jax.ShapeDtypeStruct((rows, WIDTH), F32),
        ],
        compiler_params=pltpu.CompilerParams(vmem_limit_bytes=48 << 20),
        cost_estimate=pl.CostEstimate(flops=18 * rows * rows * width, bytes_accessed=16 << 20, transcendentals=0),
    )(z.reshape(1), *slots, before, after, weights, mask8)


CHUNK = 256


def fetch_quad(away, sources, buffer, sem):
    for k, source in zip((0, 1, 2, 3, -1, -2, -3), sources):

        @pl.when(away == k)
        def _():
            pltpu.make_async_copy(source, buffer, sem).start()


def feature_group_kernel(z_ref, mask_ref, x0, x1, x2, x3, x4, x5, x6, out_ref, xbuf, sem):
    sources = (x0, x1, x2, x3, x4, x5, x6)
    fetch_quad(pl.program_id(0) - z_ref[0], sources, xbuf, sem)
    pltpu.make_async_copy(x0, xbuf, sem).wait()
    mask = mask_ref[0:1, :]

    def place(i, carry):
        at = pl.ds(pl.multiple_of(i * CHUNK, CHUNK), CHUNK)
        out_ref[at, :] = (xbuf[at, :].astype(F32) * mask).astype(BF)
        return carry

    lax.fori_loop(0, out_ref.shape[0] // CHUNK, place, 0)


def feature_group(z, mask8, sources):
    rows = sources[0].shape[0]
    width = mask8.shape[1]
    block = lambda a, z_ref: (0, a)
    return pl.pallas_call(
        feature_group_kernel,
        grid_spec=pltpu.PrefetchScalarGridSpec(
            num_scalar_prefetch=1,
            grid=(width // QUAD,),
            in_specs=[pl.BlockSpec((8, QUAD), block)] + [pl.BlockSpec(memory_space=pl.ANY)] * 7,
            out_specs=pl.BlockSpec((rows, QUAD), block),
            scratch_shapes=[pltpu.VMEM((rows, QUAD), BF), pltpu.SemaphoreType.DMA],
        ),
        out_shape=jax.ShapeDtypeStruct((rows, width), BF),
        compiler_params=pltpu.CompilerParams(vmem_limit_bytes=32 << 20),
        cost_estimate=pl.CostEstimate(flops=0, bytes_accessed=4 * rows * width, transcendentals=0),
    )(z.reshape(1), mask8, *sources)


def aspp_forward_kernel(
    z_ref, pre_ref, coef_ref, mask_ref, w_ref, x0, x1, x2, x3, x4, x5, x6,
    y_ref, slope_ref, core_ref, side_ref, pool_ref, xbuf, held, products, sem
):
    a = pl.program_id(0)
    quads = pl.num_programs(0) - 1
    sources = (x0, x1, x2, x3, x4, x5, x6)
    slot = a % 2
    channels = y_ref.shape[0]
    steps = w_ref.shape[0] // TAP_STEP
    chunk = channels // steps

    @pl.when(a == 0)
    def _():
        fetch_quad(-z_ref[0], sources, xbuf.at[0], sem.at[0])

    @pl.when(a < quads)
    def _():
        pltpu.make_async_copy(x0, xbuf.at[slot], sem.at[slot]).wait()

    @pl.when(a + 1 < quads)
    def _():
        fetch_quad(a + 1 - z_ref[0], sources, xbuf.at[1 - slot], sem.at[1 - slot])

    mask = mask_ref[0:1, :]

    def activate(i):
        at = pl.ds(pl.multiple_of(i * chunk, chunk), chunk)
        x = xbuf[slot, at, :].astype(F32) * mask
        value = pre_ref[at, :].astype(F32) * coef_ref[at, 0:1] + coef_ref[at, 1:2] + x
        sig = sigmoid_of(value)
        y_ref[at, :] = (value * sig * mask).astype(BF)
        slope_ref[at, :] = (sig * (1.0 + value * (1.0 - sig)) * mask).astype(BF)

    def multiply(i):
        at = pl.ds(pl.multiple_of(i * TAP_STEP, 16), TAP_STEP)
        products[at, :] = jnp.dot(w_ref[at, :], held[...], preferred_element_type=F32)

    @pl.when(a == 0)
    def _():
        lax.fori_loop(0, steps, lambda i, c: (activate(i), c)[1], 0)

    @pl.when((a > 0) & (a < quads))
    def _():
        def both(i, carry):
            multiply(i)
            activate(i)
            return carry

        lax.fori_loop(0, steps, both, 0)

    @pl.when(a == quads)
    def _():
        lax.fori_loop(0, steps, lambda i, c: (multiply(i), c)[1], 0)

    held[...] = y_ref[...]

    @pl.when(a > 0)
    def _():
        lanes = lax.broadcasted_iota(jnp.int32, (64, WIDTH), 1)
        core_ref[0] = products[0:64, :]
        pool_ref[0] = lane_parts(products[64 * 28 : 64 * 29, :])
        for t in range(4):
            part = slice(t * WIDTH, (t + 1) * WIDTH)
            for br, rate in enumerate(RATES):
                for i in range(3):
                    total = None
                    for j in range(3):
                        row = 64 * (1 + 9 * br + 3 * i + j)
                        moved = shift_lanes(products[row : row + 64, part], (j - 1) * rate, lanes)
                        total = moved if total is None else total + moved
                    if i == 1:
                        core_ref[1 + br, :, part] = total
                    else:
                        side_ref[2 * br + i // 2, 0, :, part] = total.astype(BF)


def aspp_forward(z, pre, coef, mask8, weights, sources):
    rows, width = pre.shape
    quads = width // QUAD
    now = lambda a: jnp.minimum(a, quads - 1)
    done = lambda a: jnp.maximum(a - 1, 0)
    wide = pl.BlockSpec((rows, QUAD), lambda a, z_ref: (0, now(a)))
    return pl.pallas_call(
        aspp_forward_kernel,
        grid_spec=pltpu.PrefetchScalarGridSpec(
            num_scalar_prefetch=1,
            grid=(quads + 1,),
            in_specs=[
                wide,
                whole(coef.shape),
                pl.BlockSpec((8, QUAD), lambda a, z_ref: (0, now(a))),
                whole(weights.shape),
            ]
            + [pl.BlockSpec(memory_space=pl.ANY)] * 7,
            out_specs=[
                wide,
                wide,
                pl.BlockSpec((4, 64, QUAD), lambda a, z_ref: (0, 0, done(a))),
                pl.BlockSpec((6, 1, 64, QUAD), lambda a, z_ref: (0, done(a), 0, 0)),
                pl.BlockSpec((1, 64, WIDTH), lambda a, z_ref: (done(a), 0, 0)),
            ],
            scratch_shapes=[
                pltpu.VMEM((2, rows, QUAD), BF),
                pltpu.VMEM((rows, QUAD), BF),
                pltpu.VMEM((weights.shape[0], QUAD), F32),
                pltpu.SemaphoreType.DMA((2,)),
            ],
        ),
        out_shape=[
            jax.ShapeDtypeStruct((rows, width), BF),
            jax.ShapeDtypeStruct((rows, width), BF),
            jax.ShapeDtypeStruct((4, 64, width), F32),
            jax.ShapeDtypeStruct((6, quads, 64, QUAD), BF),
            jax.ShapeDtypeStruct((quads, 64, WIDTH), F32),
        ],
        compiler_params=pltpu.CompilerParams(vmem_limit_bytes=58 << 20),
        cost_estimate=pl.CostEstimate(
            flops=2 * 29 * 64 * rows * width, bytes_accessed=48 << 20, transcendentals=rows * width
        ),
    )(z.reshape(1), pre, coef, mask8, weights, *sources)


def aspp_backward_kernel(
    one_ref, rows_ref, pool_in, mask_ref, w_ref, slope_ref, pre_ref,
    out_ref, act_ref, sum_ref, dot_ref
):
    @pl.when(pl.program_id(0) == 0)
    def _():
        sum_ref[...] = jnp.zeros_like(sum_ref)
        dot_ref[...] = jnp.zeros_like(dot_ref)

    lanes = lax.broadcasted_iota(jnp.int32, (64, WIDTH), 1)
    out_ref[0:64, :] = one_ref[...].astype(BF)
    out_ref[64 * 29 :, :] = jnp.zeros((out_ref.shape[0] - 64 * 29, QUAD), BF)
    for t in range(4):
        part = slice(t * WIDTH, (t + 1) * WIDTH)
        out_ref[64 * 28 : 64 * 29, part] = (pool_in[...] * mask_ref[0:1, part]).astype(BF)
        for br, rate in enumerate(RATES):
            for i in range(3):
                tile = rows_ref[br, i, 0, :, part].astype(F32)
                for j in range(3):
                    at = 64 * (1 + 9 * br + 3 * i + j)
                    out_ref[at : at + 64, part] = shift_lanes(tile, (1 - j) * rate, lanes).astype(BF)

    def multiply(i, carry):
        at = pl.ds(pl.multiple_of(i * CHUNK, CHUNK), CHUNK)
        grad = jnp.dot(w_ref[at, :], out_ref[...], preferred_element_type=F32)
        act = grad * slope_ref[at, :].astype(F32)
        act_ref[at, :] = act.astype(BF)
        sum_ref[at, :] += lane_parts(act)
        dot_ref[at, :] += lane_parts(act * pre_ref[at, :].astype(F32))
        return carry

    lax.fori_loop(0, act_ref.shape[0] // CHUNK, multiply, 0)


def aspp_backward(one, rows, pool, mask8, weights_t, slope, pre):
    channels, width = pre.shape
    quads = width // QUAD
    count = weights_t.shape[1]
    block = lambda a: (0, a)
    wide = pl.BlockSpec((channels, QUAD), block)
    return pl.pallas_call(
        aspp_backward_kernel,
        grid=(quads,),
        in_specs=[
            pl.BlockSpec((64, QUAD), block),
            pl.BlockSpec((3, 3, 1, 64, QUAD), lambda a: (0, 0, a, 0, 0)),
            whole((64, WIDTH)),
            pl.BlockSpec((8, QUAD), block),
            whole(weights_t.shape),
            wide,
            wide,
        ],
        out_specs=[
            pl.BlockSpec((count, QUAD), block),
            wide,
            pl.BlockSpec((channels, WIDTH), lambda a: (0, 0)),
            pl.BlockSpec((channels, WIDTH), lambda a: (0, 0)),
        ],
        out_shape=[
            jax.ShapeDtypeStruct((count, width), BF),
            jax.ShapeDtypeStruct((channels, width), BF),
            jax.ShapeDtypeStruct((channels, WIDTH), F32),
            jax.ShapeDtypeStruct((channels, WIDTH), F32),
        ],
        compiler_params=pltpu.CompilerParams(vmem_limit_bytes=58 << 20),
        cost_estimate=pl.CostEstimate(
            flops=2 * count * channels * width, bytes_accessed=48 << 20, transcendentals=0
        ),
    )(one, rows, pool, mask8, weights_t, slope, pre)


def taps_grad_kernel(starts, spread_ref, y_ref, project_ref, out_ref, total):
    total[...] = dot(spread_ref[...], y_ref[...], (1,), (1,)).astype(BF)
    low = 29 * 64
    total[low : low + project_ref.shape[0], :] = project_ref[...]
    for s, start in enumerate(starts):
        out_ref[s] = total[start : start + out_ref.shape[1], :]


def taps_grad(starts, frame_rows, spread, y, project, part, parts):
    rows, pixels = spread.shape
    width = y.shape[0] // parts
    block = 256
    first = part * width // block
    return pl.pallas_call(
        functools.partial(taps_grad_kernel, starts),
        grid=(width // block,),
        in_specs=[
            whole((rows, pixels)),
            pl.BlockSpec((block, pixels), lambda i: (first + i, 0)),
            pl.BlockSpec((project.shape[0], block), lambda i: (0, first + i)),
        ],
        out_specs=pl.BlockSpec((len(starts), frame_rows, block), lambda i: (0, 0, i)),
        out_shape=jax.ShapeDtypeStruct((len(starts), frame_rows, width), BF),
        scratch_shapes=[pltpu.VMEM((rows, block), BF)],
        compiler_params=pltpu.CompilerParams(vmem_limit_bytes=48 << 20),
        cost_estimate=pl.CostEstimate(
            flops=2 * rows * pixels * width, bytes_accessed=20 << 20, transcendentals=0
        ),
    )(spread, y, project)


def side_rows(side):
    result = []
    at = lax.axis_index("dp") % CROP_DP
    n = lax.axis_size("dp")
    from_one = crop_shift(jnp.concatenate([side[0, 1:4], side[2, 0:2]]), 1)
    to_one = crop_shift(jnp.concatenate([side[1, 0:3], side[3, 2:4]]), -1)
    up = jnp.concatenate([side[2, 2:4], side[4, 0:3]])
    down = jnp.concatenate([side[3, 0:2], side[5, 1:4]])
    two = xor_move(jnp.where(at < 2, up, down), "dp", 2)
    from_two = jnp.where(at < 2, jnp.zeros_like(two), two)
    to_two = jnp.where(at < 2, two, jnp.zeros_like(two))
    ends = [(i, i + 3 - 2 * (i % CROP_DP)) for i in range(n) if i % CROP_DP in (0, CROP_DP - 1)]
    three = lax.ppermute(jnp.where(at == 0, side[4, 3:4], side[5, 0:1]), "dp", ends)
    from_three = jnp.where(at == 0, jnp.zeros_like(three), three)
    to_three = jnp.where(at == 0, three, jnp.zeros_like(three))
    result.append(jnp.concatenate([from_one[0:3], side[0, 0:1]]))
    result.append(jnp.concatenate([side[1, 3:4], to_one[0:3]]))
    result.append(jnp.concatenate([from_two[0:2], from_one[3:5]]))
    result.append(jnp.concatenate([to_one[3:5], to_two[0:2]]))
    result.append(jnp.concatenate([from_three, from_two[2:5]]))
    result.append(jnp.concatenate([to_two[2:5], to_three]))
    return result


def adam_step(weight, first_m, second_m, gradient, factor, rate, decay):
    clipped = gradient * factor
    new_first = BETA_ONE * first_m + (1.0 - BETA_ONE) * clipped
    new_second = BETA_TWO * second_m + (1.0 - BETA_TWO) * clipped * clipped
    corrected = (
        new_first
        / (1.0 - BETA_ONE**STEP)
        / (jnp.sqrt(new_second / (1.0 - BETA_TWO**STEP)) + ADAM_EPSILON)
    )
    return (weight - rate * (corrected + decay * weight), new_first, new_second)


def flat_rows(quads):
    return jnp.concatenate([quads[a] for a in range(quads.shape[0])], axis=1)


def quad_blocks(flat):
    return [flat[..., a * QUAD : (a + 1) * QUAD] for a in range(flat.shape[-1] // QUAD)]


def owner_tables(n_dp, share_rows, wide, heads):
    quarter = BOT // heads
    places = []
    for p in range(n_dp):
        rows = []
        for k in range(wide):
            rows += [(share_rows * p + r) * wide + k for r in range(share_rows)]
        for tap in range(9):
            rows += [quarter * (wide + tap) + share_rows * p + r for r in range(share_rows)]
        rows += [quarter * (wide + 9) + share_rows * wide * p + r for r in range(share_rows * wide)]
        places.append(np.array(rows))
    own = len(places[0])
    lists = [[np.nonzero(place // own == s)[0] for s in range(n_dp)] for place in places]
    count = -(-max(len(x) for row in lists for x in row) // 16) * 16
    send = np.full((n_dp, n_dp, count), -1, np.int32)
    take = np.zeros((n_dp, own), np.int32)
    for p in range(n_dp):
        for s in range(n_dp):
            rows = lists[p][s]
            send[p, s, : len(rows)] = rows
            take[s, places[p][rows] - own * s] = p * count + np.arange(len(rows))
    return send, take


def shards(
    features,
    crop_rows,
    crop_cols,
    labels,
    offset_targets,
    depth_targets,
    lidar_mask,
    trunk_aspp,
    aspp_first,
    aspp_second,
    trunk_neck,
    neck_first,
    neck_second,
    norm_params,
    norm_first,
    norm_second,
    decoders,
    decoder_first,
    decoder_second,
    log_vars,
    log_first,
    log_second,
):
    heads = lax.axis_size("head")
    z = lax.axis_index("head")
    group = lax.axis_index("dp")
    crop = group // CROP_DP
    pixels = heads * QUAD
    share = 1.0 / heads
    quarter = ASP // heads

    n_dp = lax.axis_size("dp")
    neck_low = trunk_neck.reshape(1, -1, BOT).astype(BF)
    neck_low = lax.all_gather(neck_low, "head", axis=0, tiled=True)
    neck_low = lax.all_gather(neck_low, "dp", axis=1, tiled=True)
    x_left, x_right = [features, line_shift(features, 1)], [features, line_shift(features, -1)]
    neck_low, x_left[1], x_right[1] = tie(neck_low, x_left[1], x_right[1])
    first_end = FEAT // heads
    second_end = first_end + 9 * BOT // heads
    reduce_w = neck_low[:, :first_end].reshape(BOT, FEAT)
    middle = neck_low[:, first_end:second_end].reshape(heads, 9, BOT // heads, BOT)
    middle = jnp.moveaxis(middle, 0, 1).reshape(9, BOT, BOT)
    expand_w = neck_low[:, second_end:].reshape(FEAT, BOT)


    flat_total = trunk_aspp.shape[1] * n_dp // 16
    own_rows = trunk_aspp.shape[1]
    frames, frame_rows = frames_of(own_rows, n_dp)
    inset = (group * own_rows) % 256
    framed = lax.dynamic_update_slice_in_dim(
        jnp.zeros((frame_rows * 16, 128), F32), trunk_aspp[0], inset, 0
    )
    framed = framed.reshape(frame_rows, FEAT).astype(BF)
    gathered = lax.all_gather(framed, "dp", axis=0)

    place = jnp.arange(pixels, dtype=jnp.int32)
    row_place = group % CROP_DP * (pixels // WIDTH) + place // WIDTH
    col_place = place % WIDTH
    mask = ((row_place < crop_rows[crop]) & (col_place < crop_cols[crop])).astype(F32)[None, :]
    mask_own = lax.dynamic_slice_in_dim(mask, z * QUAD, QUAD, 1)
    total_n = jnp.sum((crop_rows * crop_cols).astype(F32))
    crop_n = (crop_rows[crop] * crop_cols[crop]).astype(F32)

    def own_pixels(a):
        return lax.dynamic_slice_in_dim(a, z * QUAD, QUAD, a.ndim - 1)

    labels_own = own_pixels(labels)
    offset_own = own_pixels(offset_targets)
    depth_own = own_pixels(depth_targets)
    lidar_own = own_pixels(lidar_mask).astype(F32) * mask_own[0]

    gains, shifts = (norm_params[0], norm_params[1])
    bounds = [0, BOT, 2 * BOT, 2 * BOT + FEAT, 2 * BOT + FEAT + 4 * ASP, 2 * BOT + FEAT + 5 * ASP]

    def slot(vector, index):
        return vector[bounds[index] : bounds[index + 1]]

    def own_aspp(vector):
        return lax.dynamic_slice_in_dim(vector.reshape(4, heads, quarter), z, 1, 1).reshape(-1)

    gain_one, gain_two, gain_three, gain_proj = [slot(gains, i) for i in (0, 1, 2, 4)]
    shift_one, shift_two, shift_three, shift_proj = [slot(shifts, i) for i in (0, 1, 2, 4)]
    gain_aspp, shift_aspp = own_aspp(slot(gains, 3)), own_aspp(slot(shifts, 3))

    def moments(pre, m):
        masked = pre * m
        return jnp.sum(masked, axis=-1), jnp.sum(masked * pre, axis=-1)

    def coefficients(total, square):
        mean = total / total_n
        inv = lax.rsqrt(square / total_n - mean * mean + EPSILON)
        return mean, inv

    def normed(pre, mean, inv):
        return (pre - mean[:, None]) * inv[:, None]

    def scaled(hat, gain, shift):
        return gain[:, None] * hat + shift[:, None]

    x_own = features * mask_own.astype(BF)
    pre_one = jnp.dot(reduce_w, x_own, preferred_element_type=F32)
    sums = sum_all(pack((*moments(pre_one, mask_own), jnp.broadcast_to(jnp.sum(lidar_own), (128,)))))
    total, square, lidar = unpack(sums, (BOT, BOT, 128))
    lidar_n = lidar[0]
    mean_one, inv_one = coefficients(total, square)
    low_one = (jax.nn.silu(scaled(normed(pre_one, mean_one, inv_one), gain_one, shift_one)) * mask_own).astype(BF)
    slots = exchange(low_one)
    aspp_rows = assemble(held_until(gathered, low_one), own_rows, flat_total)
    project_q = aspp_rows[29 * quarter : flat_total].reshape(quarter, 5, heads, quarter)
    project_q = jnp.moveaxis(project_q, 2, 0).reshape(heads, quarter, 5 * quarter)
    received = [lax.dynamic_index_in_dim(project_q, z, 0, False)]
    for m in range(1, heads):
        received.append(xor_move(lax.dynamic_index_in_dim(project_q, z ^ m, 0, False), "head", m))
    project_own = jnp.concatenate(in_order(received, z), axis=0)
    tap_wt = aspp_rows.T
    slots, tap_wt, project_own = tie(slots, tap_wt, project_own)
    x_left[1], x_right[1] = held_until((x_left[1], x_right[1]), slots)
    for _ in range(1, heads - 1):
        x_left.append(line_shift(x_left[-1], 1))
        x_right.append(line_shift(x_right[-1], -1))

    def block_of(j):
        block = slots[0]
        for m in range(1, heads):
            block = jnp.where((z ^ m) == j, slots[m], block)
        return block

    before = crop_shift(block_of(heads - 1), 1)
    after = crop_shift(block_of(0), -1)
    mask8 = jnp.broadcast_to(mask, (8, pixels))
    pre_two, h_one, one_part, two_part = neck_conv(z, slots, before, after, middle, mask8)
    sums = sum_dp(pack((jnp.sum(one_part, axis=1), jnp.sum(two_part, axis=1))))
    mean_two, inv_two = coefficients(*unpack(sums, (BOT, BOT)))
    hat_two = normed(pre_two, mean_two, inv_two)
    in_two = scaled(hat_two, gain_two, shift_two)
    h_two = (jax.nn.silu(in_two) * mask).astype(BF)
    pre_three = jnp.dot(expand_w, h_two, preferred_element_type=F32)
    mean_three, inv_three = coefficients(*unpack(sum_dp(pack(moments(pre_three, mask))), (FEAT, FEAT)))
    pre_three = pre_three.astype(BF)
    scale_three = gain_three * inv_three
    coef = jnp.stack([scale_three, shift_three - scale_three * mean_three], axis=1)
    sources = [features, *x_right[1:], *x_left[1:]]
    y, slope_three, middle_rows, side, pool_part = aspp_forward(
        z, pre_three, coef, mask8, aspp_rows, sources
    )

    moved = side_rows(side)
    branches = [middle_rows[0]]
    for br in range(3):
        branches.append(
            middle_rows[1 + br]
            + flat_rows(moved[2 * br]).astype(F32)
            + flat_rows(moved[2 * br + 1]).astype(F32)
        )
    pre_aspp = jnp.concatenate(branches, axis=0)
    pool_local = jnp.sum(pool_part, axis=(0, 2))
    local = pack((*moments(pre_aspp, mask), pool_local, jnp.zeros((64,), F32)))
    local = sum_crop(local)
    pool_sum = local[2 * ASP : 2 * ASP + quarter]
    for bits in rounds_of(4, lax.axis_size("dp")):
        local = xor_round(local, "dp", bits)
    mean_aspp, inv_aspp = coefficients(local[:ASP], local[ASP : 2 * ASP])
    hat_aspp = normed(pre_aspp, mean_aspp, inv_aspp)
    in_aspp = scaled(hat_aspp, gain_aspp, shift_aspp)
    act_aspp = jax.nn.silu(in_aspp) * mask
    pool_pre = pool_sum / crop_n
    joined = jnp.concatenate([act_aspp, jax.nn.silu(pool_pre)[:, None] * mask], axis=0).astype(BF)

    part_proj = jnp.dot(project_own, joined, preferred_element_type=F32)
    pre_proj = scatter_head(jnp.stack(quad_blocks(part_proj.astype(BF))), z)
    x_group = feature_group(z, held_until(mask8, part_proj), sources)
    pre_proj, x_group = tie(pre_proj, x_group)
    mean_proj, inv_proj = coefficients(*unpack(sum_all(pack(moments(pre_proj, mask_own))), (ASP, ASP)))
    hat_proj = normed(pre_proj, mean_proj, inv_proj)
    in_proj = scaled(hat_proj, gain_proj, shift_proj)
    feat = (jax.nn.silu(in_proj) * mask_own).astype(BF)

    low_dec = decoders.astype(BF)
    hidden_w, out_w = low_dec[: 3 * ASP], low_dec[3 * ASP :]
    dec_pre = jnp.dot(hidden_w, feat, preferred_element_type=F32)
    hidden = jax.nn.silu(dec_pre).astype(BF)
    row_sets = ((0, CLS), (CLS, CLS + 2), (CLS + 2, CLS + 3))
    logits = [
        jnp.dot(out_w, hidden[t * ASP : (t + 1) * ASP], preferred_element_type=F32)[lo:hi]
        for t, (lo, hi) in enumerate(row_sets)
    ]
    sem_logits, off_logits, dep_logits = logits
    valid_own = mask_own[0]
    label_hot = (jnp.arange(CLS, dtype=jnp.int32)[:, None] == labels_own[None, :]).astype(F32)
    log_total = jax.nn.logsumexp(sem_logits, axis=0)
    sem_sum = jnp.sum((log_total - jnp.sum(label_hot * sem_logits, axis=0)) * valid_own)
    off_diff = off_logits - offset_own
    off_root = jnp.sqrt(off_diff * off_diff + 1.0)
    off_sum = jnp.sum((off_root - 1.0) * valid_own)
    dep_logit = dep_logits[0]
    dep_diff = jax.nn.softplus(dep_logit) - depth_own
    dep_root = jnp.sqrt(dep_diff * dep_diff + 1.0)
    dep_sum = jnp.sum((dep_root - 1.0) * lidar_own)
    divisors = jnp.stack([total_n, total_n, lidar_n])
    weights = jnp.exp(-log_vars) / divisors
    grad_sem = (jax.nn.softmax(sem_logits, axis=0) - label_hot) * valid_own * weights[0]
    grad_off = off_diff / off_root * valid_own * weights[1]
    grad_dep = (dep_diff / dep_root * jax.nn.sigmoid(dep_logit) * lidar_own * weights[2])[None, :]
    grad_logits = [g.astype(BF) for g in (grad_sem, grad_off, grad_dep)]
    grad_out_w = []
    grad_hidden = []
    for t, (lo, hi) in enumerate(row_sets):
        grad_out_w.append(dot(grad_logits[t], hidden[t * ASP : (t + 1) * ASP], (1,), (1,)))
        grad_hidden.append(dot(out_w[lo:hi], grad_logits[t], (0,), (0,)))
    grad_dec_pre = (jnp.concatenate(grad_hidden, axis=0) * silu_slope(dec_pre)).astype(BF)
    grad_hidden_w = dot(grad_dec_pre, feat, (1,), (1,))
    grad_feat = dot(hidden_w, grad_dec_pre, (0,), (0,))
    dec_grad = lax.psum(jnp.concatenate([grad_hidden_w, *grad_out_w], axis=0), ("dp", "head"))

    grad_act = grad_feat * mask_own * silu_slope(in_proj)
    sums = sum_all(
        pack(
            (
                jnp.sum(grad_act, axis=-1),
                jnp.sum(grad_act * hat_proj, axis=-1),
                jnp.stack([sem_sum, off_sum, dep_sum]),
                jnp.zeros((125,), F32),
            )
        )
    )
    back_shift_proj, back_gain_proj, loss_sums = unpack(sums, (ASP, ASP, 3))
    losses = loss_sums / divisors
    total_loss = jnp.sum(jnp.exp(-log_vars) * losses + log_vars)
    grad_logvar = 1.0 - jnp.exp(-log_vars) * losses
    grad_proj = (
        mask_own
        * (gain_proj * inv_proj)[:, None]
        * (grad_act - (back_shift_proj / total_n)[:, None] - hat_proj * (back_gain_proj / total_n)[:, None])
    ).astype(BF)
    grad_proj = jnp.concatenate(in_order(exchange(grad_proj), z), axis=1)
    grad_project = dot(grad_proj, joined, (1,), (1,)).astype(BF).reshape(heads, quarter, 5 * quarter)
    grad_joined = dot(project_own, grad_proj, (0,), (0,))

    grad_act = grad_joined[:ASP] * mask * silu_slope(in_aspp)
    local = pack(
        (
            jnp.sum(grad_act, axis=-1),
            jnp.sum(grad_act * hat_aspp, axis=-1),
            jnp.sum(grad_joined[ASP:] * mask, axis=-1),
            jnp.zeros((64,), F32),
        )
    )
    local = sum_crop(local)
    pool_row = local[2 * ASP : 2 * ASP + quarter]
    for bits in rounds_of(4, lax.axis_size("dp")):
        local = xor_round(local, "dp", bits)
    back_shift_aspp, back_gain_aspp = local[:ASP], local[ASP : 2 * ASP]
    grad_aspp = (
        mask
        * (gain_aspp * inv_aspp)[:, None]
        * (grad_act - (back_shift_aspp / total_n)[:, None] - hat_aspp * (back_gain_aspp / total_n)[:, None])
    ).astype(BF)
    grad_pool = (pool_row * silu_slope(pool_pre)).astype(BF).astype(F32) / crop_n
    parts = [jnp.stack(quad_blocks(grad_aspp[quarter * (br + 1) : quarter * (br + 2)])) for br in range(3)]
    moved = side_rows(jnp.stack([part for part in parts for _ in range(2)]))
    rows = jnp.stack(
        [jnp.stack([moved[2 * br + 1], parts[br], moved[2 * br]]) for br in range(3)]
    )
    spread, act_three, sum_part, dot_part = aspp_backward(
        grad_aspp[:quarter],
        rows,
        jnp.broadcast_to(grad_pool[:, None], (quarter, WIDTH)),
        mask8,
        tap_wt,
        slope_three,
        pre_three,
    )

    spread_norms = jnp.stack([back_gain_aspp, back_shift_aspp]).reshape(2, 4, 1, quarter)
    own_place = (jnp.arange(heads) == z)[None, None, :, None] & (group == 0)
    spread_norms = jnp.where(own_place, spread_norms, 0.0)
    sum_three = jnp.sum(sum_part, axis=1)
    sums = xor_round(
        pack((sum_three, (jnp.sum(dot_part, axis=1) - mean_three * sum_three) * inv_three, spread_norms)),
        "dp",
        (1,),
    )

    swapped = [
        xor_move(lax.dynamic_index_in_dim(grad_project, z ^ m, 0, False), "head", m)
        if m
        else lax.dynamic_index_in_dim(grad_project, z, 0, False)
        for m in range(heads)
    ]
    own_project = jnp.stack(in_order(swapped, z)).reshape(heads, quarter, 5, quarter)
    own_project = jnp.moveaxis(own_project, 0, 2).reshape(-1, FEAT)
    own_project = jnp.concatenate([own_project, jnp.zeros((-flat_total % 16, FEAT), BF)], axis=0)
    sums, spread, own_project = tie(sums, spread, own_project)
    first_half = taps_grad(frames, frame_rows, spread, y, own_project, 0, 2)
    for bits in rounds_of(2, n_dp):
        sums = xor_round(sums, "dp", bits)
    sums, first_half, spread = tie(sums, first_half, spread)
    second_half = taps_grad(frames, frame_rows, spread, y, own_project, 1, 2)
    sums = sum_head(sums)
    sums, first_half, second_half, dec_grad = tie(sums, first_half, second_half, dec_grad)
    aspp_steps = scatter_dp((first_half, second_half), 0)
    aspp_now = next(aspp_steps)
    back_shift_three, back_gain_three, both = unpack(sums, (FEAT, FEAT, 8 * ASP))
    both = both.reshape(2, 4 * ASP)

    def norm_back(grad_act, hat, gain, inv, back_shift, back_gain):
        scale = share / total_n
        return (
            mask
            * (gain * inv)[:, None]
            * (grad_act - (back_shift * scale)[:, None] - hat * (back_gain * scale)[:, None])
        ).astype(BF)

    hat_three = normed(pre_three.astype(F32), mean_three, inv_three)
    grad_three = norm_back(
        act_three.astype(F32), hat_three, gain_three, inv_three, back_shift_three, back_gain_three
    )
    grad_h_two = dot(expand_w, grad_three, (0,), (0,))
    grad_act = grad_h_two * mask * silu_slope(in_two)
    sums = pack((jnp.sum(grad_act, axis=-1), jnp.sum(grad_act * hat_two, axis=-1)))
    sums = xor_round(sums, "dp", (1,))
    sums, grad_three = tie(sums, grad_three)
    grad_expand = dot(grad_three, h_two, (1,), (1,)).astype(BF).reshape(heads, n_dp, -1, BOT)
    for bits in rounds_of(2, n_dp):
        sums = xor_round(sums, "dp", bits)
    sums = sum_head(sums)
    sums, grad_expand, aspp_now = tie(sums, grad_expand, aspp_now)
    back_shift_two, back_gain_two = unpack(sums, (BOT, BOT))
    grad_two = norm_back(grad_act, hat_two, gain_two, inv_two, back_shift_two, back_gain_two)
    before = crop_shift(grad_two[:, -QUAD:], 1)
    after = crop_shift(grad_two[:, :QUAD], -1)
    before, after, aspp_now, grad_expand = tie(before, after, aspp_now, grad_expand)
    aspp_now = aspp_steps.send(aspp_now)
    expand_steps = scatter_dp(grad_expand, 1)
    expand_now = next(expand_steps)
    columns = neck_columns(jnp.concatenate([before, grad_two, after], axis=1), True)
    grad_h_one = lax.dot_general(middle, columns, (((0, 1), (0, 1)), ((), ())), preferred_element_type=F32)
    group_one = jnp.dot(reduce_w, x_group, preferred_element_type=F32)
    hat_one = normed(group_one, mean_one, inv_one)
    grad_act = grad_h_one * mask * silu_slope(scaled(hat_one, gain_one, shift_one))
    sums = pack((jnp.sum(grad_act, axis=-1), jnp.sum(grad_act * hat_one, axis=-1)))
    sums, aspp_now, expand_now = tie(sums, aspp_now, expand_now)
    sums = xor_round(sums, "dp", (1,))
    sums, columns = tie(sums, columns)
    grad_middle = dot(columns, h_one, (2,), (1,)).astype(BF).reshape(9, heads, n_dp, -1, BOT)
    for bits in rounds_of(2, n_dp):
        sums = xor_round(sums, "dp", bits)
    sums = sum_head(sums)
    sums, grad_middle, aspp_now, expand_now = tie(sums, grad_middle, aspp_now, expand_now)
    middle_steps = scatter_dp(grad_middle, 2)
    middle_now = next(middle_steps)
    aspp_block = last_step(aspp_steps, aspp_now)
    expand_block = last_step(expand_steps, expand_now)
    back_shift_one, back_gain_one = unpack(sums, (BOT, BOT))
    grad_one = norm_back(grad_act, hat_one, gain_one, inv_one, back_shift_one, back_gain_one)
    grad_reduce = dot(grad_one, x_group, (1,), (1,)).astype(BF)
    wide = FEAT // BOT
    grad_reduce = jnp.stack([grad_reduce[:, k * BOT : (k + 1) * BOT] for k in range(wide)])
    reduce_steps = scatter_dp(grad_reduce.reshape(wide, heads, n_dp, -1, BOT), 2)
    reduce_now, middle_now, aspp_block, expand_block = tie(
        next(reduce_steps), middle_now, aspp_block, expand_block
    )
    expand_own = scatter_head(expand_block.reshape(heads, -1, BOT), z)
    both_now = jnp.concatenate([reduce_now[0], middle_now[0]], axis=0)
    both_block = last_step(reduce_steps, reduce_steps.send((both_now,)))

    shard_aspp = lax.dynamic_slice_in_dim(
        aspp_block.astype(F32).reshape(frame_rows * 16, 128), inset, own_rows, 0
    )[None]
    share_rows = BOT // heads // n_dp
    both_block = both_block.reshape(wide + 9, heads, share_rows, BOT)
    both_own = scatter_head(jnp.moveaxis(both_block, 1, 0), z)
    pieces = jnp.concatenate([both_own, expand_own.reshape(wide, share_rows, BOT)], axis=0).astype(BF)
    pieces = pieces.reshape(-1, BOT)
    send_rows, take_rows = owner_tables(n_dp, share_rows, wide, heads)
    count = send_rows.shape[2]
    chosen = lax.dynamic_index_in_dim(jnp.asarray(send_rows), group, 0, False).reshape(-1)
    pick = (chosen[:, None] == jnp.arange(pieces.shape[0], dtype=jnp.int32)[None, :]).astype(BF)
    sent = jnp.dot(pick, pieces, preferred_element_type=F32).astype(BF).reshape(n_dp, count, BOT)
    got = lax.all_to_all(sent, "dp", 0, 0, tiled=True).reshape(n_dp * count, BOT)
    chosen = lax.dynamic_index_in_dim(jnp.asarray(take_rows), group, 0, False)
    pick = (chosen[:, None] == jnp.arange(n_dp * count, dtype=jnp.int32)[None, :]).astype(BF)
    shard_neck = jnp.dot(pick, got, preferred_element_type=F32)
    shard_neck = shard_neck.reshape(trunk_neck.shape)

    grad_norms = jnp.stack(
        [
            jnp.concatenate([back_gain_one, back_gain_two, back_gain_three, both[0], back_gain_proj]),
            jnp.concatenate([back_shift_one, back_shift_two, back_shift_three, both[1], back_shift_proj]),
        ]
    )
    local_square = (
        jnp.sum(shard_aspp * shard_aspp)
        + jnp.sum(expand_own * expand_own)
        + jnp.sum(both_own * both_own)
    )
    total_square = (
        sum_all(jnp.broadcast_to(local_square, (128,)))[0]
        + jnp.sum(grad_norms * grad_norms)
        + jnp.sum(dec_grad * dec_grad)
        + jnp.sum(grad_logvar * grad_logvar)
    )
    grad_norm = jnp.sqrt(total_square)
    factor = jnp.minimum(1.0, CLIP_LIMIT / grad_norm)
    aspp_out = adam_step(trunk_aspp, aspp_first, aspp_second, shard_aspp, factor, 0.04, 0.01)
    neck_out = adam_step(trunk_neck, neck_first, neck_second, shard_neck, factor, 0.04, 0.01)
    norm_out = adam_step(norm_params, norm_first, norm_second, grad_norms, factor, 0.6, 0.0)
    dec_out = adam_step(decoders, decoder_first, decoder_second, dec_grad, factor, 0.12, 0.01)
    log_out = adam_step(log_vars, log_first, log_second, grad_logvar, factor, 0.5, 0.0)
    return (total_loss, grad_norm, *aspp_out, *neck_out, *norm_out, *dec_out, *log_out)


def solution(mesh):
    trunk = P("head", "dp", None)
    return jax.shard_map(
        shards,
        mesh=mesh,
        in_specs=(
            P(None, ("dp", "head")),
            P(),
            P(),
            P("dp"),
            P(None, "dp"),
            P("dp"),
            P("dp"),
            *[trunk] * 6,
            *[P()] * 9,
        ),
        out_specs=(P(), P(), *[trunk] * 6, *[P()] * 9),
        check_vma=False,
    )
```

```python
import functools

import jax
import jax.numpy as jnp
import numpy as np
from jax import lax
from jax.experimental import pallas as pl
from jax.experimental.pallas import tpu as pltpu
from jax.sharding import PartitionSpec as P

FEAT = 2048
BOT = 512
ASP = 256
CLS = 19
OUTS = 22
WIDTH = 128
CROP_DP = 4
QUAD = 512
STEP = 10

EPSILON = 1e-05
BETA_ONE = 0.9
BETA_TWO = 0.95
ADAM_EPSILON = 1e-08
CLIP_LIMIT = 0.05
RATES = (12, 24, 36)

BF = jnp.bfloat16
F32 = jnp.float32


def silu_slope(pre_norm):
    sigmoid_value = jax.nn.sigmoid(pre_norm)
    return sigmoid_value * (1.0 + pre_norm * (1.0 - sigmoid_value))


def dot(a, b, ca, cb):
    return lax.dot_general(a, b, ((ca, cb), ((), ())), preferred_element_type=F32)


def xor_move(x, axis, mask):
    n = lax.axis_size(axis)
    return lax.ppermute(x, axis, [(i, i ^ mask) for i in range(n)])


def xor_round(x, axis, bits):
    if len(bits) == 1:
        return x + xor_move(x, axis, bits[0])
    one, two = bits
    a = xor_move(x, axis, one)
    b = xor_move(x, axis, two)
    c = xor_move(x, axis, one | two)
    return (x + a) + (b + c)


def sum_crop(x):
    return xor_round(xor_round(x, "dp", (1,)), "dp", (2,))


def rounds_of(first, n):
    bits = []
    while first < n:
        bits.append(first)
        first *= 2
    return [tuple(bits[i : i + 2]) for i in range(0, len(bits), 2)]


def sum_dp(x):
    x = xor_round(x, "dp", (1,))
    for bits in rounds_of(2, lax.axis_size("dp")):
        x = xor_round(x, "dp", bits)
    return x


def sum_head(x):
    for bits in rounds_of(1, lax.axis_size("head")):
        x = xor_round(x, "head", bits)
    return x


def sum_all(x):
    return sum_head(sum_dp(x))


def pack(vectors):
    return jnp.concatenate([v.reshape(-1) for v in vectors])


def unpack(joined, sizes):
    out, at = [], 0
    for size in sizes:
        out.append(joined[at : at + size])
        at += size
    return out


def crop_shift(x, by):
    n = lax.axis_size("dp")
    pairs = [(i, i + by) for i in range(n) if i // CROP_DP == (i + by) // CROP_DP and 0 <= i + by < n]
    return lax.ppermute(x, "dp", pairs)


def line_shift(x, by):
    n = lax.axis_size("head")
    return lax.ppermute(x, "head", [(i, i + by) for i in range(n) if 0 <= i + by < n])


def exchange(own):
    return [own] + [xor_move(own, "head", m) for m in range(1, lax.axis_size("head"))]


def in_order(blocks, z):
    stack = jnp.stack(blocks)
    return [lax.dynamic_index_in_dim(stack, z ^ j, 0, False) for j in range(len(blocks))]


def scatter_head(blocks, z):
    n = blocks.shape[0]
    total = lax.dynamic_index_in_dim(blocks, z, 0, False).astype(F32)
    for m in range(1, n):
        total = total + xor_move(lax.dynamic_index_in_dim(blocks, z ^ m, 0, False), "head", m).astype(F32)
    return total


def halve(t, axis, bits, bit, position):
    at = bits.index(bit)
    low = 1 << at
    shape = t.shape
    split = t.reshape(shape[:axis] + (shape[axis] // (2 * low), 2, low) + shape[axis + 1 :])
    mine = (position >> (bit.bit_length() - 1)) & 1
    keep = lax.dynamic_index_in_dim(split, mine, axis + 1, False)
    send = lax.dynamic_index_in_dim(split, 1 - mine, axis + 1, False)
    got = xor_move(send, "dp", bit)
    out = (keep.astype(F32) + got.astype(F32)).astype(BF)
    return out.reshape(shape[:axis] + (shape[axis] // 2,) + shape[axis + 1 :]), [x for x in bits if x != bit]


def scatter_dp(t, axis):
    n = lax.axis_size("dp")
    position = lax.axis_index("dp")
    bits = [1 << k for k in range(n.bit_length() - 1)]
    if not isinstance(t, tuple):
        t, bits = halve(t, axis, bits, 1, position)
        t = yield (t,)
        t = t[0]
        half = t.shape[-1] // 2
        parts = [(t[..., :half], bits), (t[..., half:], bits)]
    else:
        parts = [halve(part, axis, bits, 1, position) for part in t]
        arrays = yield tuple(part for part, _ in parts)
        parts = [(array, left) for array, (_, left) in zip(arrays, parts)]
    order = [1 << k for k in range(1, n.bit_length() - 1)]
    for k in range(0, len(order), 2):
        pair = order[k : k + 2]
        for step in range(len(pair)):
            parts = [
                halve(part, axis, left, pair[step if h == 0 else len(pair) - 1 - step], position)
                for h, (part, left) in enumerate(parts)
            ]
            arrays = yield tuple(part for part, _ in parts)
            parts = [(array, left) for array, (_, left) in zip(arrays, parts)]
    return


def tie(*trees):
    return lax.optimization_barrier(trees)


def held_until(value, *others):
    return lax.optimization_barrier((value, others))[0]


def last_step(steps, now):
    while True:
        try:
            now = steps.send(now)
        except StopIteration:
            return jnp.concatenate(now, axis=-1) if len(now) > 1 else now[0]


def shift_lanes(tile, by, lanes):
    if by == 0:
        return tile
    rolled = pltpu.roll(tile, (-by) % WIDTH, 1)
    keep = (lanes < WIDTH - by) if by > 0 else (lanes >= -by)
    return jnp.where(keep, rolled, 0.0)


def neck_columns_kernel(flip, ext_ref, out_ref):
    rows = ext_ref.shape[0]
    lanes = lax.broadcasted_iota(jnp.int32, (rows, WIDTH), 1)
    count = ext_ref.shape[1] // WIDTH
    for t in range(count):
        tile = ext_ref[:, t * WIDTH : (t + 1) * WIDTH].astype(F32)
        for j in range(3):
            moved = shift_lanes(tile, (j - 1) * 4, lanes).astype(BF)
            for i in range(3):
                at = t - 4 * i
                if 0 <= at < count - 8:
                    tap = 3 * i + j
                    out_ref[8 - tap if flip else tap, :, at * WIDTH : (at + 1) * WIDTH] = moved


def neck_columns(ext, flip):
    rows, width = ext.shape
    block = 64
    return pl.pallas_call(
        functools.partial(neck_columns_kernel, flip),
        grid=(rows // block,),
        in_specs=[pl.BlockSpec((block, width), lambda i: (i, 0))],
        out_specs=pl.BlockSpec((9, block, width - 1024), lambda i: (0, i, 0)),
        out_shape=jax.ShapeDtypeStruct((9, rows, width - 1024), BF),
        compiler_params=pltpu.CompilerParams(vmem_limit_bytes=40 << 20),
        cost_estimate=pl.CostEstimate(flops=0, bytes_accessed=2 * 12 * rows * width, transcendentals=0),
    )(ext)


TAP_STEP = 240


def frames_of(own_rows, n_dp):
    starts = [own_rows * s // 256 * 16 for s in range(n_dp)]
    ends = [-(-own_rows * (s + 1) // 16) for s in range(n_dp)]
    rows = max(end - start for start, end in zip(starts, ends))
    return starts, -(-rows // 16) * 16


def assemble_kernel(pieces, in_ref, out_ref):
    for start, stop, sources in pieces:
        total = None
        for s, at in sources:
            part = in_ref[s, at : at + stop - start, :]
            total = part if total is None else total + part
        out_ref[start:stop, :] = total
    end = pieces[-1][1]
    if end < out_ref.shape[0]:
        out_ref[end:, :] = jnp.zeros((out_ref.shape[0] - end, out_ref.shape[1]), BF)


def assemble(framed, own_rows, total_rows):
    n_dp, frame_rows, width = framed.shape
    starts, _ = frames_of(own_rows, n_dp)
    rows = -(-total_rows // TAP_STEP) * TAP_STEP
    pieces = []
    for g in range(0, -(-total_rows // 16) * 16, 16):
        sources = tuple(
            (s, g - starts[s])
            for s in range(n_dp)
            if own_rows * s < (g + 16) * 16 and own_rows * (s + 1) > g * 16
        )
        if pieces and len(sources) == 1 and len(pieces[-1][2]) == 1 and pieces[-1][2][0][0] == sources[0][0]:
            pieces[-1] = (pieces[-1][0], g + 16, pieces[-1][2])
        else:
            pieces.append((g, g + 16, sources))
    block = 256
    return pl.pallas_call(
        functools.partial(assemble_kernel, pieces),
        grid=(width // block,),
        in_specs=[pl.BlockSpec((n_dp, frame_rows, block), lambda i: (0, 0, i))],
        out_specs=pl.BlockSpec((rows, block), lambda i: (0, i)),
        out_shape=jax.ShapeDtypeStruct((rows, width), BF),
        compiler_params=pltpu.CompilerParams(vmem_limit_bytes=40 << 20),
        cost_estimate=pl.CostEstimate(flops=0, bytes_accessed=4 * rows * width, transcendentals=0),
    )(framed)


def whole(shape):
    return pl.BlockSpec(shape, lambda *_: (0,) * len(shape), pipeline_mode=pl.Buffered(1))


def lane_parts(value):
    total = value[:, :WIDTH]
    for t in range(1, value.shape[1] // WIDTH):
        total = total + value[:, t * WIDTH : (t + 1) * WIDTH]
    return total


def sigmoid_of(value):
    return 0.5 * jnp.tanh(0.5 * value) + 0.5


def shift_quad(value, by, lanes):
    return jnp.concatenate(
        [shift_lanes(value[:, t * WIDTH : (t + 1) * WIDTH], by, lanes) for t in range(4)], axis=1
    )


def neck_conv_kernel(z_ref, s0, s1, s2, s3, before, after, w_ref, mask_ref, out_ref, own_ref, one_ref, two_ref, ext):
    a = pl.program_id(0)

    @pl.when(a == 0)
    def _():
        z = z_ref[0]
        ext[0] = before[...]
        ext[5] = after[...]
        for m, slot in enumerate((s0, s1, s2, s3)):
            ext[1 + jnp.bitwise_xor(z, m)] = slot[...]
        one_ref[...] = jnp.zeros_like(one_ref)
        two_ref[...] = jnp.zeros_like(two_ref)

    own_ref[...] = ext[a + 1]
    rows = out_ref.shape[0]
    lanes = lax.broadcasted_iota(jnp.int32, (rows, WIDTH), 1)
    for j in (1, 0, 2):
        total = None
        for i in range(3):
            part = jnp.dot(w_ref[3 * i + j], ext[a + i], preferred_element_type=F32)
            total = part if total is None else total + part
        if j == 1:
            out_ref[...] = total
        else:
            out_ref[...] += shift_quad(total, (j - 1) * 4, lanes)
    value = out_ref[...]
    masked = value * mask_ref[0:1, :]
    one_ref[...] += lane_parts(masked)
    two_ref[...] += lane_parts(masked * value)


def neck_conv(z, slots, before, after, weights, mask8):
    rows = weights.shape[1]
    width = mask8.shape[1]
    block = lambda a, z_ref: (0, a)
    return pl.pallas_call(
        neck_conv_kernel,
        grid_spec=pltpu.PrefetchScalarGridSpec(
            num_scalar_prefetch=1,
            grid=(width // QUAD,),
            in_specs=[whole(before.shape)] * 6
            + [whole(weights.shape), pl.BlockSpec((8, QUAD), block)],
            out_specs=[
                pl.BlockSpec((rows, QUAD), block),
                pl.BlockSpec((rows, QUAD), block),
                pl.BlockSpec((rows, WIDTH), lambda a, z_ref: (0, 0)),
                pl.BlockSpec((rows, WIDTH), lambda a, z_ref: (0, 0)),
            ],
            scratch_shapes=[pltpu.VMEM((6, rows, QUAD), BF)],
        ),
        out_shape=[
            jax.ShapeDtypeStruct((rows, width), F32),
            jax.ShapeDtypeStruct((rows, width), BF),
            jax.ShapeDtypeStruct((rows, WIDTH), F32),
            jax.ShapeDtypeStruct((rows, WIDTH), F32),
        ],
        compiler_params=pltpu.CompilerParams(vmem_limit_bytes=48 << 20),
        cost_estimate=pl.CostEstimate(flops=18 * rows * rows * width, bytes_accessed=16 << 20, transcendentals=0),
    )(z.reshape(1), *slots, before, after, weights, mask8)


CHUNK = 256


def fetch_quad(away, sources, buffer, sem):
    for k, source in zip((0, 1, 2, 3, -1, -2, -3), sources):

        @pl.when(away == k)
        def _():
            pltpu.make_async_copy(source, buffer, sem).start()


def feature_group_kernel(z_ref, mask_ref, x0, x1, x2, x3, x4, x5, x6, out_ref, xbuf, sem):
    sources = (x0, x1, x2, x3, x4, x5, x6)
    fetch_quad(pl.program_id(0) - z_ref[0], sources, xbuf, sem)
    pltpu.make_async_copy(x0, xbuf, sem).wait()
    mask = mask_ref[0:1, :]

    def place(i, carry):
        at = pl.ds(pl.multiple_of(i * CHUNK, CHUNK), CHUNK)
        out_ref[at, :] = (xbuf[at, :].astype(F32) * mask).astype(BF)
        return carry

    lax.fori_loop(0, out_ref.shape[0] // CHUNK, place, 0)


def feature_group(z, mask8, sources):
    rows = sources[0].shape[0]
    width = mask8.shape[1]
    block = lambda a, z_ref: (0, a)
    return pl.pallas_call(
        feature_group_kernel,
        grid_spec=pltpu.PrefetchScalarGridSpec(
            num_scalar_prefetch=1,
            grid=(width // QUAD,),
            in_specs=[pl.BlockSpec((8, QUAD), block)] + [pl.BlockSpec(memory_space=pl.ANY)] * 7,
            out_specs=pl.BlockSpec((rows, QUAD), block),
            scratch_shapes=[pltpu.VMEM((rows, QUAD), BF), pltpu.SemaphoreType.DMA],
        ),
        out_shape=jax.ShapeDtypeStruct((rows, width), BF),
        compiler_params=pltpu.CompilerParams(vmem_limit_bytes=32 << 20),
        cost_estimate=pl.CostEstimate(flops=0, bytes_accessed=4 * rows * width, transcendentals=0),
    )(z.reshape(1), mask8, *sources)


def aspp_forward_kernel(
    z_ref, pre_ref, coef_ref, mask_ref, w_ref, x0, x1, x2, x3, x4, x5, x6,
    y_ref, slope_ref, core_ref, side_ref, pool_ref, xbuf, held, products, sem
):
    a = pl.program_id(0)
    quads = pl.num_programs(0) - 1
    sources = (x0, x1, x2, x3, x4, x5, x6)
    slot = a % 2
    channels = y_ref.shape[0]
    steps = w_ref.shape[0] // TAP_STEP
    chunk = channels // steps

    @pl.when(a == 0)
    def _():
        fetch_quad(-z_ref[0], sources, xbuf.at[0], sem.at[0])

    @pl.when(a < quads)
    def _():
        pltpu.make_async_copy(x0, xbuf.at[slot], sem.at[slot]).wait()

    @pl.when(a + 1 < quads)
    def _():
        fetch_quad(a + 1 - z_ref[0], sources, xbuf.at[1 - slot], sem.at[1 - slot])

    mask = mask_ref[0:1, :]

    def activate(i):
        at = pl.ds(pl.multiple_of(i * chunk, chunk), chunk)
        x = xbuf[slot, at, :].astype(F32) * mask
        value = pre_ref[at, :].astype(F32) * coef_ref[at, 0:1] + coef_ref[at, 1:2] + x
        sig = sigmoid_of(value)
        y_ref[at, :] = (value * sig * mask).astype(BF)
        slope_ref[at, :] = (sig * (1.0 + value * (1.0 - sig)) * mask).astype(BF)

    def multiply(i):
        at = pl.ds(pl.multiple_of(i * TAP_STEP, 16), TAP_STEP)
        products[at, :] = jnp.dot(w_ref[at, :], held[...], preferred_element_type=F32)

    @pl.when(a == 0)
    def _():
        lax.fori_loop(0, steps, lambda i, c: (activate(i), c)[1], 0)

    @pl.when((a > 0) & (a < quads))
    def _():
        def both(i, carry):
            multiply(i)
            activate(i)
            return carry

        lax.fori_loop(0, steps, both, 0)

    @pl.when(a == quads)
    def _():
        lax.fori_loop(0, steps, lambda i, c: (multiply(i), c)[1], 0)

    held[...] = y_ref[...]

    @pl.when(a > 0)
    def _():
        lanes = lax.broadcasted_iota(jnp.int32, (64, WIDTH), 1)
        core_ref[0] = products[0:64, :]
        pool_ref[0] = lane_parts(products[64 * 28 : 64 * 29, :])
        for t in range(4):
            part = slice(t * WIDTH, (t + 1) * WIDTH)
            for br, rate in enumerate(RATES):
                for i in range(3):
                    total = None
                    for j in range(3):
                        row = 64 * (1 + 9 * br + 3 * i + j)
                        moved = shift_lanes(products[row : row + 64, part], (j - 1) * rate, lanes)
                        total = moved if total is None else total + moved
                    if i == 1:
                        core_ref[1 + br, :, part] = total
                    else:
                        side_ref[2 * br + i // 2, 0, :, part] = total.astype(BF)


def aspp_forward(z, pre, coef, mask8, weights, sources):
    rows, width = pre.shape
    quads = width // QUAD
    now = lambda a: jnp.minimum(a, quads - 1)
    done = lambda a: jnp.maximum(a - 1, 0)
    wide = pl.BlockSpec((rows, QUAD), lambda a, z_ref: (0, now(a)))
    return pl.pallas_call(
        aspp_forward_kernel,
        grid_spec=pltpu.PrefetchScalarGridSpec(
            num_scalar_prefetch=1,
            grid=(quads + 1,),
            in_specs=[
                wide,
                whole(coef.shape),
                pl.BlockSpec((8, QUAD), lambda a, z_ref: (0, now(a))),
                whole(weights.shape),
            ]
            + [pl.BlockSpec(memory_space=pl.ANY)] * 7,
            out_specs=[
                wide,
                wide,
                pl.BlockSpec((4, 64, QUAD), lambda a, z_ref: (0, 0, done(a))),
                pl.BlockSpec((6, 1, 64, QUAD), lambda a, z_ref: (0, done(a), 0, 0)),
                pl.BlockSpec((1, 64, WIDTH), lambda a, z_ref: (done(a), 0, 0)),
            ],
            scratch_shapes=[
                pltpu.VMEM((2, rows, QUAD), BF),
                pltpu.VMEM((rows, QUAD), BF),
                pltpu.VMEM((weights.shape[0], QUAD), F32),
                pltpu.SemaphoreType.DMA((2,)),
            ],
        ),
        out_shape=[
            jax.ShapeDtypeStruct((rows, width), BF),
            jax.ShapeDtypeStruct((rows, width), BF),
            jax.ShapeDtypeStruct((4, 64, width), F32),
            jax.ShapeDtypeStruct((6, quads, 64, QUAD), BF),
            jax.ShapeDtypeStruct((quads, 64, WIDTH), F32),
        ],
        compiler_params=pltpu.CompilerParams(vmem_limit_bytes=58 << 20),
        cost_estimate=pl.CostEstimate(
            flops=2 * 29 * 64 * rows * width, bytes_accessed=48 << 20, transcendentals=rows * width
        ),
    )(z.reshape(1), pre, coef, mask8, weights, *sources)


def aspp_backward_kernel(
    one_ref, rows_ref, pool_in, mask_ref, w_ref, slope_ref, pre_ref,
    out_ref, act_ref, sum_ref, dot_ref
):
    @pl.when(pl.program_id(0) == 0)
    def _():
        sum_ref[...] = jnp.zeros_like(sum_ref)
        dot_ref[...] = jnp.zeros_like(dot_ref)

    lanes = lax.broadcasted_iota(jnp.int32, (64, WIDTH), 1)
    out_ref[0:64, :] = one_ref[...].astype(BF)
    out_ref[64 * 29 :, :] = jnp.zeros((out_ref.shape[0] - 64 * 29, QUAD), BF)
    for t in range(4):
        part = slice(t * WIDTH, (t + 1) * WIDTH)
        out_ref[64 * 28 : 64 * 29, part] = (pool_in[...] * mask_ref[0:1, part]).astype(BF)
        for br, rate in enumerate(RATES):
            for i in range(3):
                tile = rows_ref[br, i, 0, :, part].astype(F32)
                for j in range(3):
                    at = 64 * (1 + 9 * br + 3 * i + j)
                    out_ref[at : at + 64, part] = shift_lanes(tile, (1 - j) * rate, lanes).astype(BF)

    def multiply(i, carry):
        at = pl.ds(pl.multiple_of(i * CHUNK, CHUNK), CHUNK)
        grad = jnp.dot(w_ref[at, :], out_ref[...], preferred_element_type=F32)
        act = grad * slope_ref[at, :].astype(F32)
        act_ref[at, :] = act.astype(BF)
        sum_ref[at, :] += lane_parts(act)
        dot_ref[at, :] += lane_parts(act * pre_ref[at, :].astype(F32))
        return carry

    lax.fori_loop(0, act_ref.shape[0] // CHUNK, multiply, 0, unroll=4)


def aspp_backward(one, rows, pool, mask8, weights_t, slope, pre):
    channels, width = pre.shape
    quads = width // QUAD
    count = weights_t.shape[1]
    block = lambda a: (0, a)
    wide = pl.BlockSpec((channels, QUAD), block)
    return pl.pallas_call(
        aspp_backward_kernel,
        grid=(quads,),
        in_specs=[
            pl.BlockSpec((64, QUAD), block),
            pl.BlockSpec((3, 3, 1, 64, QUAD), lambda a: (0, 0, a, 0, 0)),
            whole((64, WIDTH)),
            pl.BlockSpec((8, QUAD), block),
            whole(weights_t.shape),
            wide,
            wide,
        ],
        out_specs=[
            pl.BlockSpec((count, QUAD), block),
            wide,
            pl.BlockSpec((channels, WIDTH), lambda a: (0, 0)),
            pl.BlockSpec((channels, WIDTH), lambda a: (0, 0)),
        ],
        out_shape=[
            jax.ShapeDtypeStruct((count, width), BF),
            jax.ShapeDtypeStruct((channels, width), BF),
            jax.ShapeDtypeStruct((channels, WIDTH), F32),
            jax.ShapeDtypeStruct((channels, WIDTH), F32),
        ],
        compiler_params=pltpu.CompilerParams(vmem_limit_bytes=58 << 20),
        cost_estimate=pl.CostEstimate(
            flops=2 * count * channels * width, bytes_accessed=48 << 20, transcendentals=0
        ),
    )(one, rows, pool, mask8, weights_t, slope, pre)


def taps_grad_kernel(starts, spread_ref, y_ref, project_ref, out_ref, total):
    total[...] = dot(spread_ref[...], y_ref[...], (1,), (1,)).astype(BF)
    low = 29 * 64
    total[low : low + project_ref.shape[0], :] = project_ref[...]
    for s, start in enumerate(starts):
        out_ref[s] = total[start : start + out_ref.shape[1], :]


def taps_grad(starts, frame_rows, spread, y, project, part, parts):
    rows, pixels = spread.shape
    width = y.shape[0] // parts
    block = 256
    first = part * width // block
    return pl.pallas_call(
        functools.partial(taps_grad_kernel, starts),
        grid=(width // block,),
        in_specs=[
            whole((rows, pixels)),
            pl.BlockSpec((block, pixels), lambda i: (first + i, 0)),
            pl.BlockSpec((project.shape[0], block), lambda i: (0, first + i)),
        ],
        out_specs=pl.BlockSpec((len(starts), frame_rows, block), lambda i: (0, 0, i)),
        out_shape=jax.ShapeDtypeStruct((len(starts), frame_rows, width), BF),
        scratch_shapes=[pltpu.VMEM((rows, block), BF)],
        compiler_params=pltpu.CompilerParams(vmem_limit_bytes=48 << 20),
        cost_estimate=pl.CostEstimate(
            flops=2 * rows * pixels * width, bytes_accessed=20 << 20, transcendentals=0
        ),
    )(spread, y, project)


def side_rows(side):
    result = []
    at = lax.axis_index("dp") % CROP_DP
    n = lax.axis_size("dp")
    from_one = crop_shift(jnp.concatenate([side[0, 1:4], side[2, 0:2]]), 1)
    to_one = crop_shift(jnp.concatenate([side[1, 0:3], side[3, 2:4]]), -1)
    up = jnp.concatenate([side[2, 2:4], side[4, 0:3]])
    down = jnp.concatenate([side[3, 0:2], side[5, 1:4]])
    two = xor_move(jnp.where(at < 2, up, down), "dp", 2)
    from_two = jnp.where(at < 2, jnp.zeros_like(two), two)
    to_two = jnp.where(at < 2, two, jnp.zeros_like(two))
    ends = [(i, i + 3 - 2 * (i % CROP_DP)) for i in range(n) if i % CROP_DP in (0, CROP_DP - 1)]
    three = lax.ppermute(jnp.where(at == 0, side[4, 3:4], side[5, 0:1]), "dp", ends)
    from_three = jnp.where(at == 0, jnp.zeros_like(three), three)
    to_three = jnp.where(at == 0, three, jnp.zeros_like(three))
    result.append(jnp.concatenate([from_one[0:3], side[0, 0:1]]))
    result.append(jnp.concatenate([side[1, 3:4], to_one[0:3]]))
    result.append(jnp.concatenate([from_two[0:2], from_one[3:5]]))
    result.append(jnp.concatenate([to_one[3:5], to_two[0:2]]))
    result.append(jnp.concatenate([from_three, from_two[2:5]]))
    result.append(jnp.concatenate([to_two[2:5], to_three]))
    return result


def adam_step(weight, first_m, second_m, gradient, factor, rate, decay):
    clipped = gradient * factor
    new_first = BETA_ONE * first_m + (1.0 - BETA_ONE) * clipped
    new_second = BETA_TWO * second_m + (1.0 - BETA_TWO) * clipped * clipped
    corrected = (
        new_first
        / (1.0 - BETA_ONE**STEP)
        / (jnp.sqrt(new_second / (1.0 - BETA_TWO**STEP)) + ADAM_EPSILON)
    )
    return (weight - rate * (corrected + decay * weight), new_first, new_second)


def flat_rows(quads):
    return jnp.concatenate([quads[a] for a in range(quads.shape[0])], axis=1)


def quad_blocks(flat):
    return [flat[..., a * QUAD : (a + 1) * QUAD] for a in range(flat.shape[-1] // QUAD)]


def reduce_weights(trunk_neck, z, group):
    heads, n_dp = lax.axis_size("head"), lax.axis_size("dp")
    each = BOT // heads
    rows = trunk_neck.shape[1] // 16
    if trunk_neck.shape[1] % 16 or 2 * rows < each or n_dp < 4:
        return None, ()
    room = -(-rows // 8) * 8
    mine = trunk_neck[0].reshape(rows, FEAT).astype(BF)
    mine = jnp.concatenate([mine, jnp.zeros((room - rows, FEAT), BF)], axis=0)
    mine = lax.optimization_barrier(mine)
    held = mine
    for m in range(2, n_dp, 2):
        got = lax.ppermute(mine, "dp", [(c, c ^ m) for c in range(2)])
        held = jnp.where((group ^ m) < 2, got, held)
    slots = exchange(held)
    stack = jnp.stack(slots)
    stack = jnp.concatenate([stack, xor_move(stack, "dp", 1)], axis=0).reshape(-1, FEAT)
    channel = jnp.arange(BOT, dtype=jnp.int32)
    place = channel % each
    source = ((place // rows) ^ (group & 1)) * heads + ((channel // each) ^ z)
    source = source * room + place % rows
    pick = (source[:, None] == jnp.arange(stack.shape[0], dtype=jnp.int32)[None, :]).astype(BF)
    return jnp.dot(pick, stack, preferred_element_type=F32).astype(BF), slots


def owner_tables(n_dp, share_rows, wide, heads):
    quarter = BOT // heads
    places = []
    for p in range(n_dp):
        rows = []
        for k in range(wide):
            rows += [(share_rows * p + r) * wide + k for r in range(share_rows)]
        for tap in range(9):
            rows += [quarter * (wide + tap) + share_rows * p + r for r in range(share_rows)]
        rows += [quarter * (wide + 9) + share_rows * wide * p + r for r in range(share_rows * wide)]
        places.append(np.array(rows))
    own = len(places[0])
    lists = [[np.nonzero(place // own == s)[0] for s in range(n_dp)] for place in places]
    count = -(-max(len(x) for row in lists for x in row) // 16) * 16
    send = np.full((n_dp, n_dp, count), -1, np.int32)
    take = np.zeros((n_dp, own), np.int32)
    for p in range(n_dp):
        for s in range(n_dp):
            rows = lists[p][s]
            send[p, s, : len(rows)] = rows
            take[s, places[p][rows] - own * s] = p * count + np.arange(len(rows))
    return send, take


def shards(
    features,
    crop_rows,
    crop_cols,
    labels,
    offset_targets,
    depth_targets,
    lidar_mask,
    trunk_aspp,
    aspp_first,
    aspp_second,
    trunk_neck,
    neck_first,
    neck_second,
    norm_params,
    norm_first,
    norm_second,
    decoders,
    decoder_first,
    decoder_second,
    log_vars,
    log_first,
    log_second,
):
    heads = lax.axis_size("head")
    z = lax.axis_index("head")
    group = lax.axis_index("dp")
    crop = group // CROP_DP
    pixels = heads * QUAD
    share = 1.0 / heads
    quarter = ASP // heads

    n_dp = lax.axis_size("dp")
    reduce_w, first = reduce_weights(trunk_neck, z, group)
    neck_low = held_until(trunk_neck, *first).reshape(1, -1, BOT).astype(BF)
    neck_low = lax.all_gather(neck_low, "head", axis=0, tiled=True)
    held_features = held_until(features, *first)
    x_left = [features, line_shift(held_features, 1)]
    x_right = [features, line_shift(held_features, -1)]
    if reduce_w is None:
        neck_low = lax.all_gather(neck_low, "dp", axis=1, tiled=True)
        reduce_w = neck_low[:, : FEAT // heads].reshape(BOT, FEAT)
    own_rows = trunk_aspp.shape[1]
    frames, frame_rows = frames_of(own_rows, n_dp)
    inset = (group * own_rows) % 256
    framed = lax.dynamic_update_slice_in_dim(
        jnp.zeros((frame_rows * 16, 128), F32), trunk_aspp[0], inset, 0
    )
    framed = framed.reshape(frame_rows, FEAT).astype(BF)
    gathered = lax.all_gather(framed, "dp", axis=0)

    place = jnp.arange(pixels, dtype=jnp.int32)
    row_place = group % CROP_DP * (pixels // WIDTH) + place // WIDTH
    col_place = place % WIDTH
    mask = ((row_place < crop_rows[crop]) & (col_place < crop_cols[crop])).astype(F32)[None, :]
    mask_own = lax.dynamic_slice_in_dim(mask, z * QUAD, QUAD, 1)
    total_n = jnp.sum((crop_rows * crop_cols).astype(F32))
    crop_n = (crop_rows[crop] * crop_cols[crop]).astype(F32)

    def own_pixels(a):
        return lax.dynamic_slice_in_dim(a, z * QUAD, QUAD, a.ndim - 1)

    labels_own = own_pixels(labels)
    offset_own = own_pixels(offset_targets)
    depth_own = own_pixels(depth_targets)
    lidar_own = own_pixels(lidar_mask).astype(F32) * mask_own[0]

    gains, shifts = (norm_params[0], norm_params[1])
    bounds = [0, BOT, 2 * BOT, 2 * BOT + FEAT, 2 * BOT + FEAT + 4 * ASP, 2 * BOT + FEAT + 5 * ASP]

    def slot(vector, index):
        return vector[bounds[index] : bounds[index + 1]]

    def own_aspp(vector):
        return lax.dynamic_slice_in_dim(vector.reshape(4, heads, quarter), z, 1, 1).reshape(-1)

    gain_one, gain_two, gain_three, gain_proj = [slot(gains, i) for i in (0, 1, 2, 4)]
    shift_one, shift_two, shift_three, shift_proj = [slot(shifts, i) for i in (0, 1, 2, 4)]
    gain_aspp, shift_aspp = own_aspp(slot(gains, 3)), own_aspp(slot(shifts, 3))

    def moments(pre, m):
        masked = pre * m
        return jnp.sum(masked, axis=-1), jnp.sum(masked * pre, axis=-1)

    def coefficients(total, square):
        mean = total / total_n
        inv = lax.rsqrt(square / total_n - mean * mean + EPSILON)
        return mean, inv

    def normed(pre, mean, inv):
        return (pre - mean[:, None]) * inv[:, None]

    def scaled(hat, gain, shift):
        return gain[:, None] * hat + shift[:, None]

    x_own = features * mask_own.astype(BF)
    pre_one = jnp.dot(reduce_w, x_own, preferred_element_type=F32)
    sums = sum_all(pack((*moments(pre_one, mask_own), jnp.broadcast_to(jnp.sum(lidar_own), (128,)))))
    total, square, lidar = unpack(sums, (BOT, BOT, 128))
    lidar_n = lidar[0]
    mean_one, inv_one = coefficients(total, square)
    low_one = (jax.nn.silu(scaled(normed(pre_one, mean_one, inv_one), gain_one, shift_one)) * mask_own).astype(BF)
    low_one, x_left[1], x_right[1] = tie(low_one, x_left[1], x_right[1])
    slots = exchange(low_one)
    if first:
        neck_low = lax.all_gather(held_until(neck_low, low_one), "dp", axis=1, tiled=True)
    first_end = FEAT // heads
    second_end = first_end + 9 * BOT // heads
    middle = neck_low[:, first_end:second_end].reshape(heads, 9, BOT // heads, BOT)
    middle = jnp.moveaxis(middle, 0, 1).reshape(9, BOT, BOT)
    expand_w = neck_low[:, second_end:].reshape(FEAT, BOT)


    flat_total = trunk_aspp.shape[1] * n_dp // 16
    x_left[-1], x_right[-1] = held_until((x_left[-1], x_right[-1]), slots)
    for _ in range(1, heads - 1):
        x_left.append(line_shift(x_left[-1], 1))
        x_right.append(line_shift(x_right[-1], -1))

    def block_of(j):
        block = slots[0]
        for m in range(1, heads):
            block = jnp.where((z ^ m) == j, slots[m], block)
        return block

    before = crop_shift(block_of(heads - 1), 1)
    after = crop_shift(block_of(0), -1)
    mask8 = jnp.broadcast_to(mask, (8, pixels))
    pre_two, h_one, one_part, two_part = neck_conv(z, slots, before, after, middle, mask8)
    sums = sum_dp(pack((jnp.sum(one_part, axis=1), jnp.sum(two_part, axis=1))))
    mean_two, inv_two = coefficients(*unpack(sums, (BOT, BOT)))
    hat_two = normed(pre_two, mean_two, inv_two)
    in_two = scaled(hat_two, gain_two, shift_two)
    h_two = (jax.nn.silu(in_two) * mask).astype(BF)
    aspp_rows = assemble(held_until(gathered, pre_two), own_rows, flat_total)
    pre_three = jnp.dot(expand_w, h_two, preferred_element_type=F32)
    mean_three, inv_three = coefficients(*unpack(sum_dp(pack(moments(pre_three, mask))), (FEAT, FEAT)))
    pre_three = pre_three.astype(BF)
    scale_three = gain_three * inv_three
    coef = jnp.stack([scale_three, shift_three - scale_three * mean_three], axis=1)
    sources = [features, *x_right[1:], *x_left[1:]]
    y, slope_three, middle_rows, side, pool_part = aspp_forward(
        z, pre_three, coef, mask8, aspp_rows, sources
    )

    moved = side_rows(side)
    project_q = held_until(aspp_rows, side)[29 * quarter : flat_total].reshape(quarter, 5, heads, quarter)
    project_q = jnp.moveaxis(project_q, 2, 0).reshape(heads, quarter, 5 * quarter)
    received = [lax.dynamic_index_in_dim(project_q, z, 0, False)]
    for m in range(1, heads):
        received.append(xor_move(lax.dynamic_index_in_dim(project_q, z ^ m, 0, False), "head", m))
    project_own = jnp.concatenate(in_order(received, z), axis=0)
    branches = [middle_rows[0]]
    for br in range(3):
        branches.append(
            middle_rows[1 + br]
            + flat_rows(moved[2 * br]).astype(F32)
            + flat_rows(moved[2 * br + 1]).astype(F32)
        )
    pre_aspp = jnp.concatenate(branches, axis=0)
    pool_local = jnp.sum(pool_part, axis=(0, 2))
    local = pack((*moments(pre_aspp, mask), pool_local, jnp.zeros((64,), F32)))
    local = sum_crop(local)
    pool_sum = local[2 * ASP : 2 * ASP + quarter]
    for bits in rounds_of(4, lax.axis_size("dp")):
        local = xor_round(local, "dp", bits)
    mean_aspp, inv_aspp = coefficients(local[:ASP], local[ASP : 2 * ASP])
    hat_aspp = normed(pre_aspp, mean_aspp, inv_aspp)
    in_aspp = scaled(hat_aspp, gain_aspp, shift_aspp)
    act_aspp = jax.nn.silu(in_aspp) * mask
    pool_pre = pool_sum / crop_n
    joined = jnp.concatenate([act_aspp, jax.nn.silu(pool_pre)[:, None] * mask], axis=0).astype(BF)

    part_proj = jnp.dot(project_own, joined, preferred_element_type=F32)
    pre_proj = scatter_head(jnp.stack(quad_blocks(part_proj.astype(BF))), z)
    x_group = feature_group(z, held_until(mask8, part_proj), sources)
    pre_proj, x_group = tie(pre_proj, x_group)
    mean_proj, inv_proj = coefficients(*unpack(sum_all(pack(moments(pre_proj, mask_own))), (ASP, ASP)))
    hat_proj = normed(pre_proj, mean_proj, inv_proj)
    in_proj = scaled(hat_proj, gain_proj, shift_proj)
    feat = (jax.nn.silu(in_proj) * mask_own).astype(BF)

    low_dec = decoders.astype(BF)
    hidden_w, out_w = low_dec[: 3 * ASP], low_dec[3 * ASP :]
    dec_pre = jnp.dot(hidden_w, feat, preferred_element_type=F32)
    hidden = jax.nn.silu(dec_pre).astype(BF)
    row_sets = ((0, CLS), (CLS, CLS + 2), (CLS + 2, CLS + 3))
    logits = [
        jnp.dot(out_w, hidden[t * ASP : (t + 1) * ASP], preferred_element_type=F32)[lo:hi]
        for t, (lo, hi) in enumerate(row_sets)
    ]
    sem_logits, off_logits, dep_logits = logits
    valid_own = mask_own[0]
    label_hot = (jnp.arange(CLS, dtype=jnp.int32)[:, None] == labels_own[None, :]).astype(F32)
    log_total = jax.nn.logsumexp(sem_logits, axis=0)
    sem_sum = jnp.sum((log_total - jnp.sum(label_hot * sem_logits, axis=0)) * valid_own)
    off_diff = off_logits - offset_own
    off_root = jnp.sqrt(off_diff * off_diff + 1.0)
    off_sum = jnp.sum((off_root - 1.0) * valid_own)
    dep_logit = dep_logits[0]
    dep_diff = jax.nn.softplus(dep_logit) - depth_own
    dep_root = jnp.sqrt(dep_diff * dep_diff + 1.0)
    dep_sum = jnp.sum((dep_root - 1.0) * lidar_own)
    divisors = jnp.stack([total_n, total_n, lidar_n])
    weights = jnp.exp(-log_vars) / divisors
    grad_sem = (jax.nn.softmax(sem_logits, axis=0) - label_hot) * valid_own * weights[0]
    grad_off = off_diff / off_root * valid_own * weights[1]
    grad_dep = (dep_diff / dep_root * jax.nn.sigmoid(dep_logit) * lidar_own * weights[2])[None, :]
    grad_logits = [g.astype(BF) for g in (grad_sem, grad_off, grad_dep)]
    grad_out_w = []
    grad_hidden = []
    for t, (lo, hi) in enumerate(row_sets):
        grad_out_w.append(dot(grad_logits[t], hidden[t * ASP : (t + 1) * ASP], (1,), (1,)))
        grad_hidden.append(dot(out_w[lo:hi], grad_logits[t], (0,), (0,)))
    grad_dec_pre = (jnp.concatenate(grad_hidden, axis=0) * silu_slope(dec_pre)).astype(BF)
    grad_hidden_w = dot(grad_dec_pre, feat, (1,), (1,))
    grad_feat = dot(hidden_w, grad_dec_pre, (0,), (0,))
    dec_grad = lax.psum(jnp.concatenate([grad_hidden_w, *grad_out_w], axis=0), ("dp", "head"))

    grad_act = grad_feat * mask_own * silu_slope(in_proj)
    sums = sum_all(
        pack(
            (
                jnp.sum(grad_act, axis=-1),
                jnp.sum(grad_act * hat_proj, axis=-1),
                jnp.stack([sem_sum, off_sum, dep_sum]),
                jnp.zeros((125,), F32),
            )
        )
    )
    back_shift_proj, back_gain_proj, loss_sums = unpack(sums, (ASP, ASP, 3))
    losses = loss_sums / divisors
    total_loss = jnp.sum(jnp.exp(-log_vars) * losses + log_vars)
    grad_logvar = 1.0 - jnp.exp(-log_vars) * losses
    grad_proj = (
        mask_own
        * (gain_proj * inv_proj)[:, None]
        * (grad_act - (back_shift_proj / total_n)[:, None] - hat_proj * (back_gain_proj / total_n)[:, None])
    ).astype(BF)
    tap_wt = held_until(aspp_rows, grad_proj).T
    grad_blocks, tap_wt = tie(exchange(grad_proj), tap_wt)
    grad_proj = jnp.concatenate(in_order(grad_blocks, z), axis=1)
    grad_project = dot(grad_proj, joined, (1,), (1,)).astype(BF).reshape(heads, quarter, 5 * quarter)
    grad_joined = dot(project_own, grad_proj, (0,), (0,))

    grad_act = grad_joined[:ASP] * mask * silu_slope(in_aspp)
    local = pack(
        (
            jnp.sum(grad_act, axis=-1),
            jnp.sum(grad_act * hat_aspp, axis=-1),
            jnp.sum(grad_joined[ASP:] * mask, axis=-1),
            jnp.zeros((64,), F32),
        )
    )
    local = sum_crop(local)
    pool_row = local[2 * ASP : 2 * ASP + quarter]
    for bits in rounds_of(4, lax.axis_size("dp")):
        local = xor_round(local, "dp", bits)
    back_shift_aspp, back_gain_aspp = local[:ASP], local[ASP : 2 * ASP]
    grad_aspp = (
        mask
        * (gain_aspp * inv_aspp)[:, None]
        * (grad_act - (back_shift_aspp / total_n)[:, None] - hat_aspp * (back_gain_aspp / total_n)[:, None])
    ).astype(BF)
    grad_pool = (pool_row * silu_slope(pool_pre)).astype(BF).astype(F32) / crop_n
    parts = [jnp.stack(quad_blocks(grad_aspp[quarter * (br + 1) : quarter * (br + 2)])) for br in range(3)]
    moved = side_rows(jnp.stack([part for part in parts for _ in range(2)]))
    rows = jnp.stack(
        [jnp.stack([moved[2 * br + 1], parts[br], moved[2 * br]]) for br in range(3)]
    )
    spread, act_three, sum_part, dot_part = aspp_backward(
        grad_aspp[:quarter],
        rows,
        jnp.broadcast_to(grad_pool[:, None], (quarter, WIDTH)),
        mask8,
        tap_wt,
        slope_three,
        pre_three,
    )

    spread_norms = jnp.stack([back_gain_aspp, back_shift_aspp]).reshape(2, 4, 1, quarter)
    own_place = (jnp.arange(heads) == z)[None, None, :, None] & (group == 0)
    spread_norms = jnp.where(own_place, spread_norms, 0.0)
    sum_three = jnp.sum(sum_part, axis=1)
    sums = xor_round(
        pack((sum_three, (jnp.sum(dot_part, axis=1) - mean_three * sum_three) * inv_three, spread_norms)),
        "dp",
        (1,),
    )

    swapped = [
        xor_move(lax.dynamic_index_in_dim(grad_project, z ^ m, 0, False), "head", m)
        if m
        else lax.dynamic_index_in_dim(grad_project, z, 0, False)
        for m in range(heads)
    ]
    own_project = jnp.stack(in_order(swapped, z)).reshape(heads, quarter, 5, quarter)
    own_project = jnp.moveaxis(own_project, 0, 2).reshape(-1, FEAT)
    own_project = jnp.concatenate([own_project, jnp.zeros((-flat_total % 16, FEAT), BF)], axis=0)
    sums, spread, own_project = tie(sums, spread, own_project)
    first_half = taps_grad(frames, frame_rows, spread, y, own_project, 0, 2)
    for bits in rounds_of(2, n_dp):
        sums = xor_round(sums, "dp", bits)
    sums, first_half, spread = tie(sums, first_half, spread)
    second_half = taps_grad(frames, frame_rows, spread, y, own_project, 1, 2)
    sums = sum_head(sums)
    sums, first_half, second_half, dec_grad = tie(sums, first_half, second_half, dec_grad)
    aspp_steps = scatter_dp((first_half, second_half), 0)
    aspp_now = next(aspp_steps)
    back_shift_three, back_gain_three, both = unpack(sums, (FEAT, FEAT, 8 * ASP))
    both = both.reshape(2, 4 * ASP)

    def norm_back(grad_act, hat, gain, inv, back_shift, back_gain):
        scale = share / total_n
        return (
            mask
            * (gain * inv)[:, None]
            * (grad_act - (back_shift * scale)[:, None] - hat * (back_gain * scale)[:, None])
        ).astype(BF)

    hat_three = normed(pre_three.astype(F32), mean_three, inv_three)
    grad_three = norm_back(
        act_three.astype(F32), hat_three, gain_three, inv_three, back_shift_three, back_gain_three
    )
    grad_h_two = dot(expand_w, grad_three, (0,), (0,))
    grad_act = grad_h_two * mask * silu_slope(in_two)
    sums = pack((jnp.sum(grad_act, axis=-1), jnp.sum(grad_act * hat_two, axis=-1)))
    sums = xor_round(sums, "dp", (1,))
    sums, grad_three = tie(sums, grad_three)
    grad_expand = dot(grad_three, h_two, (1,), (1,)).astype(BF).reshape(heads, n_dp, -1, BOT)
    for bits in rounds_of(2, n_dp):
        sums = xor_round(sums, "dp", bits)
    sums = sum_head(sums)
    sums, grad_expand, aspp_now = tie(sums, grad_expand, aspp_now)
    back_shift_two, back_gain_two = unpack(sums, (BOT, BOT))
    grad_two = norm_back(grad_act, hat_two, gain_two, inv_two, back_shift_two, back_gain_two)
    before = crop_shift(grad_two[:, -QUAD:], 1)
    after = crop_shift(grad_two[:, :QUAD], -1)
    before, after, aspp_now, grad_expand = tie(before, after, aspp_now, grad_expand)
    aspp_now = aspp_steps.send(aspp_now)
    expand_steps = scatter_dp(grad_expand, 1)
    expand_now = next(expand_steps)
    columns = neck_columns(jnp.concatenate([before, grad_two, after], axis=1), True)
    grad_h_one = lax.dot_general(middle, columns, (((0, 1), (0, 1)), ((), ())), preferred_element_type=F32)
    group_one = jnp.dot(reduce_w, x_group, preferred_element_type=F32)
    hat_one = normed(group_one, mean_one, inv_one)
    grad_act = grad_h_one * mask * silu_slope(scaled(hat_one, gain_one, shift_one))
    sums = pack((jnp.sum(grad_act, axis=-1), jnp.sum(grad_act * hat_one, axis=-1)))
    sums, aspp_now, expand_now = tie(sums, aspp_now, expand_now)
    sums = xor_round(sums, "dp", (1,))
    sums, columns = tie(sums, columns)
    grad_middle = dot(columns, h_one, (2,), (1,)).astype(BF).reshape(9, heads, n_dp, -1, BOT)
    for bits in rounds_of(2, n_dp):
        sums = xor_round(sums, "dp", bits)
    sums = sum_head(sums)
    sums, grad_middle, aspp_now, expand_now = tie(sums, grad_middle, aspp_now, expand_now)
    middle_steps = scatter_dp(grad_middle, 2)
    middle_now = next(middle_steps)
    aspp_block = last_step(aspp_steps, aspp_now)
    expand_block = last_step(expand_steps, expand_now)
    back_shift_one, back_gain_one = unpack(sums, (BOT, BOT))
    grad_one = norm_back(grad_act, hat_one, gain_one, inv_one, back_shift_one, back_gain_one)
    grad_reduce = dot(grad_one, x_group, (1,), (1,)).astype(BF)
    wide = FEAT // BOT
    grad_reduce = jnp.stack([grad_reduce[:, k * BOT : (k + 1) * BOT] for k in range(wide)])
    reduce_steps = scatter_dp(grad_reduce.reshape(wide, heads, n_dp, -1, BOT), 2)
    reduce_now, middle_now, aspp_block, expand_block = tie(
        next(reduce_steps), middle_now, aspp_block, expand_block
    )
    expand_own = scatter_head(expand_block.reshape(heads, -1, BOT), z)
    both_now = jnp.concatenate([reduce_now[0], middle_now[0]], axis=0)
    both_block = last_step(reduce_steps, reduce_steps.send((both_now,)))

    shard_aspp = lax.dynamic_slice_in_dim(
        aspp_block.astype(F32).reshape(frame_rows * 16, 128), inset, own_rows, 0
    )[None]
    share_rows = BOT // heads // n_dp
    both_block = both_block.reshape(wide + 9, heads, share_rows, BOT)
    both_own = scatter_head(jnp.moveaxis(both_block, 1, 0), z)
    pieces = jnp.concatenate([both_own, expand_own.reshape(wide, share_rows, BOT)], axis=0).astype(BF)
    pieces = pieces.reshape(-1, BOT)
    send_rows, take_rows = owner_tables(n_dp, share_rows, wide, heads)
    count = send_rows.shape[2]
    chosen = lax.dynamic_index_in_dim(jnp.asarray(send_rows), group, 0, False).reshape(-1)
    pick = (chosen[:, None] == jnp.arange(pieces.shape[0], dtype=jnp.int32)[None, :]).astype(BF)
    sent = jnp.dot(pick, pieces, preferred_element_type=F32).astype(BF).reshape(n_dp, count, BOT)
    got = lax.all_to_all(sent, "dp", 0, 0, tiled=True).reshape(n_dp * count, BOT)
    chosen = lax.dynamic_index_in_dim(jnp.asarray(take_rows), group, 0, False)
    pick = (chosen[:, None] == jnp.arange(n_dp * count, dtype=jnp.int32)[None, :]).astype(BF)
    shard_neck = jnp.dot(pick, got, preferred_element_type=F32)
    shard_neck = shard_neck.reshape(trunk_neck.shape)

    grad_norms = jnp.stack(
        [
            jnp.concatenate([back_gain_one, back_gain_two, back_gain_three, both[0], back_gain_proj]),
            jnp.concatenate([back_shift_one, back_shift_two, back_shift_three, both[1], back_shift_proj]),
        ]
    )
    local_square = (
        jnp.sum(shard_aspp * shard_aspp)
        + jnp.sum(expand_own * expand_own)
        + jnp.sum(both_own * both_own)
    )
    total_square = (
        sum_all(jnp.broadcast_to(local_square, (128,)))[0]
        + jnp.sum(grad_norms * grad_norms)
        + jnp.sum(dec_grad * dec_grad)
        + jnp.sum(grad_logvar * grad_logvar)
    )
    grad_norm = jnp.sqrt(total_square)
    factor = jnp.minimum(1.0, CLIP_LIMIT / grad_norm)
    aspp_out = adam_step(trunk_aspp, aspp_first, aspp_second, shard_aspp, factor, 0.04, 0.01)
    neck_out = adam_step(trunk_neck, neck_first, neck_second, shard_neck, factor, 0.04, 0.01)
    norm_out = adam_step(norm_params, norm_first, norm_second, grad_norms, factor, 0.6, 0.0)
    dec_out = adam_step(decoders, decoder_first, decoder_second, dec_grad, factor, 0.12, 0.01)
    log_out = adam_step(log_vars, log_first, log_second, grad_logvar, factor, 0.5, 0.0)
    return (total_loss, grad_norm, *aspp_out, *neck_out, *norm_out, *dec_out, *log_out)


def solution(mesh):
    trunk = P("head", "dp", None)
    return jax.shard_map(
        shards,
        mesh=mesh,
        in_specs=(
            P(None, ("dp", "head")),
            P(),
            P(),
            P("dp"),
            P(None, "dp"),
            P("dp"),
            P("dp"),
            *[trunk] * 6,
            *[P()] * 9,
        ),
        out_specs=(P(), P(), *[trunk] * 6, *[P()] * 9),
        check_vma=False,
    )
```

```python
import functools

import jax
import jax.numpy as jnp
import numpy as np
from jax import lax
from jax.experimental import pallas as pl
from jax.experimental.pallas import tpu as pltpu
from jax.sharding import PartitionSpec as P

FEAT = 2048
BOT = 512
ASP = 256
CLS = 19
OUTS = 22
WIDTH = 128
CROP_DP = 4
QUAD = 512
STEP = 10

EPSILON = 1e-05
BETA_ONE = 0.9
BETA_TWO = 0.95
ADAM_EPSILON = 1e-08
CLIP_LIMIT = 0.05
RATES = (12, 24, 36)

BF = jnp.bfloat16
F32 = jnp.float32


def silu_slope(pre_norm):
    sigmoid_value = jax.nn.sigmoid(pre_norm)
    return sigmoid_value * (1.0 + pre_norm * (1.0 - sigmoid_value))


def dot(a, b, ca, cb):
    return lax.dot_general(a, b, ((ca, cb), ((), ())), preferred_element_type=F32)


def xor_move(x, axis, mask):
    n = lax.axis_size(axis)
    return lax.ppermute(x, axis, [(i, i ^ mask) for i in range(n)])


def xor_round(x, axis, bits):
    if len(bits) == 1:
        return x + xor_move(x, axis, bits[0])
    one, two = bits
    a = xor_move(x, axis, one)
    b = xor_move(x, axis, two)
    c = xor_move(x, axis, one | two)
    return (x + a) + (b + c)


def sum_crop(x):
    return xor_round(xor_round(x, "dp", (1,)), "dp", (2,))


def rounds_of(first, n):
    bits = []
    while first < n:
        bits.append(first)
        first *= 2
    return [tuple(bits[i : i + 2]) for i in range(0, len(bits), 2)]


def sum_dp(x):
    x = xor_round(x, "dp", (1,))
    for bits in rounds_of(2, lax.axis_size("dp")):
        x = xor_round(x, "dp", bits)
    return x


def sum_head(x):
    for bits in rounds_of(1, lax.axis_size("head")):
        x = xor_round(x, "head", bits)
    return x


def sum_all(x):
    return sum_head(sum_dp(x))


def pack(vectors):
    return jnp.concatenate([v.reshape(-1) for v in vectors])


def unpack(joined, sizes):
    out, at = [], 0
    for size in sizes:
        out.append(joined[at : at + size])
        at += size
    return out


def crop_shift(x, by):
    n = lax.axis_size("dp")
    pairs = [(i, i + by) for i in range(n) if i // CROP_DP == (i + by) // CROP_DP and 0 <= i + by < n]
    return lax.ppermute(x, "dp", pairs)


def line_shift(x, by):
    n = lax.axis_size("head")
    return lax.ppermute(x, "head", [(i, i + by) for i in range(n) if 0 <= i + by < n])


def exchange(own):
    return [own] + [xor_move(own, "head", m) for m in range(1, lax.axis_size("head"))]


def in_order(blocks, z):
    stack = jnp.stack(blocks)
    return [lax.dynamic_index_in_dim(stack, z ^ j, 0, False) for j in range(len(blocks))]


def scatter_head(blocks, z):
    n = blocks.shape[0]
    total = lax.dynamic_index_in_dim(blocks, z, 0, False).astype(F32)
    for m in range(1, n):
        total = total + xor_move(lax.dynamic_index_in_dim(blocks, z ^ m, 0, False), "head", m).astype(F32)
    return total


def halve(t, axis, bits, bit, position):
    at = bits.index(bit)
    low = 1 << at
    shape = t.shape
    split = t.reshape(shape[:axis] + (shape[axis] // (2 * low), 2, low) + shape[axis + 1 :])
    mine = (position >> (bit.bit_length() - 1)) & 1
    keep = lax.dynamic_index_in_dim(split, mine, axis + 1, False)
    send = lax.dynamic_index_in_dim(split, 1 - mine, axis + 1, False)
    got = xor_move(send, "dp", bit)
    out = (keep.astype(F32) + got.astype(F32)).astype(BF)
    return out.reshape(shape[:axis] + (shape[axis] // 2,) + shape[axis + 1 :]), [x for x in bits if x != bit]


def scatter_dp(t, axis):
    n = lax.axis_size("dp")
    position = lax.axis_index("dp")
    bits = [1 << k for k in range(n.bit_length() - 1)]
    if not isinstance(t, tuple):
        t, bits = halve(t, axis, bits, 1, position)
        t = yield (t,)
        t = t[0]
        half = t.shape[-1] // 2
        parts = [(t[..., :half], bits), (t[..., half:], bits)]
    else:
        parts = [halve(part, axis, bits, 1, position) for part in t]
        arrays = yield tuple(part for part, _ in parts)
        parts = [(array, left) for array, (_, left) in zip(arrays, parts)]
    order = [1 << k for k in range(1, n.bit_length() - 1)]
    for k in range(0, len(order), 2):
        pair = order[k : k + 2]
        for step in range(len(pair)):
            parts = [
                halve(part, axis, left, pair[step if h == 0 else len(pair) - 1 - step], position)
                for h, (part, left) in enumerate(parts)
            ]
            arrays = yield tuple(part for part, _ in parts)
            parts = [(array, left) for array, (_, left) in zip(arrays, parts)]
    return


def tie(*trees):
    return lax.optimization_barrier(trees)


def held_until(value, *others):
    return lax.optimization_barrier((value, others))[0]


def last_step(steps, now):
    while True:
        try:
            now = steps.send(now)
        except StopIteration:
            return jnp.concatenate(now, axis=-1) if len(now) > 1 else now[0]


def shift_lanes(tile, by, lanes):
    if by == 0:
        return tile
    rolled = pltpu.roll(tile, (-by) % WIDTH, 1)
    keep = (lanes < WIDTH - by) if by > 0 else (lanes >= -by)
    return jnp.where(keep, rolled, 0.0)


def neck_columns_kernel(flip, ext_ref, out_ref):
    rows = ext_ref.shape[0]
    lanes = lax.broadcasted_iota(jnp.int32, (rows, WIDTH), 1)
    count = ext_ref.shape[1] // WIDTH
    for t in range(count):
        tile = ext_ref[:, t * WIDTH : (t + 1) * WIDTH].astype(F32)
        for j in range(3):
            moved = shift_lanes(tile, (j - 1) * 4, lanes).astype(BF)
            for i in range(3):
                at = t - 4 * i
                if 0 <= at < count - 8:
                    tap = 3 * i + j
                    out_ref[8 - tap if flip else tap, :, at * WIDTH : (at + 1) * WIDTH] = moved


def neck_columns(ext, flip):
    rows, width = ext.shape
    block = 64
    return pl.pallas_call(
        functools.partial(neck_columns_kernel, flip),
        grid=(rows // block,),
        in_specs=[pl.BlockSpec((block, width), lambda i: (i, 0))],
        out_specs=pl.BlockSpec((9, block, width - 1024), lambda i: (0, i, 0)),
        out_shape=jax.ShapeDtypeStruct((9, rows, width - 1024), BF),
        compiler_params=pltpu.CompilerParams(vmem_limit_bytes=40 << 20),
        cost_estimate=pl.CostEstimate(flops=0, bytes_accessed=2 * 12 * rows * width, transcendentals=0),
    )(ext)


TAP_STEP = 240


def frames_of(own_rows, n_dp):
    starts = [own_rows * s // 256 * 16 for s in range(n_dp)]
    ends = [-(-own_rows * (s + 1) // 16) for s in range(n_dp)]
    rows = max(end - start for start, end in zip(starts, ends))
    return starts, -(-rows // 16) * 16


def assemble_kernel(pieces, in_ref, out_ref):
    for start, stop, sources in pieces:
        total = None
        for s, at in sources:
            part = in_ref[s, at : at + stop - start, :]
            total = part if total is None else total + part
        out_ref[start:stop, :] = total
    end = pieces[-1][1]
    if end < out_ref.shape[0]:
        out_ref[end:, :] = jnp.zeros((out_ref.shape[0] - end, out_ref.shape[1]), BF)


def assemble(framed, own_rows, total_rows):
    n_dp, frame_rows, width = framed.shape
    starts, _ = frames_of(own_rows, n_dp)
    rows = -(-total_rows // TAP_STEP) * TAP_STEP
    pieces = []
    for g in range(0, -(-total_rows // 16) * 16, 16):
        sources = tuple(
            (s, g - starts[s])
            for s in range(n_dp)
            if own_rows * s < (g + 16) * 16 and own_rows * (s + 1) > g * 16
        )
        if pieces and len(sources) == 1 and len(pieces[-1][2]) == 1 and pieces[-1][2][0][0] == sources[0][0]:
            pieces[-1] = (pieces[-1][0], g + 16, pieces[-1][2])
        else:
            pieces.append((g, g + 16, sources))
    block = 256
    return pl.pallas_call(
        functools.partial(assemble_kernel, pieces),
        grid=(width // block,),
        in_specs=[pl.BlockSpec((n_dp, frame_rows, block), lambda i: (0, 0, i))],
        out_specs=pl.BlockSpec((rows, block), lambda i: (0, i)),
        out_shape=jax.ShapeDtypeStruct((rows, width), BF),
        compiler_params=pltpu.CompilerParams(vmem_limit_bytes=40 << 20),
        cost_estimate=pl.CostEstimate(flops=0, bytes_accessed=4 * rows * width, transcendentals=0),
    )(framed)


def whole(shape):
    return pl.BlockSpec(shape, lambda *_: (0,) * len(shape), pipeline_mode=pl.Buffered(1))


def lane_parts(value):
    total = value[:, :WIDTH]
    for t in range(1, value.shape[1] // WIDTH):
        total = total + value[:, t * WIDTH : (t + 1) * WIDTH]
    return total


def sigmoid_of(value):
    return 0.5 * jnp.tanh(0.5 * value) + 0.5


def shift_quad(value, by, lanes):
    return jnp.concatenate(
        [shift_lanes(value[:, t * WIDTH : (t + 1) * WIDTH], by, lanes) for t in range(4)], axis=1
    )


def neck_conv_kernel(z_ref, s0, s1, s2, s3, before, after, w_ref, mask_ref, out_ref, own_ref, one_ref, two_ref, ext):
    a = pl.program_id(0)

    @pl.when(a == 0)
    def _():
        z = z_ref[0]
        ext[0] = before[...]
        ext[5] = after[...]
        for m, slot in enumerate((s0, s1, s2, s3)):
            ext[1 + jnp.bitwise_xor(z, m)] = slot[...]
        one_ref[...] = jnp.zeros_like(one_ref)
        two_ref[...] = jnp.zeros_like(two_ref)

    own_ref[...] = ext[a + 1]
    rows = out_ref.shape[0]
    lanes = lax.broadcasted_iota(jnp.int32, (rows, WIDTH), 1)
    for j in (1, 0, 2):
        total = None
        for i in range(3):
            part = jnp.dot(w_ref[3 * i + j], ext[a + i], preferred_element_type=F32)
            total = part if total is None else total + part
        if j == 1:
            out_ref[...] = total
        else:
            out_ref[...] += shift_quad(total, (j - 1) * 4, lanes)
    value = out_ref[...]
    masked = value * mask_ref[0:1, :]
    one_ref[...] += lane_parts(masked)
    two_ref[...] += lane_parts(masked * value)


def neck_conv(z, slots, before, after, weights, mask8):
    rows = weights.shape[1]
    width = mask8.shape[1]
    block = lambda a, z_ref: (0, a)
    return pl.pallas_call(
        neck_conv_kernel,
        grid_spec=pltpu.PrefetchScalarGridSpec(
            num_scalar_prefetch=1,
            grid=(width // QUAD,),
            in_specs=[whole(before.shape)] * 6
            + [whole(weights.shape), pl.BlockSpec((8, QUAD), block)],
            out_specs=[
                pl.BlockSpec((rows, QUAD), block),
                pl.BlockSpec((rows, QUAD), block),
                pl.BlockSpec((rows, WIDTH), lambda a, z_ref: (0, 0)),
                pl.BlockSpec((rows, WIDTH), lambda a, z_ref: (0, 0)),
            ],
            scratch_shapes=[pltpu.VMEM((6, rows, QUAD), BF)],
        ),
        out_shape=[
            jax.ShapeDtypeStruct((rows, width), F32),
            jax.ShapeDtypeStruct((rows, width), BF),
            jax.ShapeDtypeStruct((rows, WIDTH), F32),
            jax.ShapeDtypeStruct((rows, WIDTH), F32),
        ],
        compiler_params=pltpu.CompilerParams(vmem_limit_bytes=48 << 20),
        cost_estimate=pl.CostEstimate(flops=18 * rows * rows * width, bytes_accessed=16 << 20, transcendentals=0),
    )(z.reshape(1), *slots, before, after, weights, mask8)


CHUNK = 256


def fetch_quad(away, sources, buffer, sem):
    for k, source in zip((0, 1, 2, 3, -1, -2, -3), sources):

        @pl.when(away == k)
        def _():
            pltpu.make_async_copy(source, buffer, sem).start()


def feature_group_kernel(z_ref, mask_ref, x0, x1, x2, x3, x4, x5, x6, out_ref, xbuf, sem):
    sources = (x0, x1, x2, x3, x4, x5, x6)
    fetch_quad(pl.program_id(0) - z_ref[0], sources, xbuf, sem)
    pltpu.make_async_copy(x0, xbuf, sem).wait()
    mask = mask_ref[0:1, :]

    def place(i, carry):
        at = pl.ds(pl.multiple_of(i * CHUNK, CHUNK), CHUNK)
        out_ref[at, :] = (xbuf[at, :].astype(F32) * mask).astype(BF)
        return carry

    lax.fori_loop(0, out_ref.shape[0] // CHUNK, place, 0)


def feature_group(z, mask8, sources):
    rows = sources[0].shape[0]
    width = mask8.shape[1]
    block = lambda a, z_ref: (0, a)
    return pl.pallas_call(
        feature_group_kernel,
        grid_spec=pltpu.PrefetchScalarGridSpec(
            num_scalar_prefetch=1,
            grid=(width // QUAD,),
            in_specs=[pl.BlockSpec((8, QUAD), block)] + [pl.BlockSpec(memory_space=pl.ANY)] * 7,
            out_specs=pl.BlockSpec((rows, QUAD), block),
            scratch_shapes=[pltpu.VMEM((rows, QUAD), BF), pltpu.SemaphoreType.DMA],
        ),
        out_shape=jax.ShapeDtypeStruct((rows, width), BF),
        compiler_params=pltpu.CompilerParams(vmem_limit_bytes=32 << 20),
        cost_estimate=pl.CostEstimate(flops=0, bytes_accessed=4 * rows * width, transcendentals=0),
    )(z.reshape(1), mask8, *sources)


def aspp_forward_kernel(
    z_ref, pre_ref, coef_ref, mask_ref, w_ref, x0, x1, x2, x3, x4, x5, x6,
    y_ref, slope_ref, core_ref, side_ref, pool_ref, xbuf, held, products, sem
):
    a = pl.program_id(0)
    quads = pl.num_programs(0) - 1
    sources = (x0, x1, x2, x3, x4, x5, x6)
    slot = a % 2
    channels = y_ref.shape[0]
    steps = w_ref.shape[0] // TAP_STEP
    chunk = channels // steps

    @pl.when(a == 0)
    def _():
        fetch_quad(-z_ref[0], sources, xbuf.at[0], sem.at[0])

    @pl.when(a < quads)
    def _():
        pltpu.make_async_copy(x0, xbuf.at[slot], sem.at[slot]).wait()

    @pl.when(a + 1 < quads)
    def _():
        fetch_quad(a + 1 - z_ref[0], sources, xbuf.at[1 - slot], sem.at[1 - slot])

    mask = mask_ref[0:1, :]

    def activate(i):
        at = pl.ds(pl.multiple_of(i * chunk, chunk), chunk)
        x = xbuf[slot, at, :].astype(F32) * mask
        value = pre_ref[at, :].astype(F32) * coef_ref[at, 0:1] + coef_ref[at, 1:2] + x
        sig = sigmoid_of(value)
        y_ref[at, :] = (value * sig * mask).astype(BF)
        slope_ref[at, :] = (sig * (1.0 + value * (1.0 - sig)) * mask).astype(BF)

    def multiply(i):
        at = pl.ds(pl.multiple_of(i * TAP_STEP, 16), TAP_STEP)
        products[at, :] = jnp.dot(w_ref[at, :], held[...], preferred_element_type=F32)

    @pl.when(a == 0)
    def _():
        lax.fori_loop(0, steps, lambda i, c: (activate(i), c)[1], 0)

    @pl.when((a > 0) & (a < quads))
    def _():
        def both(i, carry):
            multiply(i)
            activate(i)
            return carry

        lax.fori_loop(0, steps, both, 0)

    @pl.when(a == quads)
    def _():
        lax.fori_loop(0, steps, lambda i, c: (multiply(i), c)[1], 0)

    held[...] = y_ref[...]

    @pl.when(a > 0)
    def _():
        lanes = lax.broadcasted_iota(jnp.int32, (64, WIDTH), 1)
        core_ref[0] = products[0:64, :]
        pool_ref[0] = lane_parts(products[64 * 28 : 64 * 29, :])
        for t in range(4):
            part = slice(t * WIDTH, (t + 1) * WIDTH)
            for br, rate in enumerate(RATES):
                for i in range(3):
                    total = None
                    for j in range(3):
                        row = 64 * (1 + 9 * br + 3 * i + j)
                        moved = shift_lanes(products[row : row + 64, part], (j - 1) * rate, lanes)
                        total = moved if total is None else total + moved
                    if i == 1:
                        core_ref[1 + br, :, part] = total
                    else:
                        side_ref[2 * br + i // 2, 0, :, part] = total.astype(BF)


def aspp_forward(z, pre, coef, mask8, weights, sources):
    rows, width = pre.shape
    quads = width // QUAD
    now = lambda a: jnp.minimum(a, quads - 1)
    done = lambda a: jnp.maximum(a - 1, 0)
    wide = pl.BlockSpec((rows, QUAD), lambda a, z_ref: (0, now(a)))
    return pl.pallas_call(
        aspp_forward_kernel,
        grid_spec=pltpu.PrefetchScalarGridSpec(
            num_scalar_prefetch=1,
            grid=(quads + 1,),
            in_specs=[
                wide,
                whole(coef.shape),
                pl.BlockSpec((8, QUAD), lambda a, z_ref: (0, now(a))),
                whole(weights.shape),
            ]
            + [pl.BlockSpec(memory_space=pl.ANY)] * 7,
            out_specs=[
                wide,
                wide,
                pl.BlockSpec((4, 64, QUAD), lambda a, z_ref: (0, 0, done(a))),
                pl.BlockSpec((6, 1, 64, QUAD), lambda a, z_ref: (0, done(a), 0, 0)),
                pl.BlockSpec((1, 64, WIDTH), lambda a, z_ref: (done(a), 0, 0)),
            ],
            scratch_shapes=[
                pltpu.VMEM((2, rows, QUAD), BF),
                pltpu.VMEM((rows, QUAD), BF),
                pltpu.VMEM((weights.shape[0], QUAD), F32),
                pltpu.SemaphoreType.DMA((2,)),
            ],
        ),
        out_shape=[
            jax.ShapeDtypeStruct((rows, width), BF),
            jax.ShapeDtypeStruct((rows, width), BF),
            jax.ShapeDtypeStruct((4, 64, width), F32),
            jax.ShapeDtypeStruct((6, quads, 64, QUAD), BF),
            jax.ShapeDtypeStruct((quads, 64, WIDTH), F32),
        ],
        compiler_params=pltpu.CompilerParams(vmem_limit_bytes=58 << 20),
        cost_estimate=pl.CostEstimate(
            flops=2 * 29 * 64 * rows * width, bytes_accessed=48 << 20, transcendentals=rows * width
        ),
    )(z.reshape(1), pre, coef, mask8, weights, *sources)


def aspp_backward_kernel(
    one_ref, rows_ref, pool_in, mask_ref, w_ref, slope_ref, pre_ref,
    out_ref, act_ref, sum_ref, dot_ref
):
    @pl.when(pl.program_id(0) == 0)
    def _():
        sum_ref[...] = jnp.zeros_like(sum_ref)
        dot_ref[...] = jnp.zeros_like(dot_ref)

    lanes = lax.broadcasted_iota(jnp.int32, (64, WIDTH), 1)
    out_ref[0:64, :] = one_ref[...].astype(BF)
    out_ref[64 * 29 :, :] = jnp.zeros((out_ref.shape[0] - 64 * 29, QUAD), BF)
    for t in range(4):
        part = slice(t * WIDTH, (t + 1) * WIDTH)
        out_ref[64 * 28 : 64 * 29, part] = (pool_in[...] * mask_ref[0:1, part]).astype(BF)
        for br, rate in enumerate(RATES):
            for i in range(3):
                tile = rows_ref[br, i, 0, :, part].astype(F32)
                for j in range(3):
                    at = 64 * (1 + 9 * br + 3 * i + j)
                    out_ref[at : at + 64, part] = shift_lanes(tile, (1 - j) * rate, lanes).astype(BF)

    def multiply(i, carry):
        at = pl.ds(pl.multiple_of(i * CHUNK, CHUNK), CHUNK)
        grad = jnp.dot(w_ref[at, :], out_ref[...], preferred_element_type=F32)
        act = grad * slope_ref[at, :].astype(F32)
        act_ref[at, :] = act.astype(BF)
        sum_ref[at, :] += lane_parts(act)
        dot_ref[at, :] += lane_parts(act * pre_ref[at, :].astype(F32))
        return carry

    lax.fori_loop(0, act_ref.shape[0] // CHUNK, multiply, 0, unroll=4)


def aspp_backward(one, rows, pool, mask8, weights_t, slope, pre):
    channels, width = pre.shape
    quads = width // QUAD
    count = weights_t.shape[1]
    block = lambda a: (0, a)
    wide = pl.BlockSpec((channels, QUAD), block)
    return pl.pallas_call(
        aspp_backward_kernel,
        grid=(quads,),
        in_specs=[
            pl.BlockSpec((64, QUAD), block),
            pl.BlockSpec((3, 3, 1, 64, QUAD), lambda a: (0, 0, a, 0, 0)),
            whole((64, WIDTH)),
            pl.BlockSpec((8, QUAD), block),
            whole(weights_t.shape),
            wide,
            wide,
        ],
        out_specs=[
            pl.BlockSpec((count, QUAD), block),
            wide,
            pl.BlockSpec((channels, WIDTH), lambda a: (0, 0)),
            pl.BlockSpec((channels, WIDTH), lambda a: (0, 0)),
        ],
        out_shape=[
            jax.ShapeDtypeStruct((count, width), BF),
            jax.ShapeDtypeStruct((channels, width), BF),
            jax.ShapeDtypeStruct((channels, WIDTH), F32),
            jax.ShapeDtypeStruct((channels, WIDTH), F32),
        ],
        compiler_params=pltpu.CompilerParams(vmem_limit_bytes=58 << 20),
        cost_estimate=pl.CostEstimate(
            flops=2 * count * channels * width, bytes_accessed=48 << 20, transcendentals=0
        ),
    )(one, rows, pool, mask8, weights_t, slope, pre)


def taps_grad_kernel(starts, spread_ref, y_ref, project_ref, out_ref, total):
    total[...] = dot(spread_ref[...], y_ref[...], (1,), (1,)).astype(BF)
    low = 29 * 64
    total[low : low + project_ref.shape[0], :] = project_ref[...]
    for s, start in enumerate(starts):
        out_ref[s] = total[start : start + out_ref.shape[1], :]


def taps_grad(starts, frame_rows, spread, y, project, part, parts):
    rows, pixels = spread.shape
    width = y.shape[0] // parts
    block = 256
    first = part * width // block
    return pl.pallas_call(
        functools.partial(taps_grad_kernel, starts),
        grid=(width // block,),
        in_specs=[
            whole((rows, pixels)),
            pl.BlockSpec((block, pixels), lambda i: (first + i, 0)),
            pl.BlockSpec((project.shape[0], block), lambda i: (0, first + i)),
        ],
        out_specs=pl.BlockSpec((len(starts), frame_rows, block), lambda i: (0, 0, i)),
        out_shape=jax.ShapeDtypeStruct((len(starts), frame_rows, width), BF),
        scratch_shapes=[pltpu.VMEM((rows, block), BF)],
        compiler_params=pltpu.CompilerParams(vmem_limit_bytes=48 << 20),
        cost_estimate=pl.CostEstimate(
            flops=2 * rows * pixels * width, bytes_accessed=20 << 20, transcendentals=0
        ),
    )(spread, y, project)


def side_rows(side):
    result = []
    at = lax.axis_index("dp") % CROP_DP
    n = lax.axis_size("dp")
    from_one = crop_shift(jnp.concatenate([side[0, 1:4], side[2, 0:2]]), 1)
    to_one = crop_shift(jnp.concatenate([side[1, 0:3], side[3, 2:4]]), -1)
    up = jnp.concatenate([side[2, 2:4], side[4, 0:3]])
    down = jnp.concatenate([side[3, 0:2], side[5, 1:4]])
    two = xor_move(jnp.where(at < 2, up, down), "dp", 2)
    from_two = jnp.where(at < 2, jnp.zeros_like(two), two)
    to_two = jnp.where(at < 2, two, jnp.zeros_like(two))
    ends = [(i, i + 3 - 2 * (i % CROP_DP)) for i in range(n) if i % CROP_DP in (0, CROP_DP - 1)]
    three = lax.ppermute(jnp.where(at == 0, side[4, 3:4], side[5, 0:1]), "dp", ends)
    from_three = jnp.where(at == 0, jnp.zeros_like(three), three)
    to_three = jnp.where(at == 0, three, jnp.zeros_like(three))
    result.append(jnp.concatenate([from_one[0:3], side[0, 0:1]]))
    result.append(jnp.concatenate([side[1, 3:4], to_one[0:3]]))
    result.append(jnp.concatenate([from_two[0:2], from_one[3:5]]))
    result.append(jnp.concatenate([to_one[3:5], to_two[0:2]]))
    result.append(jnp.concatenate([from_three, from_two[2:5]]))
    result.append(jnp.concatenate([to_two[2:5], to_three]))
    return result


def adam_step(weight, first_m, second_m, gradient, factor, rate, decay):
    clipped = gradient * factor
    new_first = BETA_ONE * first_m + (1.0 - BETA_ONE) * clipped
    new_second = BETA_TWO * second_m + (1.0 - BETA_TWO) * clipped * clipped
    corrected = (
        new_first
        / (1.0 - BETA_ONE**STEP)
        / (jnp.sqrt(new_second / (1.0 - BETA_TWO**STEP)) + ADAM_EPSILON)
    )
    return (weight - rate * (corrected + decay * weight), new_first, new_second)


def flat_rows(quads):
    return jnp.concatenate([quads[a] for a in range(quads.shape[0])], axis=1)


def quad_blocks(flat):
    return [flat[..., a * QUAD : (a + 1) * QUAD] for a in range(flat.shape[-1] // QUAD)]


def owner_tables(n_dp, share_rows, wide, heads):
    quarter = BOT // heads
    places = []
    for p in range(n_dp):
        rows = []
        for k in range(wide):
            rows += [(share_rows * p + r) * wide + k for r in range(share_rows)]
        for tap in range(9):
            rows += [quarter * (wide + tap) + share_rows * p + r for r in range(share_rows)]
        rows += [quarter * (wide + 9) + share_rows * wide * p + r for r in range(share_rows * wide)]
        places.append(np.array(rows))
    own = len(places[0])
    lists = [[np.nonzero(place // own == s)[0] for s in range(n_dp)] for place in places]
    count = -(-max(len(x) for row in lists for x in row) // 16) * 16
    send = np.full((n_dp, n_dp, count), -1, np.int32)
    take = np.zeros((n_dp, own), np.int32)
    for p in range(n_dp):
        for s in range(n_dp):
            rows = lists[p][s]
            send[p, s, : len(rows)] = rows
            take[s, places[p][rows] - own * s] = p * count + np.arange(len(rows))
    return send, take


def shards(
    features,
    crop_rows,
    crop_cols,
    labels,
    offset_targets,
    depth_targets,
    lidar_mask,
    trunk_aspp,
    aspp_first,
    aspp_second,
    trunk_neck,
    neck_first,
    neck_second,
    norm_params,
    norm_first,
    norm_second,
    decoders,
    decoder_first,
    decoder_second,
    log_vars,
    log_first,
    log_second,
):
    heads = lax.axis_size("head")
    z = lax.axis_index("head")
    group = lax.axis_index("dp")
    crop = group // CROP_DP
    pixels = heads * QUAD
    share = 1.0 / heads
    quarter = ASP // heads

    n_dp = lax.axis_size("dp")
    neck_low = trunk_neck.reshape(1, -1, BOT).astype(BF)
    neck_low = lax.all_gather(neck_low, "head", axis=0, tiled=True)
    neck_low = lax.all_gather(neck_low, "dp", axis=1, tiled=True)
    x_left, x_right = [features, line_shift(features, 1)], [features, line_shift(features, -1)]
    neck_low, x_left[1], x_right[1] = tie(neck_low, x_left[1], x_right[1])
    first_end = FEAT // heads
    second_end = first_end + 9 * BOT // heads
    reduce_w = neck_low[:, :first_end].reshape(BOT, FEAT)
    middle = neck_low[:, first_end:second_end].reshape(heads, 9, BOT // heads, BOT)
    middle = jnp.moveaxis(middle, 0, 1).reshape(9, BOT, BOT)
    expand_w = neck_low[:, second_end:].reshape(FEAT, BOT)


    flat_total = trunk_aspp.shape[1] * n_dp // 16
    own_rows = trunk_aspp.shape[1]
    frames, frame_rows = frames_of(own_rows, n_dp)
    inset = (group * own_rows) % 256
    framed = lax.dynamic_update_slice_in_dim(
        jnp.zeros((frame_rows * 16, 128), F32), trunk_aspp[0], inset, 0
    )
    framed = framed.reshape(frame_rows, FEAT).astype(BF)
    gathered = lax.all_gather(framed, "dp", axis=0)

    place = jnp.arange(pixels, dtype=jnp.int32)
    row_place = group % CROP_DP * (pixels // WIDTH) + place // WIDTH
    col_place = place % WIDTH
    mask = ((row_place < crop_rows[crop]) & (col_place < crop_cols[crop])).astype(F32)[None, :]
    mask_own = lax.dynamic_slice_in_dim(mask, z * QUAD, QUAD, 1)
    total_n = jnp.sum((crop_rows * crop_cols).astype(F32))
    crop_n = (crop_rows[crop] * crop_cols[crop]).astype(F32)

    def own_pixels(a):
        return lax.dynamic_slice_in_dim(a, z * QUAD, QUAD, a.ndim - 1)

    labels_own = own_pixels(labels)
    offset_own = own_pixels(offset_targets)
    depth_own = own_pixels(depth_targets)
    lidar_own = own_pixels(lidar_mask).astype(F32) * mask_own[0]

    gains, shifts = (norm_params[0], norm_params[1])
    bounds = [0, BOT, 2 * BOT, 2 * BOT + FEAT, 2 * BOT + FEAT + 4 * ASP, 2 * BOT + FEAT + 5 * ASP]

    def slot(vector, index):
        return vector[bounds[index] : bounds[index + 1]]

    def own_aspp(vector):
        return lax.dynamic_slice_in_dim(vector.reshape(4, heads, quarter), z, 1, 1).reshape(-1)

    gain_one, gain_two, gain_three, gain_proj = [slot(gains, i) for i in (0, 1, 2, 4)]
    shift_one, shift_two, shift_three, shift_proj = [slot(shifts, i) for i in (0, 1, 2, 4)]
    gain_aspp, shift_aspp = own_aspp(slot(gains, 3)), own_aspp(slot(shifts, 3))

    def moments(pre, m):
        masked = pre * m
        return jnp.sum(masked, axis=-1), jnp.sum(masked * pre, axis=-1)

    def coefficients(total, square):
        mean = total / total_n
        inv = lax.rsqrt(square / total_n - mean * mean + EPSILON)
        return mean, inv

    def normed(pre, mean, inv):
        return (pre - mean[:, None]) * inv[:, None]

    def scaled(hat, gain, shift):
        return gain[:, None] * hat + shift[:, None]

    x_own = features * mask_own.astype(BF)
    pre_one = jnp.dot(reduce_w, x_own, preferred_element_type=F32)
    sums = sum_all(pack((*moments(pre_one, mask_own), jnp.broadcast_to(jnp.sum(lidar_own), (128,)))))
    total, square, lidar = unpack(sums, (BOT, BOT, 128))
    lidar_n = lidar[0]
    mean_one, inv_one = coefficients(total, square)
    low_one = (jax.nn.silu(scaled(normed(pre_one, mean_one, inv_one), gain_one, shift_one)) * mask_own).astype(BF)
    slots = exchange(low_one)
    aspp_rows = assemble(held_until(gathered, low_one), own_rows, flat_total)
    project_q = aspp_rows[29 * quarter : flat_total].reshape(quarter, 5, heads, quarter)
    project_q = jnp.moveaxis(project_q, 2, 0).reshape(heads, quarter, 5 * quarter)
    received = [lax.dynamic_index_in_dim(project_q, z, 0, False)]
    for m in range(1, heads):
        received.append(xor_move(lax.dynamic_index_in_dim(project_q, z ^ m, 0, False), "head", m))
    project_own = jnp.concatenate(in_order(received, z), axis=0)
    tap_wt = aspp_rows.T
    slots, tap_wt, project_own = tie(slots, tap_wt, project_own)
    x_left[1], x_right[1] = held_until((x_left[1], x_right[1]), slots)
    for _ in range(1, heads - 1):
        x_left.append(line_shift(x_left[-1], 1))
        x_right.append(line_shift(x_right[-1], -1))

    def block_of(j):
        block = slots[0]
        for m in range(1, heads):
            block = jnp.where((z ^ m) == j, slots[m], block)
        return block

    before = crop_shift(block_of(heads - 1), 1)
    after = crop_shift(block_of(0), -1)
    mask8 = jnp.broadcast_to(mask, (8, pixels))
    pre_two, h_one, one_part, two_part = neck_conv(z, slots, before, after, middle, mask8)
    sums = sum_dp(pack((jnp.sum(one_part, axis=1), jnp.sum(two_part, axis=1))))
    mean_two, inv_two = coefficients(*unpack(sums, (BOT, BOT)))
    hat_two = normed(pre_two, mean_two, inv_two)
    in_two = scaled(hat_two, gain_two, shift_two)
    h_two = (jax.nn.silu(in_two) * mask).astype(BF)
    pre_three = jnp.dot(expand_w, h_two, preferred_element_type=F32)
    mean_three, inv_three = coefficients(*unpack(sum_dp(pack(moments(pre_three, mask))), (FEAT, FEAT)))
    pre_three = pre_three.astype(BF)
    scale_three = gain_three * inv_three
    coef = jnp.stack([scale_three, shift_three - scale_three * mean_three], axis=1)
    sources = [features, *x_right[1:], *x_left[1:]]
    y, slope_three, middle_rows, side, pool_part = aspp_forward(
        z, pre_three, coef, mask8, aspp_rows, sources
    )

    moved = side_rows(side)
    branches = [middle_rows[0]]
    for br in range(3):
        branches.append(
            middle_rows[1 + br]
            + flat_rows(moved[2 * br]).astype(F32)
            + flat_rows(moved[2 * br + 1]).astype(F32)
        )
    pre_aspp = jnp.concatenate(branches, axis=0)
    pool_local = jnp.sum(pool_part, axis=(0, 2))
    local = pack((*moments(pre_aspp, mask), pool_local, jnp.zeros((64,), F32)))
    local = sum_crop(local)
    pool_sum = local[2 * ASP : 2 * ASP + quarter]
    for bits in rounds_of(4, lax.axis_size("dp")):
        local = xor_round(local, "dp", bits)
    mean_aspp, inv_aspp = coefficients(local[:ASP], local[ASP : 2 * ASP])
    hat_aspp = normed(pre_aspp, mean_aspp, inv_aspp)
    in_aspp = scaled(hat_aspp, gain_aspp, shift_aspp)
    act_aspp = jax.nn.silu(in_aspp) * mask
    pool_pre = pool_sum / crop_n
    joined = jnp.concatenate([act_aspp, jax.nn.silu(pool_pre)[:, None] * mask], axis=0).astype(BF)

    part_proj = jnp.dot(project_own, joined, preferred_element_type=F32)
    pre_proj = scatter_head(jnp.stack(quad_blocks(part_proj.astype(BF))), z)
    x_group = feature_group(z, held_until(mask8, part_proj), sources)
    pre_proj, x_group = tie(pre_proj, x_group)
    mean_proj, inv_proj = coefficients(*unpack(sum_all(pack(moments(pre_proj, mask_own))), (ASP, ASP)))
    hat_proj = normed(pre_proj, mean_proj, inv_proj)
    in_proj = scaled(hat_proj, gain_proj, shift_proj)
    feat = (jax.nn.silu(in_proj) * mask_own).astype(BF)

    low_dec = decoders.astype(BF)
    hidden_w, out_w = low_dec[: 3 * ASP], low_dec[3 * ASP :]
    dec_pre = jnp.dot(hidden_w, feat, preferred_element_type=F32)
    hidden = jax.nn.silu(dec_pre).astype(BF)
    row_sets = ((0, CLS), (CLS, CLS + 2), (CLS + 2, CLS + 3))
    logits = [
        jnp.dot(out_w, hidden[t * ASP : (t + 1) * ASP], preferred_element_type=F32)[lo:hi]
        for t, (lo, hi) in enumerate(row_sets)
    ]
    sem_logits, off_logits, dep_logits = logits
    valid_own = mask_own[0]
    label_hot = (jnp.arange(CLS, dtype=jnp.int32)[:, None] == labels_own[None, :]).astype(F32)
    log_total = jax.nn.logsumexp(sem_logits, axis=0)
    sem_sum = jnp.sum((log_total - jnp.sum(label_hot * sem_logits, axis=0)) * valid_own)
    off_diff = off_logits - offset_own
    off_root = jnp.sqrt(off_diff * off_diff + 1.0)
    off_sum = jnp.sum((off_root - 1.0) * valid_own)
    dep_logit = dep_logits[0]
    dep_diff = jax.nn.softplus(dep_logit) - depth_own
    dep_root = jnp.sqrt(dep_diff * dep_diff + 1.0)
    dep_sum = jnp.sum((dep_root - 1.0) * lidar_own)
    divisors = jnp.stack([total_n, total_n, lidar_n])
    weights = jnp.exp(-log_vars) / divisors
    grad_sem = (jax.nn.softmax(sem_logits, axis=0) - label_hot) * valid_own * weights[0]
    grad_off = off_diff / off_root * valid_own * weights[1]
    grad_dep = (dep_diff / dep_root * jax.nn.sigmoid(dep_logit) * lidar_own * weights[2])[None, :]
    grad_logits = [g.astype(BF) for g in (grad_sem, grad_off, grad_dep)]
    grad_out_w = []
    grad_hidden = []
    for t, (lo, hi) in enumerate(row_sets):
        grad_out_w.append(dot(grad_logits[t], hidden[t * ASP : (t + 1) * ASP], (1,), (1,)))
        grad_hidden.append(dot(out_w[lo:hi], grad_logits[t], (0,), (0,)))
    grad_dec_pre = (jnp.concatenate(grad_hidden, axis=0) * silu_slope(dec_pre)).astype(BF)
    grad_hidden_w = dot(grad_dec_pre, feat, (1,), (1,))
    grad_feat = dot(hidden_w, grad_dec_pre, (0,), (0,))
    dec_grad = lax.psum(jnp.concatenate([grad_hidden_w, *grad_out_w], axis=0), ("dp", "head"))

    grad_act = grad_feat * mask_own * silu_slope(in_proj)
    sums = sum_all(
        pack(
            (
                jnp.sum(grad_act, axis=-1),
                jnp.sum(grad_act * hat_proj, axis=-1),
                jnp.stack([sem_sum, off_sum, dep_sum]),
                jnp.zeros((125,), F32),
            )
        )
    )
    back_shift_proj, back_gain_proj, loss_sums = unpack(sums, (ASP, ASP, 3))
    losses = loss_sums / divisors
    total_loss = jnp.sum(jnp.exp(-log_vars) * losses + log_vars)
    grad_logvar = 1.0 - jnp.exp(-log_vars) * losses
    grad_proj = (
        mask_own
        * (gain_proj * inv_proj)[:, None]
        * (grad_act - (back_shift_proj / total_n)[:, None] - hat_proj * (back_gain_proj / total_n)[:, None])
    ).astype(BF)
    grad_proj = jnp.concatenate(in_order(exchange(grad_proj), z), axis=1)
    grad_project = dot(grad_proj, joined, (1,), (1,)).astype(BF).reshape(heads, quarter, 5 * quarter)
    grad_joined = dot(project_own, grad_proj, (0,), (0,))

    grad_act = grad_joined[:ASP] * mask * silu_slope(in_aspp)
    local = pack(
        (
            jnp.sum(grad_act, axis=-1),
            jnp.sum(grad_act * hat_aspp, axis=-1),
            jnp.sum(grad_joined[ASP:] * mask, axis=-1),
            jnp.zeros((64,), F32),
        )
    )
    local = sum_crop(local)
    pool_row = local[2 * ASP : 2 * ASP + quarter]
    for bits in rounds_of(4, lax.axis_size("dp")):
        local = xor_round(local, "dp", bits)
    back_shift_aspp, back_gain_aspp = local[:ASP], local[ASP : 2 * ASP]
    grad_aspp = (
        mask
        * (gain_aspp * inv_aspp)[:, None]
        * (grad_act - (back_shift_aspp / total_n)[:, None] - hat_aspp * (back_gain_aspp / total_n)[:, None])
    ).astype(BF)
    grad_pool = (pool_row * silu_slope(pool_pre)).astype(BF).astype(F32) / crop_n
    parts = [jnp.stack(quad_blocks(grad_aspp[quarter * (br + 1) : quarter * (br + 2)])) for br in range(3)]
    moved = side_rows(jnp.stack([part for part in parts for _ in range(2)]))
    rows = jnp.stack(
        [jnp.stack([moved[2 * br + 1], parts[br], moved[2 * br]]) for br in range(3)]
    )
    spread, act_three, sum_part, dot_part = aspp_backward(
        grad_aspp[:quarter],
        rows,
        jnp.broadcast_to(grad_pool[:, None], (quarter, WIDTH)),
        mask8,
        tap_wt,
        slope_three,
        pre_three,
    )

    spread_norms = jnp.stack([back_gain_aspp, back_shift_aspp]).reshape(2, 4, 1, quarter)
    own_place = (jnp.arange(heads) == z)[None, None, :, None] & (group == 0)
    spread_norms = jnp.where(own_place, spread_norms, 0.0)
    sum_three = jnp.sum(sum_part, axis=1)
    sums = xor_round(
        pack((sum_three, (jnp.sum(dot_part, axis=1) - mean_three * sum_three) * inv_three, spread_norms)),
        "dp",
        (1,),
    )

    swapped = [
        xor_move(lax.dynamic_index_in_dim(grad_project, z ^ m, 0, False), "head", m)
        if m
        else lax.dynamic_index_in_dim(grad_project, z, 0, False)
        for m in range(heads)
    ]
    own_project = jnp.stack(in_order(swapped, z)).reshape(heads, quarter, 5, quarter)
    own_project = jnp.moveaxis(own_project, 0, 2).reshape(-1, FEAT)
    own_project = jnp.concatenate([own_project, jnp.zeros((-flat_total % 16, FEAT), BF)], axis=0)
    sums, spread, own_project = tie(sums, spread, own_project)
    first_half = taps_grad(frames, frame_rows, spread, y, own_project, 0, 2)
    for bits in rounds_of(2, n_dp):
        sums = xor_round(sums, "dp", bits)
    sums, first_half, spread = tie(sums, first_half, spread)
    second_half = taps_grad(frames, frame_rows, spread, y, own_project, 1, 2)
    sums = sum_head(sums)
    sums, first_half, second_half, dec_grad = tie(sums, first_half, second_half, dec_grad)
    aspp_steps = scatter_dp((first_half, second_half), 0)
    aspp_now = next(aspp_steps)
    back_shift_three, back_gain_three, both = unpack(sums, (FEAT, FEAT, 8 * ASP))
    both = both.reshape(2, 4 * ASP)

    def norm_back(grad_act, hat, gain, inv, back_shift, back_gain):
        scale = share / total_n
        return (
            mask
            * (gain * inv)[:, None]
            * (grad_act - (back_shift * scale)[:, None] - hat * (back_gain * scale)[:, None])
        ).astype(BF)

    hat_three = normed(pre_three.astype(F32), mean_three, inv_three)
    grad_three = norm_back(
        act_three.astype(F32), hat_three, gain_three, inv_three, back_shift_three, back_gain_three
    )
    grad_h_two = dot(expand_w, grad_three, (0,), (0,))
    grad_act = grad_h_two * mask * silu_slope(in_two)
    sums = pack((jnp.sum(grad_act, axis=-1), jnp.sum(grad_act * hat_two, axis=-1)))
    sums = xor_round(sums, "dp", (1,))
    sums, grad_three = tie(sums, grad_three)
    grad_expand = dot(grad_three, h_two, (1,), (1,)).astype(BF).reshape(heads, n_dp, -1, BOT)
    for bits in rounds_of(2, n_dp):
        sums = xor_round(sums, "dp", bits)
    sums = sum_head(sums)
    sums, grad_expand, aspp_now = tie(sums, grad_expand, aspp_now)
    back_shift_two, back_gain_two = unpack(sums, (BOT, BOT))
    grad_two = norm_back(grad_act, hat_two, gain_two, inv_two, back_shift_two, back_gain_two)
    before = crop_shift(grad_two[:, -QUAD:], 1)
    after = crop_shift(grad_two[:, :QUAD], -1)
    before, after, aspp_now, grad_expand = tie(before, after, aspp_now, grad_expand)
    aspp_now = aspp_steps.send(aspp_now)
    expand_steps = scatter_dp(grad_expand, 1)
    expand_now = next(expand_steps)
    columns = neck_columns(jnp.concatenate([before, grad_two, after], axis=1), True)
    grad_h_one = lax.dot_general(middle, columns, (((0, 1), (0, 1)), ((), ())), preferred_element_type=F32)
    group_one = jnp.dot(reduce_w, x_group, preferred_element_type=F32)
    hat_one = normed(group_one, mean_one, inv_one)
    grad_act = grad_h_one * mask * silu_slope(scaled(hat_one, gain_one, shift_one))
    sums = pack((jnp.sum(grad_act, axis=-1), jnp.sum(grad_act * hat_one, axis=-1)))
    sums, aspp_now, expand_now = tie(sums, aspp_now, expand_now)
    sums = xor_round(sums, "dp", (1,))
    sums, columns = tie(sums, columns)
    grad_middle = dot(columns, h_one, (2,), (1,)).astype(BF).reshape(9, heads, n_dp, -1, BOT)
    for bits in rounds_of(2, n_dp):
        sums = xor_round(sums, "dp", bits)
    sums = sum_head(sums)
    sums, grad_middle, aspp_now, expand_now = tie(sums, grad_middle, aspp_now, expand_now)
    middle_steps = scatter_dp(grad_middle, 2)
    middle_now = next(middle_steps)
    aspp_block = last_step(aspp_steps, aspp_now)
    expand_block = last_step(expand_steps, expand_now)
    back_shift_one, back_gain_one = unpack(sums, (BOT, BOT))
    grad_one = norm_back(grad_act, hat_one, gain_one, inv_one, back_shift_one, back_gain_one)
    grad_reduce = dot(grad_one, x_group, (1,), (1,)).astype(BF)
    wide = FEAT // BOT
    grad_reduce = jnp.stack([grad_reduce[:, k * BOT : (k + 1) * BOT] for k in range(wide)])
    reduce_steps = scatter_dp(grad_reduce.reshape(wide, heads, n_dp, -1, BOT), 2)
    reduce_now, middle_now, aspp_block, expand_block = tie(
        next(reduce_steps), middle_now, aspp_block, expand_block
    )
    expand_own = scatter_head(expand_block.reshape(heads, -1, BOT), z)
    both_now = jnp.concatenate([reduce_now[0], middle_now[0]], axis=0)
    both_block = last_step(reduce_steps, reduce_steps.send((both_now,)))

    shard_aspp = lax.dynamic_slice_in_dim(
        aspp_block.astype(F32).reshape(frame_rows * 16, 128), inset, own_rows, 0
    )[None]
    share_rows = BOT // heads // n_dp
    both_block = both_block.reshape(wide + 9, heads, share_rows, BOT)
    both_own = scatter_head(jnp.moveaxis(both_block, 1, 0), z)
    pieces = jnp.concatenate([both_own, expand_own.reshape(wide, share_rows, BOT)], axis=0).astype(BF)
    pieces = pieces.reshape(-1, BOT)
    send_rows, take_rows = owner_tables(n_dp, share_rows, wide, heads)
    count = send_rows.shape[2]
    chosen = lax.dynamic_index_in_dim(jnp.asarray(send_rows), group, 0, False).reshape(-1)
    pick = (chosen[:, None] == jnp.arange(pieces.shape[0], dtype=jnp.int32)[None, :]).astype(BF)
    sent = jnp.dot(pick, pieces, preferred_element_type=F32).astype(BF).reshape(n_dp, count, BOT)
    got = lax.all_to_all(sent, "dp", 0, 0, tiled=True).reshape(n_dp * count, BOT)
    chosen = lax.dynamic_index_in_dim(jnp.asarray(take_rows), group, 0, False)
    pick = (chosen[:, None] == jnp.arange(n_dp * count, dtype=jnp.int32)[None, :]).astype(BF)
    shard_neck = jnp.dot(pick, got, preferred_element_type=F32)
    shard_neck = shard_neck.reshape(trunk_neck.shape)

    grad_norms = jnp.stack(
        [
            jnp.concatenate([back_gain_one, back_gain_two, back_gain_three, both[0], back_gain_proj]),
            jnp.concatenate([back_shift_one, back_shift_two, back_shift_three, both[1], back_shift_proj]),
        ]
    )
    local_square = (
        jnp.sum(shard_aspp * shard_aspp)
        + jnp.sum(expand_own * expand_own)
        + jnp.sum(both_own * both_own)
    )
    total_square = (
        sum_all(jnp.broadcast_to(local_square, (128,)))[0]
        + jnp.sum(grad_norms * grad_norms)
        + jnp.sum(dec_grad * dec_grad)
        + jnp.sum(grad_logvar * grad_logvar)
    )
    grad_norm = jnp.sqrt(total_square)
    factor = jnp.minimum(1.0, CLIP_LIMIT / grad_norm)
    aspp_out = adam_step(trunk_aspp, aspp_first, aspp_second, shard_aspp, factor, 0.04, 0.01)
    neck_out = adam_step(trunk_neck, neck_first, neck_second, shard_neck, factor, 0.04, 0.01)
    norm_out = adam_step(norm_params, norm_first, norm_second, grad_norms, factor, 0.6, 0.0)
    dec_out = adam_step(decoders, decoder_first, decoder_second, dec_grad, factor, 0.12, 0.01)
    log_out = adam_step(log_vars, log_first, log_second, grad_logvar, factor, 0.5, 0.0)
    return (total_loss, grad_norm, *aspp_out, *neck_out, *norm_out, *dec_out, *log_out)


def solution(mesh):
    trunk = P("head", "dp", None)
    return jax.shard_map(
        shards,
        mesh=mesh,
        in_specs=(
            P(None, ("dp", "head")),
            P(),
            P(),
            P("dp"),
            P(None, "dp"),
            P("dp"),
            P("dp"),
            *[trunk] * 6,
            *[P()] * 9,
        ),
        out_specs=(P(), P(), *[trunk] * 6, *[P()] * 9),
        check_vma=False,
    )
```
